128 devices in a mesh: ctx: 16 (over z, y), exp: 8 (over x, core).
Axes of the slice: x: 4, y: 4, z: 4, core: 2. Of those that a mesh axis runs over, the one named last changes fastest.
Arguments:
- block_in: bfloat16 [8, 2048, 768], P('exp', 'ctx'), may hold values from -6 to 6
- attn_gain: bfloat16 [768], P('exp'), may hold values from 0.5 to 1.5
- moe_gain: bfloat16 [768], P('exp'), may hold values from 0.5 to 1.5
- query_key_value_weight: bfloat16 [768, 2304], P('exp'), may hold values from -0.21875 to 0.21875
- output_matrix: bfloat16 [768, 768], P('exp'), may hold values from -3.5 to 3.5
- routing_weight: bfloat16 [768, 8], P('exp'), may hold values from -0.15625 to 0.15625
- bias_table: bfloat16 [32, 12], P('exp'), may hold values from -4 to 4
- up_weight: bfloat16 [8, 3072, 768], P('exp', 'ctx'), may hold values from -0.21875 to 0.21875
- down_weight: bfloat16 [8, 3072, 768], P('exp', 'ctx'), may hold values from -0.109375 to 0.109375
- routes: int32 [8, 2048, 2], P('exp', 'ctx'), may hold values from 0 to 7, all different within a row; in each aligned block of 128 rows (0 to 127, 128 to 255, ..., all dimensions but the last counted through in order) at most 64 rows name the same one
- doc_lengths: int32 [8, 4], P('exp'), may hold values from 1 to 2045, as said below
- cotangent: bfloat16 [8, 2048, 768], P('exp', 'ctx'), may hold values from -6 to 6
Outputs:
- block_out: bfloat16 [8, 2048, 768], P('exp', 'ctx')
- grad_in: float32 [8, 2048, 768], P('exp', 'ctx')
- grad_attn_gain: float32 [768], P('exp')
- grad_moe_gain: float32 [768], P('exp')
- grad_qkv: float32 [768, 2304], P('exp')
- grad_out_weight: float32 [768, 768], P('exp')
- grad_router: float32 [768, 8], P('exp')
- grad_bias_table: float32 [32, 12], P('exp')
- grad_up: float32 [8, 3072, 768], P('exp', 'ctx')
- grad_down: float32 [8, 3072, 768], P('exp', 'ctx')
The draws below stay inside these ranges and needn't reach their ends.
Inputs may be any that keep to these rules, and one draw needn't show every extreme that they name: `routes`: A token's two experts differ. In the 128 tokens of one device no expert is named more than 64 times; in the rows of some devices one expert is named exactly 64 times. `doc_lengths`: each row holds 4 lengths that sum to 2048; the second document starts within the sequence's first 128 positions and ends within its last 128.
All inputs are finite; a program needn't handle non-finite values.
Results may differ from the reference program's by a relative error of at most 0.028.
Values may be sent and summed in bfloat16 or wider, within the bound.
A program may use at most 256 MiB of HBM per device.

```python
import math
import jax
import jax.numpy as jnp
import numpy as np
from jax import lax

D = 768
HEADS = 12
FF = 3072
NB = 32
MAXD = 128
NDOC = 4
TOK_DEV = 128
EXPERTS = 8
SEQS = 8
SEQ_LEN = 2048
CAP = 64


def draw_doc_lengths(key, part):
    key = jax.random.fold_in(key, 7)
    short_docs = jax.random.randint(key, (SEQS, NDOC - 1), 1, TOK_DEV // 4 + 1, dtype=jnp.int32)
    long_doc = SEQ_LEN - jnp.sum(short_docs, axis=1, keepdims=True)
    return jnp.concatenate([short_docs[:, :1], long_doc, short_docs[:, 1:]], axis=1).astype(jnp.int32)


def shard_levels(stream_key, extent, split, low, largest):
    def one(position, parts):
        heights = jax.random.uniform(jax.random.fold_in(jax.random.fold_in(stream_key, 6), position), (parts,), jnp.float32, low / len(split), largest / len(split))
        return jnp.repeat(jnp.exp(heights), extent[position] // parts).reshape((-1,) + (1,) * (len(extent) - position - 1))

    level = one(*split[0])
    for cut in split[1:]:
        level = level * one(*cut)
    return level


def deal_out(own_key, own, number, rows, number_of, top, limit, slope):
    ranking = jax.random.permutation(own_key, number_of)
    heavy_load, common = shares(number_of, rows * top, limit, slope, True), shares(number_of, rows * top, limit, slope, False)
    places = jnp.arange(number_of)

    def named(sizes, rotation):
        used = int((sizes > 0).sum())
        fixed = max(1, used // 4)
        moved = fixed + (places - fixed + rotation * (used - fixed)) % max(1, number_of - fixed)
        return jnp.zeros((number_of,), jnp.int32).at[ranking[jnp.where(places < fixed, places, moved)]].set(jnp.asarray(sizes, jnp.int32))

    sizes = jnp.where(number % 4 == 0, named(heavy_load, number // 4), named(common, number - number // 4 - 1))
    mixed = jax.random.permutation(jax.random.fold_in(own, 3), number_of)
    donor, taker = mixed[0:number_of // 2 * 2:2], mixed[1:number_of // 2 * 2:2]
    slack = jnp.minimum(sizes[donor] - 1, limit - sizes[taker]) // 2
    slack = jnp.where((donor == ranking[0]) | (taker == ranking[0]) | (sizes[taker] == 0), 0, jnp.maximum(slack, 0))
    moved = jax.random.randint(jax.random.fold_in(own, 4), (number_of // 2,), 0, 1 << 20) % (slack + 1)
    sizes = sizes.at[donor].add(-moved).at[taker].add(moved)
    items = jnp.searchsorted(jnp.cumsum(sizes), jnp.arange(rows * top), side="right").astype(jnp.int32)
    grid = items.reshape(top, rows).T
    grid = grid[jax.random.permutation(jax.random.fold_in(own, 1), rows)]
    rotation = jax.random.randint(jax.random.fold_in(own, 2), (rows, 1), 0, top)
    return jnp.take_along_axis(grid, (jnp.arange(top)[None, :] + rotation) % top, axis=1)


def shares(amount, total, reach, skew, full):
    portions = [(1 << 20) // math.isqrt(rank ** skew) + 1 for rank in range(1, amount + 1)]
    largest = reach if full else min(reach, max(-(-total // amount), total * portions[0] // sum(portions)))
    least = 1 if total - largest >= amount - 1 else 0
    given, rest = [largest] + [least] * (amount - 1), total - largest - least * (amount - 1)
    while rest > 0:
        free = [i for i in range(1, amount) if given[i] < largest] or [i for i in range(1, amount) if given[i] < reach]
        mass, budget = sum([portions[i] for i in free]), rest
        for i in free:
            addition = min(reach - given[i], max(1, budget * portions[i] // mass), rest)
            given[i] = given[i] + addition
            rest = rest - addition
    return np.array(given)


def gaussian(stream_key, dims, width, bound, split=(), held_as=jnp.bfloat16):
    entries = width * jax.random.normal(stream_key, dims, jnp.float32)
    if split:
        entries = entries * shard_levels(stream_key, dims, split, -0.22, 0.18)
    return jnp.clip(entries, -bound, bound).astype(held_as)


def setup_inputs(seed: int = 0) -> dict:
    key_list = jax.random.split(jax.random.key(seed), 13)
    block_in = gaussian(key_list[0], (SEQS, SEQ_LEN, D), 1.0, 6.0, ((0, 8), (1, 16)))
    attn_gain = jnp.clip(1.0 + 0.1 * jax.random.normal(key_list[1], (D,), jnp.float32), 0.5, 1.5).astype(jnp.bfloat16)
    moe_gain = jnp.clip(1.0 + 0.1 * jax.random.normal(key_list[2], (D,), jnp.float32), 0.5, 1.5).astype(jnp.bfloat16)
    query_key_value_weight = gaussian(key_list[3], (D, 3 * D), D ** -0.5, 0.21875, ((0, 8),))
    output_matrix = gaussian(key_list[4], (D, D), (max(D // 256, 1)) ** -0.5, 3.5, ((0, 8),))
    routing_weight = gaussian(key_list[5], (D, EXPERTS), (2 * D) ** -0.5, 0.15625, ((0, 8),))
    bias_table = gaussian(key_list[6], (NB, HEADS), 1.0, 4.0, ((0, 8),))
    up_weight = gaussian(key_list[7], (EXPERTS, FF, D), D ** -0.5, 0.21875, ((0, 8), (1, 16)))
    down_weight = gaussian(key_list[8], (EXPERTS, FF, D), FF ** -0.5, 0.109375, ((0, 8), (1, 16)))
    routes_keys = jax.random.split(jax.random.fold_in(key_list[9], 1), SEQS * SEQ_LEN // TOK_DEV)
    routes_turns = jax.random.permutation(jax.random.fold_in(key_list[9], 3), SEQS * SEQ_LEN // TOK_DEV)
    routes = jax.vmap(lambda own, number: deal_out(jax.random.fold_in(key_list[9], 2), own, number, TOK_DEV, EXPERTS, 2, CAP, 2))(routes_keys, routes_turns).reshape((SEQS, SEQ_LEN, 2))
    doc_lengths = draw_doc_lengths(jax.random.fold_in(key_list[12], 71), 0)
    cotangent = gaussian(key_list[11], (SEQS, SEQ_LEN, D), 1.0, 6.0, ((0, 8), (1, 16)))
    return dict(block_in=block_in, attn_gain=attn_gain, moe_gain=moe_gain, query_key_value_weight=query_key_value_weight, output_matrix=output_matrix, routing_weight=routing_weight, bias_table=bias_table, up_weight=up_weight, down_weight=down_weight, routes=routes, doc_lengths=doc_lengths, cotangent=cotangent)


epsilon = 1e-06
masked_score = -1e+30
largest_choice = lax.Precision.HIGHEST

@jax.custom_vjp
def low(v):
    return lax.optimization_barrier(v.astype(jnp.bfloat16)).astype(jnp.float32)

@jax.custom_vjp
def lower_backward(v):
    return v

def low_keep(v):
    return (low(v), None)

def low_pass(kept, grad):
    return (grad,)

def back_keep(v):
    return (v, None)

def back_low(kept, grad):
    return (low(grad),)
low.defvjp(low_keep, low_pass)
lower_backward.defvjp(back_keep, back_low)

def bucket_list(buckets, reach_len):
    exact_part = buckets // 2
    spread_part = buckets - exact_part
    thresholds = [int(math.ceil(exact_part * (reach_len / exact_part) ** (level_index / spread_part))) for level_index in range(1, spread_part)]
    result = []
    for distance in range(reach_len + 1):
        if distance < exact_part:
            result.append(distance)
        else:
            result.append(exact_part + sum((1 for limit_value in thresholds if distance >= limit_value)))
    return np.array(result, dtype=np.int32)

def rms_scale(values, gain_row):
    return values * lax.rsqrt(lax.optimization_barrier(jnp.mean(values * values, axis=-1, keepdims=True)) + epsilon) * gain_row

def document_ids(lengths, positions):
    bounds = jnp.cumsum(lengths)[:-1]
    return lax.optimization_barrier(jnp.sum((positions[:, None] >= bounds[None, :]).astype(jnp.int32), axis=1))

def sequence_attention(queries, keys, values, rel_rows, lengths):
    seq_len, head_count, head_size = queries.shape
    score_scale = 1.0 / math.sqrt(head_size)
    query_block = min(512, seq_len)
    key_pos = jnp.arange(seq_len, dtype=jnp.int32)
    key_doc = document_ids(lengths, key_pos)

    def one_block(block_start):
        block_queries = lax.dynamic_slice_in_dim(queries, block_start, query_block, 0)
        query_pos = block_start + jnp.arange(query_block, dtype=jnp.int32)
        query_doc = document_ids(lengths, query_pos)
        allowed = (key_pos[None, :] <= query_pos[:, None]) & (key_doc[None, :] == query_doc[:, None])
        distance = jnp.clip(query_pos[:, None] - key_pos[None, :], 0, MAXD)
        rel_bias = jnp.take(rel_rows, distance, axis=1)
        raw_scores = lower_backward(jnp.einsum('qhe,khe->hqk', block_queries, keys, precision=largest_choice))
        logits = jnp.where(allowed[None], raw_scores * score_scale + rel_bias, masked_score)
        row_max = lax.optimization_barrier(jnp.max(logits, axis=-1, keepdims=True))
        shifted = jnp.exp(logits - row_max)
        prob_rows = shifted / lax.optimization_barrier(jnp.sum(shifted, axis=-1, keepdims=True))
        return jnp.einsum('hqk,khe->qhe', low(prob_rows), values, precision=largest_choice)
    block_starts = jnp.arange(0, seq_len, query_block, dtype=jnp.int32)
    blocks = lax.map(jax.checkpoint(one_block), block_starts)
    return blocks.reshape(seq_len, head_count * head_size)

def layer(block_in, attn_gain, moe_gain, query_key_value_weight, output_matrix, routing_weight, bias_table, up_weight, down_weight, routes, doc_lengths):
    seq_count, seq_len, model_width = block_in.shape
    head_count = bias_table.shape[1]
    head_size = model_width // head_count
    experts_all = routing_weight.shape[1]
    hidden_first_layer = low(rms_scale(block_in, attn_gain))
    query_key_value_rows = jnp.einsum('kqa,ar->kqr', hidden_first_layer, query_key_value_weight, precision=largest_choice)
    queries = low(lower_backward(query_key_value_rows[..., :model_width])).reshape(seq_count, seq_len, head_count, head_size)
    keys = low(lower_backward(query_key_value_rows[..., model_width:2 * model_width])).reshape(seq_count, seq_len, head_count, head_size)
    values = low(lower_backward(query_key_value_rows[..., 2 * model_width:])).reshape(seq_count, seq_len, head_count, head_size)
    rel_rows = jnp.take(bias_table, jnp.asarray(bucket_list(bias_table.shape[0], MAXD)), axis=0).T

    def per_sequence(members):
        return sequence_attention(members[0], members[1], members[2], rel_rows, members[3])
    attention_result = lax.map(per_sequence, (queries, keys, values, doc_lengths))
    attention_result = low(lower_backward(attention_result))
    attention_projected = lower_backward(jnp.einsum('kqa,ar->kqr', attention_result, output_matrix, precision=largest_choice))
    x_mid = block_in + attention_projected
    hidden_second_layer = low(rms_scale(x_mid, moe_gain))
    routing_logits = lower_backward(jnp.einsum('kqa,ar->kqr', hidden_second_layer, routing_weight, precision=largest_choice))
    choose = (routes[..., None] == jnp.arange(experts_all, dtype=jnp.int32)).astype(jnp.float32)
    chosen = lax.optimization_barrier(jnp.sum(choose * routing_logits[:, :, None, :], axis=-1))
    gate_probs = jax.nn.softmax(chosen, axis=-1)
    tokens_all = seq_count * seq_len
    block_count = tokens_all // TOK_DEV
    block_routes = routes.reshape(block_count, TOK_DEV * 2)
    route_marks = (block_routes[..., None] == jnp.arange(experts_all, dtype=jnp.int32)).astype(jnp.int32)
    slot_rank = lax.optimization_barrier(jnp.sum(route_marks * (jnp.cumsum(route_marks, axis=1) - 1), axis=-1))
    slot_index = (jnp.arange(block_count, dtype=jnp.int32)[:, None] * CAP + slot_rank).reshape(tokens_all, 2)
    expert_index = routes.reshape(tokens_all, 2)
    flat_h = hidden_second_layer.reshape(tokens_all, model_width)
    buffer = jnp.zeros((experts_all, block_count * CAP, model_width), jnp.float32)
    buffer = buffer.at[expert_index, slot_index].set(jnp.broadcast_to(flat_h[:, None, :], (tokens_all, 2, model_width)))
    buffer = lower_backward(buffer)

    def one_expert(members):
        expert_in, up_rows, down_rows = members
        pre_act = lower_backward(jnp.dot(expert_in, up_rows.T, precision=largest_choice))
        hidden = low(jax.nn.gelu(pre_act))
        return jnp.dot(hidden, down_rows, precision=largest_choice)
    expert_out = low(lower_backward(lax.map(jax.checkpoint(one_expert), (buffer, up_weight, down_weight))))
    picked = expert_out[expert_index, slot_index]
    mixed_rows = x_mid.reshape(tokens_all, model_width) + lax.optimization_barrier(jnp.sum(gate_probs.reshape(tokens_all, 2)[..., None] * picked, axis=1))
    return mixed_rows.reshape(seq_count, seq_len, model_width)

def reference(block_in, attn_gain, moe_gain, query_key_value_weight, output_matrix, routing_weight, bias_table, up_weight, down_weight, routes, doc_lengths, cotangent):
    floats = tuple((tensor.astype(jnp.float32) for tensor in (block_in, attn_gain, moe_gain, query_key_value_weight, output_matrix, routing_weight, bias_table, up_weight, down_weight)))

    def closed(*params):
        return layer(*params, routes, doc_lengths)
    mixed_rows, pullback = jax.vjp(closed, *floats)
    grads = pullback(cotangent.astype(jnp.float32))
    return (mixed_rows.astype(jnp.bfloat16), grads[0], grads[1], grads[2], grads[3], grads[4], grads[5], grads[6], grads[7], grads[8])
```

```python
import functools
import math

import jax
import jax.numpy as jnp
import numpy as np
from jax import lax
from jax.experimental import pallas as pl
from jax.experimental.pallas import tpu as pltpu
from jax.sharding import PartitionSpec as P

MAXD = 128
BLOCK = 256
MESH = pl.DeviceIdType.MESH
VMEM_BYTES = 56 * 1024 * 1024

epsilon = 1e-06
masked_score = -1e30


def bucket_thresholds(buckets, reach_len):
    exact_part = buckets // 2
    spread_part = buckets - exact_part
    return [
        int(math.ceil(exact_part * (reach_len / exact_part) ** (level / spread_part)))
        for level in range(1, spread_part)
    ]


def exchange_kernel(plan, sizes, *refs):
    count = len(plan)
    ins, outs = refs[:count], refs[count : 2 * count]
    send_sem, recv_sem, own_sem = refs[2 * count :]
    axes = sorted({p["axis"] for p in plan})
    place = {a: lax.axis_index(a) for a in axes}

    barrier = pltpu.get_barrier_semaphore()
    total = 0
    for a in axes:
        for r in range(1, sizes[a]):
            peer = lax.rem(place[a] + r, sizes[a])
            pl.semaphore_signal(barrier, inc=1, device_id={a: peer}, device_id_type=MESH)
            total += 1
    pl.semaphore_wait(barrier, total)

    def guarded(condition, action):
        if condition is None:
            action()
        else:
            pl.when(condition)(action)

    def both(p, src, dst):
        n = sizes[p["axis"]]
        tests = []
        if p["senders"] < n:
            tests.append(src < p["senders"])
        if p["takers"] < n:
            tests.append(dst < p["takers"])
        if not tests:
            return None
        return functools.reduce(jnp.logical_and, tests)

    def copy(k, p, r, dst):
        me = place[p["axis"]]
        src_ref = ins[k].at[dst] if p["split"] else ins[k]
        return pltpu.make_async_remote_copy(
            src_ref=src_ref,
            dst_ref=outs[k].at[me],
            send_sem=send_sem.at[k, r],
            recv_sem=recv_sem.at[k, r],
            device_id={p["axis"]: dst},
            device_id_type=MESH,
        )

    def own(k, p):
        me = place[p["axis"]]
        src_ref = ins[k].at[me] if p["split"] else ins[k]
        return pltpu.make_async_copy(src_ref, outs[k].at[me], own_sem.at[k])

    def arrival(k, p, r, src):
        src_ref = ins[k].at[0] if p["split"] else ins[k]
        return pltpu.make_async_remote_copy(
            src_ref=src_ref,
            dst_ref=outs[k].at[src],
            send_sem=send_sem.at[k, r],
            recv_sem=recv_sem.at[k, r],
            device_id={p["axis"]: src},
            device_id_type=MESH,
        )

    widest = max(sizes[a] for a in axes)
    for r in range(1, widest):
        for k, p in enumerate(plan):
            n = sizes[p["axis"]]
            if r < n:
                me = place[p["axis"]]
                dst = lax.rem(me + r, n)
                guarded(both(p, me, dst), lambda k=k, p=p, r=r, dst=dst: copy(k, p, r, dst).start())
    for k, p in enumerate(plan):
        me = place[p["axis"]]
        guarded(both(p, me, me), lambda k=k, p=p: own(k, p).start())
    for k, p in enumerate(plan):
        me = place[p["axis"]]
        guarded(both(p, me, me), lambda k=k, p=p: own(k, p).wait())
    for r in range(1, widest):
        for k, p in enumerate(plan):
            n = sizes[p["axis"]]
            if r < n:
                me = place[p["axis"]]
                dst = lax.rem(me + r, n)
                src = lax.rem(me + n - r, n)
                guarded(
                    both(p, me, dst), lambda k=k, p=p, r=r, dst=dst: copy(k, p, r, dst).wait_send()
                )
                guarded(
                    both(p, src, me),
                    lambda k=k, p=p, r=r, src=src: arrival(k, p, r, src).wait_recv(),
                )


def exchange(sizes, number, moves):
    plan, arrays, shapes = [], [], []
    for array, axis, split, senders, takers in moves:
        n = sizes[axis]
        senders, takers = senders or n, takers or n
        plan.append(dict(axis=axis, split=split, senders=senders, takers=takers))
        arrays.append(array)
        piece = array.shape[1:] if split else array.shape
        shapes.append(jax.ShapeDtypeStruct((senders,) + piece, array.dtype))
    widest = max(sizes[p["axis"]] for p in plan)
    return pl.pallas_call(
        functools.partial(exchange_kernel, plan, sizes),
        out_shape=shapes,
        in_specs=[pl.BlockSpec(memory_space=pl.ANY)] * len(plan),
        out_specs=[pl.BlockSpec(memory_space=pl.ANY)] * len(plan),
        scratch_shapes=[
            pltpu.SemaphoreType.DMA((len(plan), widest)),
            pltpu.SemaphoreType.DMA((len(plan), widest)),
            pltpu.SemaphoreType.DMA((len(plan),)),
        ],
        compiler_params=pltpu.CompilerParams(
            collective_id=number, has_side_effects=True, vmem_limit_bytes=4 * 1024 * 1024
        ),
        cost_estimate=pl.CostEstimate(flops=0, bytes_accessed=20_000_000, transcendentals=0),
        name=f"exchange_{number}",
    )(*arrays)


def dot_nt(left, right):
    return lax.dot_general(
        left, right, (((1,), (1,)), ((), ())), preferred_element_type=jnp.float32
    )


def dot_nn(left, right):
    return jnp.dot(left, right, preferred_element_type=jnp.float32)


def near_buckets(buckets, offset, rows, cols):
    key = lax.broadcasted_iota(jnp.int32, (rows, cols), 0)
    query = lax.broadcasted_iota(jnp.int32, (rows, cols), 1)
    distance = jnp.clip(query - key + offset, 0, MAXD)
    bucket = jnp.minimum(distance, buckets // 2)
    for level in bucket_thresholds(buckets, MAXD):
        bucket = bucket + (distance >= level).astype(jnp.int32)
    return bucket


def near_bias(table_ref, buckets, offset, rows, cols):
    bucket = near_buckets(buckets, offset, rows, cols)
    last = table_ref[buckets - 1]
    bias = jnp.zeros((rows, cols), jnp.float32)
    for b in range(buckets - 1):
        bias = jnp.where(bucket == b, table_ref[b] - last, bias)
    return bias


def first_keys(bounds_ref, start):
    query = start + lax.broadcasted_iota(jnp.int32, (1, BLOCK), 1)
    first = jnp.zeros((1, BLOCK), jnp.int32)
    for d in range(3):
        first = jnp.where(query >= bounds_ref[d], bounds_ref[d], first)
    return first


def block_scores(i, j, blocks, q, k, diag_bias, side_bias, first):
    s = dot_nt(k, q)
    half = BLOCK // 2
    if j == i:
        s = s + diag_bias
    elif j == i - 1:
        lower = jnp.concatenate([s[half:, :half] + side_bias, s[half:, half:]], axis=1)
        s = jnp.concatenate([s[:half], lower], axis=0)
    if j == i or j == 0 or i == blocks - 1:
        key = lax.broadcasted_iota(jnp.int32, (BLOCK, BLOCK), 0)
        keep = key + j * BLOCK >= first
        if j == i:
            keep = keep & (key <= lax.broadcasted_iota(jnp.int32, (BLOCK, BLOCK), 1))
        s = jnp.where(keep, s, masked_score)
    return s


def forward_kernel(
    buckets,
    x_ref,
    w_ref,
    gain_ref,
    table_ref,
    bounds_ref,
    out_ref,
    h_ref,
    q_ref,
    k_ref,
    v_ref,
    stat_ref,
    vt_ref,
    diag_ref,
    side_ref,
):
    rows = x_ref.shape[0]
    blocks = rows // BLOCK
    half = BLOCK // 2
    size = q_ref.shape[1]
    scale = 1.0 / math.sqrt(size)

    @pl.loop(0, blocks)
    def _(b):
        at = pl.ds(pl.multiple_of(b * BLOCK, BLOCK), BLOCK)
        x = x_ref[at, :].astype(jnp.float32)
        mean = jnp.mean(x * x, axis=-1, keepdims=True)
        h = (x * lax.rsqrt(mean + epsilon) * gain_ref[...]).astype(jnp.bfloat16)
        h_ref[at, :] = h
        qkv = dot_nn(h, w_ref[...])
        q_ref[at, :] = (qkv[:, :size].astype(jnp.bfloat16) * scale).astype(jnp.bfloat16)
        k_ref[at, :] = qkv[:, size : 2 * size].astype(jnp.bfloat16)
        v = qkv[:, 2 * size :]
        v_ref[at, :] = v.astype(jnp.bfloat16)
        vt_ref[:, at] = v.T.astype(jnp.bfloat16)

    diag_ref[...] = near_bias(table_ref, buckets, 0, BLOCK, BLOCK)
    side_ref[...] = near_bias(table_ref, buckets, half, half, half)

    for i in range(blocks):
        q = q_ref[i * BLOCK : (i + 1) * BLOCK, :]
        first = first_keys(bounds_ref, i * BLOCK)
        scores = []
        top = None
        for j in range(i + 1):
            s = block_scores(
                i,
                j,
                blocks,
                q,
                k_ref[j * BLOCK : (j + 1) * BLOCK, :],
                diag_ref[...],
                side_ref[...],
                first,
            )
            scores.append(s)
            here = jnp.max(s, axis=0, keepdims=True)
            top = here if top is None else jnp.maximum(top, here)
        total = jnp.zeros((1, BLOCK), jnp.float32)
        for j in range(i + 1):
            scores[j] = jnp.exp(scores[j] - top)
            total = total + jnp.sum(scores[j], axis=0, keepdims=True)
        inverse = 1.0 / total
        mixed = jnp.zeros((size, BLOCK), jnp.float32)
        for j in range(i + 1):
            probs = (scores[j] * inverse).astype(jnp.bfloat16)
            mixed = mixed + dot_nn(vt_ref[:, j * BLOCK : (j + 1) * BLOCK], probs)
        out_ref[i * BLOCK : (i + 1) * BLOCK, :] = mixed.T.astype(jnp.bfloat16)
        stat_ref[i : i + 1, :] = top + jnp.log(total)


def backward_kernel(
    buckets,
    q_ref,
    k_ref,
    v_ref,
    stat_ref,
    do_ref,
    table_ref,
    bounds_ref,
    grad_ref,
    bias_ref,
    kt_ref,
    dk_ref,
    dv_ref,
    diag_ref,
    side_ref,
    diag_sum,
    side_sum,
):
    rows, size = q_ref.shape
    blocks = rows // BLOCK
    half = BLOCK // 2
    scale = 1.0 / math.sqrt(size)

    kt_ref[...] = k_ref[...].astype(jnp.float32).T.astype(jnp.bfloat16)
    diag_ref[...] = near_bias(table_ref, buckets, 0, BLOCK, BLOCK)
    side_ref[...] = near_bias(table_ref, buckets, half, half, half)
    diag_sum[...] = jnp.zeros_like(diag_sum)
    side_sum[...] = jnp.zeros_like(side_sum)
    dk_ref[...] = jnp.zeros_like(dk_ref)
    dv_ref[...] = jnp.zeros_like(dv_ref)
    far = jnp.zeros((1, BLOCK), jnp.float32)

    for i in range(blocks):
        mine = slice(i * BLOCK, (i + 1) * BLOCK)
        q, do = q_ref[mine, :], do_ref[mine, :]
        first = first_keys(bounds_ref, i * BLOCK)
        stat = stat_ref[i : i + 1, :]
        probs, grads = [], []
        delta = jnp.zeros((1, BLOCK), jnp.float32)
        for j in range(i + 1):
            at = slice(j * BLOCK, (j + 1) * BLOCK)
            s = block_scores(
                i, j, blocks, q, k_ref[at, :], diag_ref[...], side_ref[...], first
            )
            p = jnp.exp(s - stat)
            dp = dot_nt(v_ref[at, :], do)
            delta = delta + jnp.sum(p * dp, axis=0, keepdims=True)
            probs.append(p)
            grads.append(dp)
        dqt = jnp.zeros((size, BLOCK), jnp.float32)
        for j in range(i + 1):
            at = slice(j * BLOCK, (j + 1) * BLOCK)
            ds = probs[j] * (grads[j] - delta)
            if j == i:
                diag_sum[...] += ds
            elif j == i - 1:
                side_sum[...] += ds
            else:
                far = far + jnp.sum(ds, axis=0, keepdims=True)
            low = ds.astype(jnp.bfloat16)
            dk_ref[at, :] += dot_nn(low, q)
            dv_ref[at, :] += dot_nn(probs[j].astype(jnp.bfloat16), do)
            dqt = dqt + dot_nn(kt_ref[:, at], low)
        grad_ref[mine, :size] = (dqt.T * scale).astype(jnp.bfloat16)
    grad_ref[:, size : 2 * size] = dk_ref[...].astype(jnp.bfloat16)
    grad_ref[:, 2 * size :] = dv_ref[...].astype(jnp.bfloat16)

    far = far + jnp.sum(side_sum[:half, :], axis=0, keepdims=True)
    far_half = jnp.sum(side_sum[half:, half:], axis=0, keepdims=True)
    far = far + jnp.concatenate([jnp.zeros_like(far_half), far_half], axis=1)
    diag_bucket = near_buckets(buckets, 0, BLOCK, BLOCK)
    side_bucket = near_buckets(buckets, half, half, half)
    for b in range(buckets):
        one = jnp.sum(jnp.where(diag_bucket == b, diag_sum[...], 0.0), axis=0, keepdims=True)
        two = jnp.sum(
            jnp.where(side_bucket == b, side_sum[half:, :half], 0.0), axis=0, keepdims=True
        )
        row = one + jnp.concatenate([two, jnp.zeros_like(two)], axis=1)
        if b == buckets - 1:
            row = row + far
        bias_ref[b : b + 1, :] = row


def in_vmem(count):
    return [pl.BlockSpec(memory_space=pltpu.VMEM)] * count


def in_smem(count):
    return [pl.BlockSpec(memory_space=pltpu.SMEM)] * count


def attention_forward(x_rows, weight, gain, table, bounds):
    rows, width = x_rows.shape
    size = weight.shape[1] // 3
    buckets = table.shape[0]
    low, full = jnp.bfloat16, jnp.float32
    return pl.pallas_call(
        functools.partial(forward_kernel, buckets),
        out_shape=[
            jax.ShapeDtypeStruct((rows, size), low),
            jax.ShapeDtypeStruct((rows, width), low),
            jax.ShapeDtypeStruct((rows, size), low),
            jax.ShapeDtypeStruct((rows, size), low),
            jax.ShapeDtypeStruct((rows, size), low),
            jax.ShapeDtypeStruct((rows // BLOCK, BLOCK), full),
        ],
        in_specs=in_vmem(3) + in_smem(2),
        out_specs=in_vmem(6),
        scratch_shapes=[
            pltpu.VMEM((size, rows), low),
            pltpu.VMEM((BLOCK, BLOCK), full),
            pltpu.VMEM((BLOCK // 2, BLOCK // 2), full),
        ],
        compiler_params=pltpu.CompilerParams(vmem_limit_bytes=VMEM_BYTES),
        cost_estimate=pl.CostEstimate(
            flops=8_000_000_000, bytes_accessed=10_000_000, transcendentals=2_400_000
        ),
        name="attention_forward",
    )(x_rows, weight, gain, table, bounds)


def attention_backward(q, k, v, stat, do, table, bounds):
    rows, size = q.shape
    buckets = table.shape[0]
    low, full = jnp.bfloat16, jnp.float32
    return pl.pallas_call(
        functools.partial(backward_kernel, buckets),
        out_shape=[
            jax.ShapeDtypeStruct((rows, 3 * size), low),
            jax.ShapeDtypeStruct((buckets, BLOCK), full),
        ],
        in_specs=in_vmem(5) + in_smem(2),
        out_specs=in_vmem(2),
        scratch_shapes=[
            pltpu.VMEM((size, rows), low),
            pltpu.VMEM((rows, size), full),
            pltpu.VMEM((rows, size), full),
            pltpu.VMEM((BLOCK, BLOCK), full),
            pltpu.VMEM((BLOCK // 2, BLOCK // 2), full),
            pltpu.VMEM((BLOCK, BLOCK), full),
            pltpu.VMEM((BLOCK, BLOCK), full),
        ],
        compiler_params=pltpu.CompilerParams(vmem_limit_bytes=VMEM_BYTES),
        cost_estimate=pl.CostEstimate(
            flops=12_000_000_000, bytes_accessed=10_000_000, transcendentals=2_400_000
        ),
        name="attention_backward",
    )(q, k, v, stat, do, table, bounds)


def rms_scale(values, gain_row):
    return (
        values * lax.rsqrt(jnp.mean(values * values, axis=-1, keepdims=True) + epsilon) * gain_row
    )


def gelu_back(pre_act, grad_hidden):
    return jax.vjp(jax.nn.gelu, pre_act)[1](grad_hidden)[0]


def contract_rows(left, right):
    return lax.dot_general(
        left, right, (((0,), (0,)), ((), ())), preferred_element_type=jnp.float32
    )


def local(
    sizes,
    block_in,
    attn_gain,
    moe_gain,
    query_key_value_weight,
    output_matrix,
    routing_weight,
    bias_table,
    up_weight,
    down_weight,
    routes,
    doc_lengths,
    cotangent,
):
    low, full = jnp.bfloat16, jnp.float32
    n_ctx, n_exp = sizes["ctx"], sizes["exp"]
    rows, width = block_in.shape[1:]
    seq_len = rows * n_ctx
    share = width // n_exp
    buckets = bias_table.shape[0] * n_exp
    heads = bias_table.shape[1]
    size = width // heads
    experts = routing_weight.shape[1]
    x_low = block_in[0]
    x_in = x_low.astype(full)

    expert_weights = lax.all_gather(
        jnp.concatenate([up_weight, down_weight], axis=0), "ctx", axis=1, tiled=True
    )

    head = jnp.minimum(lax.axis_index("ctx"), heads - 1)
    own_columns = [
        lax.dynamic_slice_in_dim(query_key_value_weight, part * width + head * size, size, 1)
        for part in range(3)
    ]
    table_rows = jnp.pad(bias_table, ((0, share - bias_table.shape[0]), (0, 0)))
    packed = jnp.concatenate(
        [output_matrix]
        + own_columns
        + [routing_weight, attn_gain[:, None], moe_gain[:, None], table_rows],
        axis=1,
    )
    packed = jnp.pad(packed, ((0, 0), (0, -packed.shape[1] % 128)))
    x_rows, dense = exchange(
        sizes, 1, [(x_low, "ctx", False, None, heads), (packed, "exp", False, None, None)]
    )
    flat = dense.reshape(width, packed.shape[1])
    proj_full = flat[:, :width]
    head_weight = flat[:, width : width + 3 * size]
    at = width + 3 * size
    router_full = flat[:, at : at + experts]
    gain_one = flat[:, at + experts].astype(full)
    gain_two = flat[:, at + experts + 1].astype(full)
    table_full = dense[:, : bias_table.shape[0], at + experts + 2 : at + experts + 2 + heads]
    table_full = table_full.reshape(buckets, heads).astype(full)
    table_head = lax.dynamic_slice_in_dim(table_full, head, 1, 1)[:, 0]
    bounds = jnp.cumsum(doc_lengths[0]).astype(jnp.int32)

    mixed, h_rows, q, k, v, stat = attention_forward(
        x_rows.reshape(seq_len, width), head_weight, gain_one[None], table_head, bounds
    )
    (attended,) = exchange(
        sizes, 2, [(mixed.reshape(n_ctx, rows, size), "ctx", True, heads, None)]
    )
    attended = jnp.transpose(attended, (1, 0, 2)).reshape(rows, width)

    late_weight, attended = lax.optimization_barrier((query_key_value_weight, attended))
    qkv_full = lax.all_gather(late_weight, "exp", axis=0, tiled=True)

    x_mid = x_in + jnp.dot(attended, proj_full, preferred_element_type=full)
    h_second = rms_scale(x_mid, gain_two).astype(low)
    routing_logits = jnp.dot(h_second, router_full, preferred_element_type=full)
    route = routes[0]
    choose = (route[:, :, None] == jnp.arange(experts, dtype=jnp.int32)).astype(full)
    gates = jax.nn.softmax(jnp.sum(choose * routing_logits[:, None, :], axis=-1), axis=-1)
    capacity = min(rows, 4 * rows // experts)
    flat_routes = route.reshape(2 * rows)
    marks = (flat_routes[:, None] == jnp.arange(experts, dtype=jnp.int32)).astype(full)
    before = jnp.asarray(np.tril(np.ones((2 * rows, 2 * rows), np.float32), -1), low)
    rank = jnp.sum(marks * jnp.dot(before, marks.astype(low), preferred_element_type=full), axis=-1)
    slot = (flat_routes * capacity + rank.astype(jnp.int32)).reshape(rows, 2)
    slots = jnp.arange(experts * capacity, dtype=jnp.int32)[:, None]
    place = [(slots == slot[:, c][None, :]) for c in range(2)]
    place_low = [p.astype(low) for p in place]
    grad_out = cotangent[0].astype(full)
    send_rows = jnp.dot(
        place_low[0] + place_low[1], h_second, preferred_element_type=full
    ).astype(low)
    gated = [(gates[:, c : c + 1] * grad_out).astype(low) for c in range(2)]
    send_grads = (
        jnp.dot(
            jnp.concatenate(place_low, axis=1),
            jnp.concatenate(gated, axis=0),
            preferred_element_type=full,
        )
    ).astype(low)
    piece = (experts, capacity, width)
    expert_rows, grad_rows = exchange(
        sizes,
        3,
        [
            (send_rows.reshape(piece), "exp", True, None, None),
            (send_grads.reshape(piece), "exp", True, None, None),
        ],
    )
    expert_rows = expert_rows.reshape(experts * capacity, width)
    grad_rows = grad_rows.reshape(experts * capacity, width)

    up_full, down_full = expert_weights[0], expert_weights[1]
    pre_act = lax.dot_general(
        expert_rows, up_full, (((1,), (1,)), ((), ())), preferred_element_type=full
    )
    hidden = jax.nn.gelu(pre_act).astype(low)
    grad_hidden = lax.dot_general(
        grad_rows, down_full, (((1,), (1,)), ((), ())), preferred_element_type=full
    )
    grad_pre = gelu_back(pre_act, grad_hidden).astype(low)
    up_terms = contract_rows(grad_pre, expert_rows).astype(low)
    down_terms = contract_rows(hidden, grad_rows).astype(low)
    weight_grads = lax.psum_scatter(
        jnp.concatenate([up_terms, down_terms], axis=1), "ctx", scatter_dimension=0, tiled=True
    ).astype(full)
    grad_up = weight_grads[None, :, :width]
    grad_down = weight_grads[None, :, width:]
    expert_out = jnp.dot(hidden, down_full, preferred_element_type=full).astype(low)
    expert_back = jnp.dot(grad_pre, up_full, preferred_element_type=full).astype(low)
    returned, grad_back = exchange(
        sizes,
        4,
        [
            (expert_out.reshape(piece), "exp", True, None, None),
            (expert_back.reshape(piece), "exp", True, None, None),
        ],
    )
    returned = returned.reshape(experts * capacity, width)
    grad_back = grad_back.reshape(experts * capacity, width)
    picked = [jnp.take(returned, slot[:, c], axis=0).astype(full) for c in range(2)]
    block_out = (
        (x_mid + (gates[:, :1] * picked[0] + gates[:, 1:] * picked[1])).astype(low)[None]
    )
    grad_gates = jnp.stack([jnp.sum(grad_out * picked[c], axis=-1) for c in range(2)], axis=-1)
    grad_chosen = gates * (grad_gates - jnp.sum(gates * grad_gates, axis=-1, keepdims=True))
    grad_logits = jnp.sum(choose * grad_chosen[:, :, None], axis=1).astype(low)
    grad_h_second = jnp.take(grad_back, slot[:, 0], axis=0).astype(full) + jnp.take(
        grad_back, slot[:, 1], axis=0
    ).astype(full)
    grad_h_second = grad_h_second + dot_nt(grad_logits, router_full)
    grad_router = contract_rows(h_second, grad_logits)
    grad_x_norm, grad_gain_two = jax.vjp(rms_scale, x_mid, gain_two)[1](grad_h_second)
    grad_x_mid = grad_out + grad_x_norm
    grad_proj = grad_x_mid.astype(low)
    grad_attended = dot_nt(grad_proj, proj_full).astype(low)
    grad_attended = jnp.transpose(grad_attended.reshape(rows, heads, size), (1, 0, 2))
    (do_rows,) = exchange(sizes, 5, [(grad_attended, "ctx", True, None, heads)])

    grad_head, bias_rows = attention_backward(
        q, k, v, stat, do_rows.reshape(seq_len, size), table_head, bounds
    )
    out_terms = contract_rows(attended, grad_proj).astype(low).reshape(n_exp, share, width)
    grad_qkv_rows, out_parts = exchange(
        sizes,
        6,
        [
            (grad_head.reshape(n_ctx, rows, 3 * size), "ctx", True, heads, None),
            (out_terms, "exp", True, None, None),
        ],
    )
    grad_qkv_rows = jnp.transpose(
        grad_qkv_rows.reshape(heads, rows, 3, size), (1, 2, 0, 3)
    ).reshape(rows, 3 * width)
    grad_h_first = dot_nt(grad_qkv_rows, qkv_full)
    grad_x_first, grad_gain_one = jax.vjp(rms_scale, x_in, gain_one)[1](grad_h_first)
    grad_in = (grad_x_mid + grad_x_first)[None]

    head_terms = contract_rows(h_rows, grad_head).astype(low).reshape(n_exp, share, 3 * size)
    small = jnp.concatenate(
        [
            grad_gain_one.reshape(n_exp, share),
            grad_gain_two.reshape(n_exp, share),
            grad_router.reshape(n_exp, share * experts),
            jnp.sum(bias_rows, axis=1).reshape(n_exp, buckets // n_exp),
        ],
        axis=1,
    )
    used = small.shape[1]
    small = jnp.pad(small, ((0, 0), (0, -used % 1024))).reshape(n_exp, -1, 128)
    out_pieces = jnp.sum(out_parts.astype(full), axis=0).reshape(n_ctx, share // n_ctx, width)
    head_parts, small_parts, out_ready = exchange(
        sizes,
        7,
        [
            (head_terms, "exp", True, None, None),
            (small, "exp", True, None, None),
            (out_pieces, "ctx", True, None, None),
        ],
    )
    head_sum = jnp.sum(head_parts.astype(full), axis=0).astype(low)
    small_sum = jnp.sum(small_parts, axis=0)
    out_sum = jnp.sum(out_ready, axis=0)
    head_all, small_all, out_all = exchange(
        sizes,
        8,
        [
            (head_sum, "ctx", False, heads, None),
            (small_sum, "ctx", False, None, None),
            (out_sum, "ctx", False, None, None),
        ],
    )
    grad_qkv = (
        jnp.transpose(head_all.reshape(heads, share, 3, size), (1, 2, 0, 3))
        .reshape(share, 3 * width)
        .astype(full)
    )
    grad_out_weight = out_all.reshape(share, width)
    small_all = small_all.reshape(n_ctx, -1)
    sums = jnp.sum(small_all[:, : used - buckets // n_exp], axis=0)
    grad_table = small_all[:heads, used - buckets // n_exp : used].T
    return (
        block_out,
        grad_in,
        sums[:share],
        sums[share : 2 * share],
        grad_qkv,
        grad_out_weight,
        sums[2 * share :].reshape(share, experts),
        grad_table,
        grad_up,
        grad_down,
    )


def solution(mesh):
    sizes = {name: mesh.shape[name] for name in ("ctx", "exp")}
    tokens = P("exp", "ctx", None)
    row_split = P("exp", None)
    return jax.shard_map(
        functools.partial(local, sizes),
        mesh=mesh,
        in_specs=(
            tokens,
            P("exp"),
            P("exp"),
            row_split,
            row_split,
            row_split,
            row_split,
            tokens,
            tokens,
            tokens,
            row_split,
            tokens,
        ),
        out_specs=(
            tokens,
            tokens,
            P("exp"),
            P("exp"),
            row_split,
            row_split,
            row_split,
            row_split,
            tokens,
            tokens,
        ),
        check_vma=False,
    )
```

```python
import functools
import math

import jax
import jax.numpy as jnp
import numpy as np
from jax import lax
from jax.experimental import pallas as pl
from jax.experimental.pallas import tpu as pltpu
from jax.sharding import PartitionSpec as P

MAXD = 128
BLOCK = 256
MESH = pl.DeviceIdType.MESH
VMEM_BYTES = 40 * 1024 * 1024

epsilon = 1e-06
masked_score = -1e30


def bucket_thresholds(buckets, reach_len):
    exact_part = buckets // 2
    spread_part = buckets - exact_part
    return [
        int(math.ceil(exact_part * (reach_len / exact_part) ** (level / spread_part)))
        for level in range(1, spread_part)
    ]


def guarded(tests, action):
    tests = [t for t in tests if t is not None]
    if not tests:
        action()
    else:
        pl.when(functools.reduce(jnp.logical_and, tests))(action)


def greet(sizes, axes):
    barrier = pltpu.get_barrier_semaphore()
    total = 0
    for a in axes:
        me = lax.axis_index(a)
        for r in range(1, sizes[a]):
            peer = lax.rem(me + r, sizes[a])
            pl.semaphore_signal(barrier, inc=1, device_id={a: peer}, device_id_type=MESH)
            total += 1
    pl.semaphore_wait(barrier, total)


class Move:
    def __init__(self, sizes, axis, src, out, sems, split=False, senders=None, takers=None):
        self.n = sizes[axis]
        self.axis, self.src, self.out, self.split = axis, src, out, split
        self.send_sem, self.recv_sem, self.own_sem = sems
        self.senders, self.takers = senders or self.n, takers or self.n
        self.me = lax.axis_index(axis)

    def sends(self, device):
        return device < self.senders if self.senders < self.n else None

    def takes(self, device):
        return device < self.takers if self.takers < self.n else None

    def copy(self, r, peer, slot, piece):
        return pltpu.make_async_remote_copy(
            src_ref=self.src.at[piece] if self.split else self.src,
            dst_ref=self.out.at[slot],
            send_sem=self.send_sem.at[r],
            recv_sem=self.recv_sem.at[r],
            device_id={self.axis: peer},
            device_id_type=MESH,
        )

    def to(self, r):
        return lax.rem(self.me + r, self.n)

    def start(self, r):
        dst = self.to(r)
        guarded(
            [self.sends(self.me), self.takes(dst)],
            lambda: self.copy(r, dst, self.me, dst).start(),
        )

    def own(self):
        src = self.src.at[self.me] if self.split else self.src
        return pltpu.make_async_copy(src, self.out.at[self.me], self.own_sem)

    def start_own(self):
        guarded([self.sends(self.me), self.takes(self.me)], lambda: self.own().start())

    def wait(self):
        guarded([self.sends(self.me), self.takes(self.me)], lambda: self.own().wait())
        for r in range(1, self.n):
            src = lax.rem(self.me + self.n - r, self.n)
            guarded(
                [self.sends(src), self.takes(self.me)],
                lambda: self.copy(r, src, src, 0).wait_recv(),
            )

    def wait_sent(self):
        for r in range(1, self.n):
            dst = self.to(r)
            guarded(
                [self.sends(self.me), self.takes(dst)],
                lambda: self.copy(r, dst, self.me, dst).wait_send(),
            )


def start_all(moves):
    for r in range(1, max(m.n for m in moves)):
        for m in moves:
            if r < m.n:
                m.start(r)
    for m in moves:
        m.start_own()


class PairGather:
    def __init__(self, sizes, src, out, sems):
        self.n = sizes["exp"]
        self.src, self.out = src, out
        self.send_sem, self.recv_sem, self.own_sem = sems
        self.me = lax.axis_index("exp")
        core = lax.rem(self.me, 2)
        self.mate = self.me + 1 - 2 * core

    def copy(self, src, slot, k, peer):
        return pltpu.make_async_remote_copy(
            src_ref=src,
            dst_ref=self.out.at[slot],
            send_sem=self.send_sem.at[k],
            recv_sem=self.recv_sem.at[k],
            device_id={"exp": peer},
            device_id_type=MESH,
        )

    def own(self):
        return pltpu.make_async_copy(self.src, self.out.at[self.me], self.own_sem)

    def chips(self):
        return range(1, self.n // 2)

    def start(self):
        for r in self.chips():
            self.copy(self.src, self.me, r, lax.rem(self.me + 2 * r, self.n)).start()
        self.copy(self.src, self.me, 0, self.mate).start()
        self.own().start()

    def forward(self, r):
        slot = lax.rem(self.me + self.n - 2 * r, self.n)
        return self.copy(self.out.at[slot], slot, self.n // 2 + r, self.mate)

    def pass_on(self):
        for r in self.chips():
            slot = lax.rem(self.me + self.n - 2 * r, self.n)
            self.copy(self.src, slot, r, slot).wait_recv()
            self.forward(r).start()

    def finish(self):
        for r in self.chips():
            slot = lax.rem(self.mate + self.n - 2 * r, self.n)
            self.copy(self.src, slot, self.n // 2 + r, self.mate).wait_recv()
            self.forward(r).wait_send()
            self.copy(self.src, self.me, r, lax.rem(self.me + 2 * r, self.n)).wait_send()
        self.copy(self.src, self.mate, 0, self.mate).wait_recv()
        self.copy(self.src, self.me, 0, self.mate).wait_send()
        self.own().wait()


def move_sems(count):
    return [
        pltpu.SemaphoreType.DMA((count,)),
        pltpu.SemaphoreType.DMA((count,)),
        pltpu.SemaphoreType.DMA,
    ]


def any_space(count):
    return [pl.BlockSpec(memory_space=pl.ANY)] * count


def in_vmem(count):
    return [pl.BlockSpec(memory_space=pltpu.VMEM)] * count


def in_smem(count):
    return [pl.BlockSpec(memory_space=pltpu.SMEM)] * count


def remote_params(number, limit=VMEM_BYTES):
    return pltpu.CompilerParams(
        collective_id=number, has_side_effects=True, vmem_limit_bytes=limit
    )


def cost(flops, moved, special=0):
    return pl.CostEstimate(flops=flops, bytes_accessed=moved, transcendentals=special)


def gather_dense(sizes, weight, small):
    n = sizes["exp"]

    def kernel(w_ref, s_ref, w_out, s_out, *sems):
        greet(sizes, ["exp"])
        big = PairGather(sizes, w_ref, w_out, sems[:3])
        little = Move(sizes, "exp", s_ref, s_out, sems[3:])
        start_all([little])
        big.start()
        big.pass_on()
        big.finish()
        little.wait()
        little.wait_sent()

    return pl.pallas_call(
        kernel,
        out_shape=[jax.ShapeDtypeStruct((n,) + a.shape, a.dtype) for a in (weight, small)],
        in_specs=any_space(2),
        out_specs=any_space(2),
        scratch_shapes=move_sems(n) + move_sems(n),
        compiler_params=remote_params(1, 4 * 1024 * 1024),
        cost_estimate=cost(0, 40_000_000),
        name="gather_dense",
    )(weight, small)


def swap_experts(sizes, number, rows, values):
    n = sizes["exp"]

    def kernel(a_ref, b_ref, a_out, b_out, *sems):
        greet(sizes, ["exp"])
        one = Move(sizes, "exp", a_ref, a_out, sems[:3], split=True)
        two = Move(sizes, "exp", b_ref, b_out, sems[3:], split=True)
        start_all([two, one])
        for m in (two, one):
            m.wait()
        for m in (two, one):
            m.wait_sent()

    return pl.pallas_call(
        kernel,
        out_shape=[jax.ShapeDtypeStruct(a.shape, a.dtype) for a in (rows, values)],
        in_specs=any_space(2),
        out_specs=any_space(2),
        scratch_shapes=move_sems(n) + move_sems(n),
        compiler_params=remote_params(number, 4 * 1024 * 1024),
        cost_estimate=cost(0, 30_000_000),
        name=f"swap_experts_{number}",
    )(rows, values)


def dot_nt(left, right):
    return lax.dot_general(
        left, right, (((1,), (1,)), ((), ())), preferred_element_type=jnp.float32
    )


def dot_tn(left, right):
    return lax.dot_general(
        left, right, (((0,), (0,)), ((), ())), preferred_element_type=jnp.float32
    )


def dot_nn(left, right):
    return jnp.dot(left, right, preferred_element_type=jnp.float32)


def near_buckets(buckets, offset, rows, cols):
    key = lax.broadcasted_iota(jnp.int32, (rows, cols), 0)
    query = lax.broadcasted_iota(jnp.int32, (rows, cols), 1)
    distance = jnp.clip(query - key + offset, 0, MAXD)
    bucket = jnp.minimum(distance, buckets // 2)
    for level in bucket_thresholds(buckets, MAXD):
        bucket = bucket + (distance >= level).astype(jnp.int32)
    return bucket


def near_bias(table_ref, buckets, offset, rows, cols):
    bucket = near_buckets(buckets, offset, rows, cols)
    last = table_ref[buckets - 1]
    bias = jnp.zeros((rows, cols), jnp.float32)
    for b in range(buckets - 1):
        bias = jnp.where(bucket == b, table_ref[b] - last, bias)
    return bias


def first_keys(bounds_ref, start):
    query = start + lax.broadcasted_iota(jnp.int32, (1, BLOCK), 1)
    first = jnp.zeros((1, BLOCK), jnp.int32)
    for d in range(3):
        first = jnp.where(query >= bounds_ref[d], bounds_ref[d], first)
    return first


def block_scores(i, j, blocks, qt, k, diag_bias, side_bias, first):
    s = dot_nn(k, qt)
    half = BLOCK // 2
    if j == i:
        s = s + diag_bias
    elif j == i - 1:
        lower = jnp.concatenate([s[half:, :half] + side_bias, s[half:, half:]], axis=1)
        s = jnp.concatenate([s[:half], lower], axis=0)
    if j == i or j == 0 or i == blocks - 1:
        key = lax.broadcasted_iota(jnp.int32, (BLOCK, BLOCK), 0)
        keep = key + j * BLOCK >= first
        if j == i:
            keep = keep & (key <= lax.broadcasted_iota(jnp.int32, (BLOCK, BLOCK), 1))
        s = jnp.where(keep, s, masked_score)
    return s


def transposed(piece):
    return piece.astype(jnp.float32).T.astype(jnp.bfloat16)


def scaled_queries(qkv_ref, i, size):
    scale = 1.0 / math.sqrt(size)
    both = jnp.concatenate([qkv_ref[2 * i, :size, :], qkv_ref[2 * i + 1, :size, :]], axis=1)
    return (both * scale).astype(jnp.bfloat16)


def block_of(j):
    return slice(j * BLOCK, (j + 1) * BLOCK)


def forward_kernel(
    sizes,
    heads,
    buckets,
    qkv_in,
    proj_in,
    g_in,
    table_ref,
    bounds_ref,
    mixed_out,
    proj_out,
    g_out,
    qkv_ref,
    stat_ref,
    sent_ref,
    k_ref,
    vt_ref,
    diag_ref,
    side_ref,
    *sems,
):
    parts, _, rows = qkv_ref.shape
    size = sent_ref.shape[1]
    blocks = parts * rows // BLOCK
    half = BLOCK // 2
    greet(sizes, ["ctx", "exp"])
    arrive = Move(sizes, "ctx", qkv_in, qkv_ref, sems[0:3], split=True, takers=heads)
    back = Move(sizes, "ctx", sent_ref, mixed_out, sems[3:6], split=True, senders=heads)
    proj = PairGather(sizes, proj_in, proj_out, sems[6:9])
    grads = Move(sizes, "exp", g_in, g_out, sems[9:12], split=True)
    start_all([arrive])
    proj.start()
    start_all([grads])
    diag_ref[...] = near_bias(table_ref, buckets, 0, BLOCK, BLOCK)
    side_ref[...] = near_bias(table_ref, buckets, half, half, half)
    proj.pass_on()
    arrive.wait()

    @pl.when(lax.axis_index("ctx") < heads)
    def _():
        for c in range(parts):
            at = slice(c * rows, (c + 1) * rows)
            k_ref[at, :] = transposed(qkv_ref[c, size : 2 * size, :])
            vt_ref[:, at] = qkv_ref[c, 2 * size :, :]
        for i in range(blocks):
            qt = scaled_queries(qkv_ref, i, size)
            first = first_keys(bounds_ref, i * BLOCK)
            scores = []
            top = None
            for j in range(i + 1):
                s = block_scores(
                    i, j, blocks, qt, k_ref[block_of(j), :], diag_ref[...], side_ref[...], first
                )
                scores.append(s)
                here = jnp.max(s, axis=0, keepdims=True)
                top = here if top is None else jnp.maximum(top, here)
            total = jnp.zeros((1, BLOCK), jnp.float32)
            for j in range(i + 1):
                scores[j] = jnp.exp(scores[j] - top)
                total = total + jnp.sum(scores[j], axis=0, keepdims=True)
            inverse = 1.0 / total
            mixed = jnp.zeros((size, BLOCK), jnp.float32)
            for j in range(i + 1):
                probs = (scores[j] * inverse).astype(jnp.bfloat16)
                mixed = mixed + dot_nn(vt_ref[:, block_of(j)], probs)
            mixed = mixed.astype(jnp.bfloat16)
            sent_ref[2 * i] = mixed[:, :half]
            sent_ref[2 * i + 1] = mixed[:, half:]
            stat_ref[i : i + 1, :] = top + jnp.log(total)

    start_all([back])
    proj.finish()
    grads.wait()
    back.wait()
    for m in (arrive, back, grads):
        m.wait_sent()


def attention_forward(sizes, qkv, proj, g, table, bounds):
    n_ctx, n_exp = sizes["ctx"], sizes["exp"]
    heads, three, rows = qkv.shape
    size = three // 3
    buckets = table.shape[0]
    seq = n_ctx * rows
    low, full = jnp.bfloat16, jnp.float32
    assert 2 * rows == BLOCK
    return pl.pallas_call(
        functools.partial(forward_kernel, sizes, heads, buckets),
        out_shape=[
            jax.ShapeDtypeStruct((heads, size, rows), low),
            jax.ShapeDtypeStruct((n_exp,) + proj.shape, low),
            jax.ShapeDtypeStruct(g.shape, low),
            jax.ShapeDtypeStruct((n_ctx, three, rows), low),
            jax.ShapeDtypeStruct((seq // BLOCK, BLOCK), full),
        ],
        in_specs=any_space(3) + in_smem(2),
        out_specs=any_space(3) + in_vmem(2),
        scratch_shapes=[
            pltpu.VMEM((n_ctx, size, rows), low),
            pltpu.VMEM((seq, size), low),
            pltpu.VMEM((size, seq), low),
            pltpu.VMEM((BLOCK, BLOCK), full),
            pltpu.VMEM((BLOCK // 2, BLOCK // 2), full),
        ]
        + move_sems(n_ctx)
        + move_sems(n_ctx)
        + move_sems(n_exp)
        + move_sems(n_exp),
        compiler_params=remote_params(2),
        cost_estimate=cost(12_000_000_000, 50_000_000, 2_400_000),
        name="attention_forward",
    )(qkv, proj, g, table, bounds)


def backward_kernel(
    sizes,
    heads,
    buckets,
    do_in,
    out_in,
    terms_in,
    qkv_ref,
    stat_ref,
    table_ref,
    bounds_ref,
    grad_out,
    out_out,
    terms_out,
    grad_ref,
    bias_ref,
    do_ref,
    sent_ref,
    k_ref,
    v_ref,
    kt_ref,
    dq_ref,
    dk_ref,
    dv_ref,
    diag_ref,
    side_ref,
    diag_sum,
    side_sum,
    *sems,
):
    parts, three, rows = qkv_ref.shape
    size = three // 3
    blocks = parts * rows // BLOCK
    half = BLOCK // 2
    scale = 1.0 / math.sqrt(size)
    greet(sizes, ["ctx", "exp"])
    arrive = Move(sizes, "ctx", do_in, do_ref, sems[0:3], split=True, takers=heads)
    back = Move(sizes, "ctx", sent_ref, grad_out, sems[3:6], split=True, senders=heads)
    experts = Move(sizes, "exp", out_in, out_out, sems[6:9], split=True)
    terms = Move(sizes, "exp", terms_in, terms_out, sems[9:12], split=True)
    start_all([arrive])
    start_all([experts, terms])
    is_head = lax.axis_index("ctx") < heads

    @pl.when(is_head)
    def _():
        diag_ref[...] = near_bias(table_ref, buckets, 0, BLOCK, BLOCK)
        side_ref[...] = near_bias(table_ref, buckets, half, half, half)
        diag_sum[...] = jnp.zeros_like(diag_sum)
        side_sum[...] = jnp.zeros_like(side_sum)
        dk_ref[...] = jnp.zeros_like(dk_ref)
        dv_ref[...] = jnp.zeros_like(dv_ref)
        for c in range(parts):
            at = slice(c * rows, (c + 1) * rows)
            kt_ref[:, at] = qkv_ref[c, size : 2 * size, :]
            k_ref[at, :] = transposed(qkv_ref[c, size : 2 * size, :])
            v_ref[at, :] = transposed(qkv_ref[c, 2 * size :, :])

    arrive.wait()

    @pl.when(is_head)
    def _():
        far = jnp.zeros((1, BLOCK), jnp.float32)
        for i in range(blocks):
            qt = scaled_queries(qkv_ref, i, size)
            dot_ = jnp.concatenate([do_ref[2 * i], do_ref[2 * i + 1]], axis=1)
            first = first_keys(bounds_ref, i * BLOCK)
            stat = stat_ref[i : i + 1, :]
            probs, grads = [], []
            delta = jnp.zeros((1, BLOCK), jnp.float32)
            for j in range(i + 1):
                s = block_scores(
                    i, j, blocks, qt, k_ref[block_of(j), :], diag_ref[...], side_ref[...], first
                )
                p = jnp.exp(s - stat)
                dp = dot_nn(v_ref[block_of(j), :], dot_)
                delta = delta + jnp.sum(p * dp, axis=0, keepdims=True)
                probs.append(p)
                grads.append(dp)
            dqt = jnp.zeros((size, BLOCK), jnp.float32)
            for j in range(i + 1):
                ds = probs[j] * (grads[j] - delta)
                if j == i:
                    diag_sum[...] += ds
                elif j == i - 1:
                    side_sum[...] += ds
                else:
                    far = far + jnp.sum(ds, axis=0, keepdims=True)
                low = ds.astype(jnp.bfloat16)
                dk_ref[:, block_of(j)] += dot_nt(qt, low)
                dv_ref[:, block_of(j)] += dot_nt(dot_, probs[j].astype(jnp.bfloat16))
                dqt = dqt + dot_nn(kt_ref[:, block_of(j)], low)
            dq_ref[:, block_of(i)] = (dqt * scale).astype(jnp.bfloat16)
        for c in range(parts):
            at = slice(c * rows, (c + 1) * rows)
            sent_ref[c, :size, :] = dq_ref[:, at]
            sent_ref[c, size : 2 * size, :] = dk_ref[:, at].astype(jnp.bfloat16)
            sent_ref[c, 2 * size :, :] = dv_ref[:, at].astype(jnp.bfloat16)
        bias_ref[0:1, :] = far

    start_all([back])

    @pl.when(is_head)
    def _():
        grad_ref[:size, :] = dq_ref[...]
        grad_ref[size : 2 * size, :] = dk_ref[...].astype(jnp.bfloat16)
        grad_ref[2 * size :, :] = dv_ref[...].astype(jnp.bfloat16)
        far = bias_ref[0:1, :] + jnp.sum(side_sum[:half, :], axis=0, keepdims=True)
        far_half = jnp.sum(side_sum[half:, half:], axis=0, keepdims=True)
        far = far + jnp.concatenate([jnp.zeros_like(far_half), far_half], axis=1)
        diag_bucket = near_buckets(buckets, 0, BLOCK, BLOCK)
        side_bucket = near_buckets(buckets, half, half, half)
        for b in range(buckets):
            one = jnp.sum(jnp.where(diag_bucket == b, diag_sum[...], 0.0), axis=0, keepdims=True)
            two = jnp.sum(
                jnp.where(side_bucket == b, side_sum[half:, :half], 0.0), axis=0, keepdims=True
            )
            row = one + jnp.concatenate([two, jnp.zeros_like(two)], axis=1)
            if b == buckets - 1:
                row = row + far
            bias_ref[b : b + 1, :] = row

    experts.wait()
    terms.wait()
    back.wait()
    for m in (arrive, back, experts, terms):
        m.wait_sent()


def attention_backward(sizes, do, expert_out, terms, qkv, stat, table, bounds):
    n_ctx, n_exp = sizes["ctx"], sizes["exp"]
    heads, size, rows = do.shape
    buckets = table.shape[0]
    seq = n_ctx * rows
    low, full = jnp.bfloat16, jnp.float32
    return pl.pallas_call(
        functools.partial(backward_kernel, sizes, heads, buckets),
        out_shape=[
            jax.ShapeDtypeStruct((heads, 3 * size, rows), low),
            jax.ShapeDtypeStruct(expert_out.shape, low),
            jax.ShapeDtypeStruct(terms.shape, low),
            jax.ShapeDtypeStruct((3 * size, seq), low),
            jax.ShapeDtypeStruct((buckets, BLOCK), full),
        ],
        in_specs=any_space(3) + in_vmem(2) + in_smem(2),
        out_specs=any_space(3) + in_vmem(2),
        scratch_shapes=[
            pltpu.VMEM((n_ctx, size, rows), low),
            pltpu.VMEM((n_ctx, 3 * size, rows), low),
            pltpu.VMEM((seq, size), low),
            pltpu.VMEM((seq, size), low),
            pltpu.VMEM((size, seq), low),
            pltpu.VMEM((size, seq), low),
            pltpu.VMEM((size, seq), full),
            pltpu.VMEM((size, seq), full),
            pltpu.VMEM((BLOCK, BLOCK), full),
            pltpu.VMEM((BLOCK // 2, BLOCK // 2), full),
            pltpu.VMEM((BLOCK, BLOCK), full),
            pltpu.VMEM((BLOCK, BLOCK), full),
        ]
        + move_sems(n_ctx)
        + move_sems(n_ctx)
        + move_sems(n_exp)
        + move_sems(n_exp),
        compiler_params=remote_params(3),
        cost_estimate=cost(20_000_000_000, 60_000_000, 2_400_000),
        name="attention_backward",
    )(do, expert_out, terms, qkv, stat, table, bounds)


def expert_kernel(
    rows_ref, g_ref, gate_ref, up_ref, down_ref, out_ref, back_ref, dgate_ref, wg_ref,
    dy_ref, sum_out, sum_back,
):
    step = pl.program_id(0)
    count, width = rows_ref.shape
    sources = gate_ref.shape[0]
    cap = count // sources

    @pl.when(step == 0)
    def _():
        lanes = jnp.concatenate([gate_ref[s, 0:1, :] for s in range(sources)], axis=0)
        columns = lanes.T
        for s in range(sources):
            at = slice(s * cap, (s + 1) * cap)
            gate = columns[:cap, s : s + 1]
            dy_ref[at, :] = (gate * g_ref[at, :].astype(jnp.float32)).astype(jnp.bfloat16)
        sum_out[...] = jnp.zeros_like(sum_out)
        sum_back[...] = jnp.zeros_like(sum_back)

    rows, dy = rows_ref[...], dy_ref[...]
    up, down = up_ref[0], down_ref[0]
    x = dot_nt(rows, up)
    c, a = math.sqrt(2.0 / math.pi), 0.044715
    square = x * x
    t = jnp.tanh(c * x * (1.0 + a * square))
    half = 0.5 * (1.0 + t)
    hidden = (x * half).astype(jnp.bfloat16)
    slope = half + 0.5 * x * (1.0 - t * t) * (c * (1.0 + 3.0 * a * square))
    dpre = (dot_nt(dy, down) * slope).astype(jnp.bfloat16)
    wg_ref[:, :width] = dot_tn(dpre, rows).astype(jnp.bfloat16)
    wg_ref[:, width:] = dot_tn(hidden, dy).astype(jnp.bfloat16)
    sum_out[...] += dot_nn(hidden, down)
    sum_back[...] += dot_nn(dpre, up)

    @pl.when(step == pl.num_programs(0) - 1)
    def _():
        back_ref[...] = sum_back[...].astype(jnp.bfloat16)
        out = sum_out[...].astype(jnp.bfloat16)
        out_ref[...] = out
        dgate = jnp.sum(out.astype(jnp.float32) * g_ref[...].astype(jnp.float32), axis=1, keepdims=True)
        lane = lax.broadcasted_iota(jnp.int32, (cap, 128), 1)
        columns = jnp.zeros((cap, 128), jnp.float32)
        for s in range(sources):
            columns = jnp.where(lane == s, dgate[s * cap : (s + 1) * cap, :], columns)
        turned = jnp.concatenate([columns] * (128 // cap), axis=0).T
        for s in range(sources):
            dgate_ref[s] = jnp.broadcast_to(turned[s : s + 1, :], (8, 128))


def run_expert(rows, g, gates, weights):
    count, width = rows.shape
    hidden = weights.shape[1]
    tile = 256
    low, full = jnp.bfloat16, jnp.float32
    whole = lambda shape: pl.BlockSpec(shape, lambda f: (0,) * len(shape))
    return pl.pallas_call(
        expert_kernel,
        grid=(hidden // tile,),
        out_shape=[
            jax.ShapeDtypeStruct((count, width), low),
            jax.ShapeDtypeStruct((count, width), low),
            jax.ShapeDtypeStruct(gates.shape, full),
            jax.ShapeDtypeStruct((hidden, 2 * width), low),
        ],
        in_specs=[
            whole((count, width)),
            whole((count, width)),
            whole(gates.shape),
            pl.BlockSpec((1, tile, width), lambda f: (0, f, 0)),
            pl.BlockSpec((1, tile, width), lambda f: (1, f, 0)),
        ],
        out_specs=[
            whole((count, width)),
            whole((count, width)),
            whole(gates.shape),
            pl.BlockSpec((tile, 2 * width), lambda f: (f, 0)),
        ],
        scratch_shapes=[
            pltpu.VMEM((count, width), low),
            pltpu.VMEM((count, width), full),
            pltpu.VMEM((count, width), full),
        ],
        compiler_params=pltpu.CompilerParams(vmem_limit_bytes=VMEM_BYTES),
        cost_estimate=cost(14_500_000_000, 24_000_000, 1_600_000),
        name="run_expert",
    )(rows, g, gates, weights, weights)


def total_kernel(
    sizes, heads, takers, head_in, small_in, out_in, qkv_out, weight_out, small_out, table_out,
    head_parts, small_parts, out_parts, head_sent, small_sent, out_sent,
    head_all, small_all, out_all, *sems,
):
    share, three = head_in.shape[1:]
    size = three // 3
    half = share // 2
    width = heads * size
    sixteen = out_sent.shape[0]
    me = lax.axis_index("ctx")
    greet(sizes, ["ctx", "exp"])
    first = [
        Move(sizes, "exp", head_in, head_parts, sems[0:3], split=True),
        Move(sizes, "exp", small_in, small_parts, sems[3:6], split=True),
        Move(sizes, "ctx", out_in, out_parts, sems[6:9], split=True, takers=takers),
    ]
    second = [
        Move(sizes, "ctx", head_sent, head_all, sems[9:12], senders=heads),
        Move(sizes, "ctx", small_sent, small_all, sems[12:15]),
        Move(sizes, "ctx", out_sent, out_all, sems[15:18], senders=takers),
    ]
    start_all(first)
    first[0].wait()
    total = head_parts[0].astype(jnp.float32)
    for s in range(1, sizes["exp"]):
        total = total + head_parts[s].astype(jnp.float32)
    total = total.astype(jnp.bfloat16)
    head_sent[:share, :] = total[:, : 2 * size]
    head_sent[share:, :] = jnp.concatenate(
        [total[:half, 2 * size :], total[half:, 2 * size :]], axis=1
    )
    start_all(second[:1])
    first[1].wait()
    little = small_parts[0]
    for s in range(1, sizes["exp"]):
        little = little + small_parts[s]
    small_sent[...] = little
    start_all(second[1:2])
    first[2].wait()

    @pl.when(me < takers)
    def _():
        weight = out_parts[0].astype(jnp.float32)
        for s in range(1, sizes["ctx"]):
            weight = weight + out_parts[s].astype(jnp.float32)
        out_sent[...] = weight.astype(jnp.bfloat16)

    start_all(second[2:])
    second[0].wait()
    for h in range(heads):
        got = head_all[h].astype(jnp.float32)
        at = h * size
        qkv_out[:, at : at + size] = got[:share, :size]
        qkv_out[:, width + at : width + at + size] = got[:share, size:]
        qkv_out[:half, 2 * width + at : 2 * width + at + size] = got[share:, :size]
        qkv_out[half:, 2 * width + at : 2 * width + at + size] = got[share:, size:]
    second[1].wait()
    sums = small_all[0]
    for s in range(1, sizes["ctx"]):
        sums = sums + small_all[s]
    small_out[...] = sums
    for h in range(heads):
        table_out[h : h + 1, :] = small_all[h, 0:1, :]
    second[2].wait()
    for s in range(takers):
        weight_out[s * sixteen : (s + 1) * sixteen, :] = out_all[s].astype(jnp.float32)
    for m in first + second:
        m.wait_sent()


def total_dense(sizes, heads, head_terms, small, out_terms):
    n_ctx, n_exp = sizes["ctx"], sizes["exp"]
    _, share, three = head_terms.shape
    takers, sixteen, width = out_terms.shape
    low, full = jnp.bfloat16, jnp.float32
    return pl.pallas_call(
        functools.partial(total_kernel, sizes, heads, takers),
        out_shape=[
            jax.ShapeDtypeStruct((share, 3 * width), full),
            jax.ShapeDtypeStruct((share, width), full),
            jax.ShapeDtypeStruct(small.shape[1:], full),
            jax.ShapeDtypeStruct((heads, 128), full),
        ],
        in_specs=in_vmem(3),
        out_specs=in_vmem(4),
        scratch_shapes=[
            pltpu.VMEM(head_terms.shape, low),
            pltpu.VMEM(small.shape, full),
            pltpu.VMEM((n_ctx, sixteen, width), low),
            pltpu.VMEM((share * 3 // 2, 128), low),
            pltpu.VMEM(small.shape[1:], full),
            pltpu.VMEM((sixteen, width), low),
            pltpu.VMEM((heads, share * 3 // 2, 128), low),
            pltpu.VMEM((n_ctx,) + small.shape[1:], full),
            pltpu.VMEM((takers, sixteen, width), low),
        ]
        + move_sems(n_exp)
        + move_sems(n_exp)
        + move_sems(n_ctx)
        + move_sems(n_ctx)
        + move_sems(n_ctx)
        + move_sems(n_ctx),
        compiler_params=remote_params(4),
        cost_estimate=cost(0, 60_000_000),
        name="total_dense",
    )(head_terms, small, out_terms)


def split_kernel(both_ref, up_ref, down_ref):
    width = up_ref.shape[1]
    up_ref[...] = both_ref[:, :width].astype(jnp.float32)
    down_ref[...] = both_ref[:, width:].astype(jnp.float32)


def split_weights(both):
    rows, width = both.shape[0], both.shape[1] // 2
    return pl.pallas_call(
        split_kernel,
        out_shape=[jax.ShapeDtypeStruct((rows, width), jnp.float32)] * 2,
        in_specs=in_vmem(1),
        out_specs=in_vmem(2),
        compiler_params=pltpu.CompilerParams(vmem_limit_bytes=8 * 1024 * 1024),
        cost_estimate=cost(0, 2_000_000),
        name="split_weights",
    )(both)


def rms_scale(values, gain_row):
    return (
        values * lax.rsqrt(jnp.mean(values * values, axis=-1, keepdims=True) + epsilon) * gain_row
    )


def local(
    sizes,
    block_in,
    attn_gain,
    moe_gain,
    query_key_value_weight,
    output_matrix,
    routing_weight,
    bias_table,
    up_weight,
    down_weight,
    routes,
    doc_lengths,
    cotangent,
):
    low, full = jnp.bfloat16, jnp.float32
    n_ctx, n_exp = sizes["ctx"], sizes["exp"]
    rows, width = block_in.shape[1:]
    seq_len = rows * n_ctx
    share = width // n_exp
    own_buckets, heads = bias_table.shape
    buckets = own_buckets * n_exp
    size = width // heads
    experts = routing_weight.shape[1]
    x_in = block_in[0].astype(full)
    g_low = cotangent[0]
    grad_out = g_low.astype(full)

    expert_weights = lax.all_gather(
        jnp.concatenate([up_weight, down_weight], axis=0), "ctx", axis=1, tiled=True
    )

    lanes = lambda a: jnp.pad(a, ((0, 0), (0, 128 - a.shape[1])))
    small = jnp.concatenate(
        [lanes(attn_gain[None]), lanes(moe_gain[None]), lanes(bias_table), lanes(routing_weight.T)],
        axis=0,
    )
    small = jnp.pad(small, ((0, -small.shape[0] % 16), (0, 0)))
    qkv_full, dense = gather_dense(sizes, query_key_value_weight, small)
    qkv_full = qkv_full.reshape(width, 3 * width)
    gain_one = dense[:, 0, :share].reshape(width).astype(full)
    gain_two = dense[:, 1, :share].reshape(width).astype(full)
    table_full = dense[:, 2 : 2 + own_buckets, :heads].reshape(buckets, heads).astype(full)
    router_t = dense[:, 2 + own_buckets : 2 + own_buckets + experts, :share]
    router_t = jnp.transpose(router_t, (1, 0, 2)).reshape(experts, width)
    head = jnp.minimum(lax.axis_index("ctx"), heads - 1)
    table_head = lax.dynamic_slice_in_dim(table_full, head, 1, 1)[:, 0]
    bounds = jnp.cumsum(doc_lengths[0]).astype(jnp.int32)

    route = routes[0]
    choose = (route[:, :, None] == jnp.arange(experts, dtype=jnp.int32)).astype(full)
    capacity = min(rows, 4 * rows // experts)
    flat_routes = route.reshape(2 * rows)
    marks = (flat_routes[:, None] == jnp.arange(experts, dtype=jnp.int32)).astype(full)
    before = jnp.asarray(np.tril(np.ones((2 * rows, 2 * rows), np.float32), -1), low)
    rank = jnp.sum(marks * jnp.dot(before, marks.astype(low), preferred_element_type=full), axis=-1)
    slot = (flat_routes * capacity + rank.astype(jnp.int32)).reshape(rows, 2)
    slots = jnp.arange(experts * capacity, dtype=jnp.int32)
    hit = [slots[:, None] == slot[:, c][None, :] for c in range(2)]
    either = (hit[0] | hit[1]).astype(low)
    found = [(slot[:, c][:, None] == slots[None, :]) for c in range(2)]
    piece = (experts, capacity, width)
    send_g = jnp.dot(either, g_low, preferred_element_type=full).astype(low)

    h_first = lax.optimization_barrier(rms_scale(x_in, gain_one).astype(low))
    h_all = lax.all_gather(h_first, "ctx", axis=0, tiled=True)
    qkv_t = lax.dot_general(
        qkv_full, h_first, (((0,), (1,)), ((), ())), preferred_element_type=full
    ).astype(low)
    qkv_t = jnp.transpose(qkv_t.reshape(3, heads, size, rows), (1, 0, 2, 3)).reshape(
        heads, 3 * size, rows
    )
    mixed, proj_full, g_rows, qkv_head, stat = attention_forward(
        sizes, qkv_t, output_matrix, send_g.reshape(piece), table_head, bounds
    )
    attended_t = mixed.reshape(width, rows)
    proj_full = proj_full.reshape(width, width)

    x_mid = x_in + dot_tn(attended_t, proj_full)
    h_second = rms_scale(x_mid, gain_two).astype(low)
    routing_logits = dot_nt(h_second, router_t)
    gates = jax.nn.softmax(jnp.sum(choose * routing_logits[:, None, :], axis=-1), axis=-1)
    send_rows = jnp.dot(either, h_second, preferred_element_type=full).astype(low)
    gate_slots = sum(
        jnp.sum(jnp.where(hit[c], gates[:, c][None, :], 0.0), axis=1) for c in range(2)
    )
    gate_slots = jnp.broadcast_to(
        lanes(gate_slots.reshape(experts, capacity))[:, None, :], (experts, 8, 128)
    )
    expert_rows, gate_rows = swap_experts(sizes, 5, send_rows.reshape(piece), gate_slots)
    expert_out, expert_back, dgate, weight_terms = run_expert(
        expert_rows.reshape(experts * capacity, width),
        g_rows.reshape(experts * capacity, width),
        gate_rows,
        expert_weights,
    )
    h_all, weight_terms = lax.optimization_barrier((h_all, weight_terms))
    weight_grads = lax.psum_scatter(weight_terms, "ctx", scatter_dimension=0, tiled=True)
    grad_back, dgate = swap_experts(sizes, 6, expert_back.reshape(piece), dgate)

    grad_back = grad_back.reshape(experts * capacity, width)
    dgate = dgate[:, 0, :capacity].reshape(1, experts * capacity)
    grad_gates = jnp.stack(
        [jnp.sum(jnp.where(found[c], dgate, 0.0), axis=1) for c in range(2)], axis=-1
    )
    grad_chosen = gates * (grad_gates - jnp.sum(gates * grad_gates, axis=-1, keepdims=True))
    grad_logits = jnp.sum(choose * grad_chosen[:, :, None], axis=1).astype(low)
    grad_h_second = jnp.dot(
        (found[0] | found[1]).astype(low), grad_back, preferred_element_type=full
    ) + jnp.dot(grad_logits, router_t, preferred_element_type=full)
    grad_x_norm, grad_gain_two = jax.vjp(rms_scale, x_mid, gain_two)[1](grad_h_second)
    grad_x_mid = grad_out + grad_x_norm
    grad_proj = grad_x_mid.astype(low)
    grad_attended = dot_nt(proj_full, grad_proj).astype(low).reshape(heads, size, rows)
    out_terms = jnp.dot(attended_t, grad_proj, preferred_element_type=full).astype(low)

    grad_qkv_t, returned, out_parts, grad_head, bias_rows = attention_backward(
        sizes,
        grad_attended,
        expert_out.reshape(piece),
        out_terms.reshape(n_exp, share, width),
        qkv_head,
        stat,
        table_head,
        bounds,
    )
    grad_qkv_t = jnp.transpose(
        grad_qkv_t.reshape(heads, 3, size, rows), (1, 0, 2, 3)
    ).reshape(3 * width, rows)
    grad_h_first = lax.dot_general(
        grad_qkv_t, qkv_full, (((0,), (1,)), ((), ())), preferred_element_type=full
    )
    grad_x_first, grad_gain_one = jax.vjp(rms_scale, x_in, gain_one)[1](grad_h_first)
    grad_in = (grad_x_mid + grad_x_first)[None]
    grad_router = dot_tn(grad_logits, h_second).reshape(experts, n_exp, share)
    head_terms = (
        lax.dot_general(h_all, grad_head, (((0,), (1,)), ((), ())), preferred_element_type=full)
        .astype(low)
        .reshape(n_exp, share, 3 * size)
    )
    bias_part = jnp.sum(bias_rows, axis=1).reshape(n_exp, own_buckets)
    first_row = jnp.concatenate([grad_gain_one.reshape(n_exp, share), bias_part], axis=1)
    totals = jnp.concatenate(
        [
            lanes(first_row)[:, None, :],
            lanes(grad_gain_two.reshape(n_exp, share))[:, None, :],
            jnp.pad(jnp.transpose(grad_router, (1, 0, 2)), ((0, 0), (0, 0), (0, 128 - share))),
        ],
        axis=1,
    )
    totals = jnp.pad(totals, ((0, 0), (0, -totals.shape[1] % 8), (0, 0)))
    out_sum = jnp.sum(out_parts.astype(full), axis=0).astype(low).reshape(share // 16, 16, width)
    grad_qkv, grad_out_weight, sums, table_rows = total_dense(
        sizes, heads, head_terms, totals, out_sum
    )
    returned = returned.reshape(experts * capacity, width)
    picked = jnp.dot(
        jnp.concatenate(found, axis=0).astype(low), returned, preferred_element_type=full
    )
    block_out = x_mid + (gates[:, :1] * picked[:rows] + gates[:, 1:] * picked[rows:])
    grad_up, grad_down = split_weights(weight_grads)
    return (
        block_out.astype(low)[None],
        grad_in,
        sums[0, :share],
        sums[1, :share],
        grad_qkv,
        grad_out_weight,
        sums[2 : 2 + experts, :share].T,
        table_rows[:, share : share + own_buckets].T,
        grad_up[None],
        grad_down[None],
    )


def solution(mesh):
    sizes = {name: mesh.shape[name] for name in ("ctx", "exp")}
    tokens = P("exp", "ctx", None)
    row_split = P("exp", None)
    return jax.shard_map(
        functools.partial(local, sizes),
        mesh=mesh,
        in_specs=(
            tokens,
            P("exp"),
            P("exp"),
            row_split,
            row_split,
            row_split,
            row_split,
            tokens,
            tokens,
            tokens,
            row_split,
            tokens,
        ),
        out_specs=(
            tokens,
            tokens,
            P("exp"),
            P("exp"),
            row_split,
            row_split,
            row_split,
            row_split,
            tokens,
            tokens,
        ),
        check_vma=False,
    )
```

```python
import functools
import math

import jax
import jax.numpy as jnp
import numpy as np
from jax import lax
from jax.experimental import pallas as pl
from jax.experimental.pallas import tpu as pltpu
from jax.sharding import PartitionSpec as P

MAXD = 128
BLOCK = 256
MESH = pl.DeviceIdType.MESH
VMEM_BYTES = 40 * 1024 * 1024

epsilon = 1e-06
masked_score = -1e30


def bucket_thresholds(buckets, reach_len):
    exact_part = buckets // 2
    spread_part = buckets - exact_part
    return [
        int(math.ceil(exact_part * (reach_len / exact_part) ** (level / spread_part)))
        for level in range(1, spread_part)
    ]


def guarded(tests, action):
    tests = [t for t in tests if t is not None]
    if not tests:
        action()
    else:
        pl.when(functools.reduce(jnp.logical_and, tests))(action)


def greet(sizes, axes):
    barrier = pltpu.get_barrier_semaphore()
    total = 0
    for a in axes:
        me = lax.axis_index(a)
        for r in range(1, sizes[a]):
            peer = lax.rem(me + r, sizes[a])
            pl.semaphore_signal(barrier, inc=1, device_id={a: peer}, device_id_type=MESH)
            total += 1
    pl.semaphore_wait(barrier, total)


class Move:
    def __init__(self, sizes, axis, src, out, sems, split=False, senders=None, takers=None):
        self.n = sizes[axis]
        self.axis, self.src, self.out, self.split = axis, src, out, split
        self.send_sem, self.recv_sem, self.own_sem = sems
        self.senders, self.takers = senders or self.n, takers or self.n
        self.me = lax.axis_index(axis)

    def sends(self, device):
        return device < self.senders if self.senders < self.n else None

    def takes(self, device):
        return device < self.takers if self.takers < self.n else None

    def copy(self, r, peer, slot, piece):
        return pltpu.make_async_remote_copy(
            src_ref=self.src.at[piece] if self.split else self.src,
            dst_ref=self.out.at[slot],
            send_sem=self.send_sem.at[r],
            recv_sem=self.recv_sem.at[r],
            device_id={self.axis: peer},
            device_id_type=MESH,
        )

    def to(self, r):
        return lax.rem(self.me + r, self.n)

    def start(self, r):
        dst = self.to(r)
        guarded(
            [self.sends(self.me), self.takes(dst)],
            lambda: self.copy(r, dst, self.me, dst).start(),
        )

    def own(self):
        src = self.src.at[self.me] if self.split else self.src
        return pltpu.make_async_copy(src, self.out.at[self.me], self.own_sem)

    def start_own(self):
        guarded([self.sends(self.me), self.takes(self.me)], lambda: self.own().start())

    def wait(self):
        guarded([self.sends(self.me), self.takes(self.me)], lambda: self.own().wait())
        for r in range(1, self.n):
            src = lax.rem(self.me + self.n - r, self.n)
            guarded(
                [self.sends(src), self.takes(self.me)],
                lambda: self.copy(r, src, src, 0).wait_recv(),
            )

    def wait_sent(self):
        for r in range(1, self.n):
            dst = self.to(r)
            guarded(
                [self.sends(self.me), self.takes(dst)],
                lambda: self.copy(r, dst, self.me, dst).wait_send(),
            )


def start_all(moves):
    for r in range(1, max(m.n for m in moves)):
        for m in moves:
            if r < m.n:
                m.start(r)
    for m in moves:
        m.start_own()


class PairGather:
    def __init__(self, sizes, src, out, sems):
        self.n = sizes["exp"]
        self.src, self.out = src, out
        self.send_sem, self.recv_sem, self.own_sem = sems
        self.me = lax.axis_index("exp")
        core = lax.rem(self.me, 2)
        self.mate = self.me + 1 - 2 * core

    def copy(self, src, slot, k, peer):
        return pltpu.make_async_remote_copy(
            src_ref=src,
            dst_ref=self.out.at[slot],
            send_sem=self.send_sem.at[k],
            recv_sem=self.recv_sem.at[k],
            device_id={"exp": peer},
            device_id_type=MESH,
        )

    def own(self):
        return pltpu.make_async_copy(self.src, self.out.at[self.me], self.own_sem)

    def chips(self):
        return range(1, self.n // 2)

    def start(self):
        for r in self.chips():
            self.copy(self.src, self.me, r, lax.rem(self.me + 2 * r, self.n)).start()
        self.copy(self.src, self.me, 0, self.mate).start()
        self.own().start()

    def forward(self, r):
        slot = lax.rem(self.me + self.n - 2 * r, self.n)
        return self.copy(self.out.at[slot], slot, self.n // 2 + r, self.mate)

    def pass_on(self):
        for r in self.chips():
            slot = lax.rem(self.me + self.n - 2 * r, self.n)
            self.copy(self.src, slot, r, slot).wait_recv()
            self.forward(r).start()

    def finish(self):
        for r in self.chips():
            slot = lax.rem(self.mate + self.n - 2 * r, self.n)
            self.copy(self.src, slot, self.n // 2 + r, self.mate).wait_recv()
            self.forward(r).wait_send()
            self.copy(self.src, self.me, r, lax.rem(self.me + 2 * r, self.n)).wait_send()
        self.copy(self.src, self.mate, 0, self.mate).wait_recv()
        self.copy(self.src, self.me, 0, self.mate).wait_send()
        self.own().wait()


def move_sems(count):
    return [
        pltpu.SemaphoreType.DMA((count,)),
        pltpu.SemaphoreType.DMA((count,)),
        pltpu.SemaphoreType.DMA,
    ]


def any_space(count):
    return [pl.BlockSpec(memory_space=pl.ANY)] * count


def in_vmem(count):
    return [pl.BlockSpec(memory_space=pltpu.VMEM)] * count


def in_smem(count):
    return [pl.BlockSpec(memory_space=pltpu.SMEM)] * count


def remote_params(number, limit=VMEM_BYTES):
    return pltpu.CompilerParams(
        collective_id=number, has_side_effects=True, vmem_limit_bytes=limit
    )


def cost(flops, moved, special=0):
    return pl.CostEstimate(flops=flops, bytes_accessed=moved, transcendentals=special)


def swap_experts(sizes, number, rows, values):
    n = sizes["exp"]

    def kernel(a_ref, b_ref, a_out, b_out, *sems):
        greet(sizes, ["exp"])
        one = Move(sizes, "exp", a_ref, a_out, sems[:3], split=True)
        two = Move(sizes, "exp", b_ref, b_out, sems[3:], split=True)
        start_all([two, one])
        for m in (two, one):
            m.wait()
        for m in (two, one):
            m.wait_sent()

    return pl.pallas_call(
        kernel,
        out_shape=[jax.ShapeDtypeStruct(a.shape, a.dtype) for a in (rows, values)],
        in_specs=any_space(2),
        out_specs=any_space(2),
        scratch_shapes=move_sems(n) + move_sems(n),
        compiler_params=remote_params(number, 4 * 1024 * 1024),
        cost_estimate=cost(0, 30_000_000),
        name=f"swap_experts_{number}",
    )(rows, values)


def dot_nt(left, right):
    return lax.dot_general(
        left, right, (((1,), (1,)), ((), ())), preferred_element_type=jnp.float32
    )


def dot_tn(left, right):
    return lax.dot_general(
        left, right, (((0,), (0,)), ((), ())), preferred_element_type=jnp.float32
    )


def dot_nn(left, right):
    return jnp.dot(left, right, preferred_element_type=jnp.float32)


def near_buckets(buckets, offset, rows, cols):
    key = lax.broadcasted_iota(jnp.int32, (rows, cols), 0)
    query = lax.broadcasted_iota(jnp.int32, (rows, cols), 1)
    distance = jnp.clip(query - key + offset, 0, MAXD)
    bucket = jnp.minimum(distance, buckets // 2)
    for level in bucket_thresholds(buckets, MAXD):
        bucket = bucket + (distance >= level).astype(jnp.int32)
    return bucket


def near_bias(table_ref, buckets, offset, rows, cols):
    bucket = near_buckets(buckets, offset, rows, cols)
    last = table_ref[buckets - 1 : buckets, 0:1]
    bias = jnp.zeros((rows, cols), jnp.float32)
    for b in range(buckets - 1):
        bias = jnp.where(bucket == b, table_ref[b : b + 1, 0:1] - last, bias)
    return bias


def first_keys(bounds_ref, start):
    query = start + lax.broadcasted_iota(jnp.int32, (1, BLOCK), 1)
    first = jnp.zeros((1, BLOCK), jnp.int32)
    for d in range(3):
        first = jnp.where(query >= bounds_ref[d], bounds_ref[d], first)
    return first


def block_scores(i, j, blocks, qt, k, diag_bias, side_bias, first):
    s = dot_nn(k, qt)
    half = BLOCK // 2
    if j == i:
        s = s + diag_bias
    elif j == i - 1:
        lower = jnp.concatenate([s[half:, :half] + side_bias, s[half:, half:]], axis=1)
        s = jnp.concatenate([s[:half], lower], axis=0)
    if j == i or j == 0 or i == blocks - 1:
        key = lax.broadcasted_iota(jnp.int32, (BLOCK, BLOCK), 0)
        keep = key + j * BLOCK >= first
        if j == i:
            keep = keep & (key <= lax.broadcasted_iota(jnp.int32, (BLOCK, BLOCK), 1))
        s = jnp.where(keep, s, masked_score)
    return s


def transposed(piece):
    return piece.astype(jnp.float32).T.astype(jnp.bfloat16)


def scaled_queries(qkv_ref, i, size):
    scale = 1.0 / math.sqrt(size)
    both = jnp.concatenate([qkv_ref[2 * i, :size, :], qkv_ref[2 * i + 1, :size, :]], axis=1)
    return (both * scale).astype(jnp.bfloat16)


def block_of(j):
    return slice(j * BLOCK, (j + 1) * BLOCK)


def bucket_values(small_ref, own_buckets, heads):
    head = jnp.minimum(lax.axis_index("ctx"), heads - 1)
    rows = jnp.concatenate(
        [small_ref[e, 2 : 2 + own_buckets, :] for e in range(small_ref.shape[0])], axis=0
    ).astype(jnp.float32)
    lane = lax.broadcasted_iota(jnp.int32, rows.shape, 1)
    value = jnp.sum(jnp.where(lane == head, rows, 0.0), axis=1, keepdims=True)
    return jnp.broadcast_to(value, rows.shape)


def full_row(small_ref, row, share):
    pieces = [small_ref[e, row : row + 1, :share] for e in range(small_ref.shape[0])]
    return jnp.concatenate(pieces, axis=1).astype(jnp.float32)


def norm_rows(x, gain):
    scale = lax.rsqrt(jnp.mean(x * x, axis=-1, keepdims=True) + epsilon)
    return (x * scale * gain).astype(jnp.bfloat16)


def columns_to_rows(column, groups):
    cap = column.shape[0] // groups
    lane = lax.broadcasted_iota(jnp.int32, (cap, 128), 1)
    spread = jnp.zeros((cap, 128), jnp.float32)
    for s in range(groups):
        spread = jnp.where(lane == s, column[s * cap : (s + 1) * cap, :], spread)
    return jnp.concatenate([spread] * (128 // cap), axis=0).T


def front_kernel(
    sizes,
    heads,
    experts,
    own_buckets,
    w_in,
    small_in,
    proj_in,
    x_ref,
    g_ref,
    route_ref,
    bounds_ref,
    w_ref,
    small_ref,
    proj_ref,
    h_ref,
    mid_ref,
    second_ref,
    info_ref,
    mixed_ref,
    qkv_ref,
    stat_ref,
    table_ref,
    rows_out,
    g_out,
    gate_out,
    qkv_sent,
    sent_ref,
    k_ref,
    vt_ref,
    diag_ref,
    side_ref,
    rows_sent,
    g_sent,
    gate_sent,
    *sems,
):
    n_exp = sizes["exp"]
    parts, three, rows = qkv_ref.shape
    size = three // 3
    width = heads * size
    share = width // n_exp
    blocks = parts * rows // BLOCK
    half = BLOCK // 2
    buckets = own_buckets * n_exp
    cap = rows_sent.shape[1]
    greet(sizes, ["exp", "ctx"])
    weight = PairGather(sizes, w_in, w_ref, sems[0:3])
    little = Move(sizes, "exp", small_in, small_ref, sems[3:6])
    proj = PairGather(sizes, proj_in, proj_ref, sems[6:9])
    grads = Move(sizes, "exp", g_sent, g_out, sems[9:12], split=True)
    arrive = Move(sizes, "ctx", qkv_sent, qkv_ref, sems[12:15], split=True, takers=heads)
    back = Move(sizes, "ctx", sent_ref, mixed_ref, sems[15:18], split=True, senders=heads)
    hidden = Move(sizes, "exp", rows_sent, rows_out, sems[18:21], split=True)
    gating = Move(sizes, "exp", gate_sent, gate_out, sems[21:24], split=True)
    start_all([little])
    weight.start()

    expert = lax.broadcasted_iota(jnp.int32, (experts, rows), 0)
    chosen = [(expert == route_ref[c : c + 1, :]).astype(jnp.float32) for c in range(2)]
    earlier = lax.broadcasted_iota(jnp.int32, (rows, rows), 0) < lax.broadcasted_iota(
        jnp.int32, (rows, rows), 1
    )
    count = dot_nn((chosen[0] + chosen[1]).astype(jnp.bfloat16), earlier.astype(jnp.bfloat16))
    place = count + (expert * cap).astype(jnp.float32)
    slot = [jnp.sum(chosen[c] * place, axis=0, keepdims=True) for c in range(2)]
    slots = lax.broadcasted_iota(jnp.int32, (experts * cap, rows), 0).astype(jnp.float32)
    hit = [slots == slot[c] for c in range(2)]
    either = (hit[0] | hit[1]).astype(jnp.bfloat16)
    send_g = dot_nn(either, g_ref[...]).astype(jnp.bfloat16)
    for e in range(experts):
        g_sent[e] = send_g[e * cap : (e + 1) * cap, :]

    little.wait()
    table_ref[...] = bucket_values(small_ref, own_buckets, heads)
    x = x_ref[...].astype(jnp.float32)
    h = norm_rows(x, full_row(small_ref, 0, share))
    h_ref[...] = h
    diag_ref[...] = near_bias(table_ref, buckets, 0, BLOCK, BLOCK)
    side_ref[...] = near_bias(table_ref, buckets, half, half, half)
    weight.pass_on()
    proj.start()
    weight.finish()
    for at in range(0, 3 * width, 2 * rows):
        piece = w_ref[:, :, at : at + 2 * rows].reshape(width, 2 * rows)
        turned = dot_nn(h, piece).T.astype(jnp.bfloat16)
        for begin in range(0, 2 * rows, size):
            part, head = divmod((at + begin) // size, heads)
            qkv_sent[head, part * size : (part + 1) * size, :] = turned[begin : begin + size, :]
    start_all([arrive])
    proj.pass_on()
    start_all([grads])
    arrive.wait()

    @pl.when(lax.axis_index("ctx") < heads)
    def _():
        for c in range(parts):
            at = slice(c * rows, (c + 1) * rows)
            k_ref[at, :] = transposed(qkv_ref[c, size : 2 * size, :])
            vt_ref[:, at] = qkv_ref[c, 2 * size :, :]
        for i in range(blocks):
            qt = scaled_queries(qkv_ref, i, size)
            first = first_keys(bounds_ref, i * BLOCK)
            scores = []
            top = None
            for j in range(i + 1):
                s = block_scores(
                    i, j, blocks, qt, k_ref[block_of(j), :], diag_ref[...], side_ref[...], first
                )
                scores.append(s)
                here = jnp.max(s, axis=0, keepdims=True)
                top = here if top is None else jnp.maximum(top, here)
            total = jnp.zeros((1, BLOCK), jnp.float32)
            for j in range(i + 1):
                scores[j] = jnp.exp(scores[j] - top)
                total = total + jnp.sum(scores[j], axis=0, keepdims=True)
            inverse = 1.0 / total
            mixed = jnp.zeros((size, BLOCK), jnp.float32)
            for j in range(i + 1):
                probs = (scores[j] * inverse).astype(jnp.bfloat16)
                mixed = mixed + dot_nn(vt_ref[:, block_of(j)], probs)
            mixed = mixed.astype(jnp.bfloat16)
            sent_ref[2 * i] = mixed[:, :half]
            sent_ref[2 * i + 1] = mixed[:, half:]
            stat_ref[i : i + 1, :] = top + jnp.log(total)

    start_all([back])
    proj.finish()
    back.wait()

    attended = transposed(mixed_ref[...].reshape(width, rows))
    mid = x + dot_nn(attended, proj_ref[...].reshape(width, width))
    mid_ref[...] = mid
    second = norm_rows(mid, full_row(small_ref, 1, share))
    second_ref[...] = second
    send = dot_nn(either, second).astype(jnp.bfloat16)
    for e in range(experts):
        rows_sent[e] = send[e * cap : (e + 1) * cap, :]
    start_all([hidden])
    begin = 2 + own_buckets
    router = jnp.concatenate(
        [small_ref[e, begin : begin + experts, :share] for e in range(n_exp)], axis=1
    )
    z = dot_nt(router, second)
    picked = [jnp.sum(chosen[c] * z, axis=0, keepdims=True) for c in range(2)]
    top = jnp.maximum(picked[0], picked[1])
    raised = [jnp.exp(p - top) for p in picked]
    gates = [r / (raised[0] + raised[1]) for r in raised]
    column = sum(
        jnp.sum(jnp.where(hit[c], gates[c], 0.0), axis=1, keepdims=True) for c in range(2)
    )
    turned = columns_to_rows(column, experts)
    for e in range(experts):
        gate_sent[e] = jnp.broadcast_to(turned[e : e + 1, :], (8, 128))
    start_all([gating])
    info_ref[...] = jnp.concatenate(
        gates + slot + [route_ref[c : c + 1, :].astype(jnp.float32) for c in range(2)] + slot,
        axis=0,
    )
    grads.wait()
    gating.wait()
    hidden.wait()
    for m in (little, grads, arrive, back, hidden, gating):
        m.wait_sent()


def run_front(sizes, heads, experts, own_buckets, weight, small, proj, x, g, route_t, bounds):
    n_ctx, n_exp = sizes["ctx"], sizes["exp"]
    rows, width = x.shape
    size = width // heads
    seq = n_ctx * rows
    cap = min(rows, 4 * rows // experts)
    low, full = jnp.bfloat16, jnp.float32
    assert 2 * rows == BLOCK and rows == 128 and 3 * width % (2 * rows) == 0
    return pl.pallas_call(
        functools.partial(front_kernel, sizes, heads, experts, own_buckets),
        out_shape=[
            jax.ShapeDtypeStruct((n_exp,) + weight.shape, low),
            jax.ShapeDtypeStruct((n_exp,) + small.shape, low),
            jax.ShapeDtypeStruct((n_exp,) + proj.shape, low),
            jax.ShapeDtypeStruct((rows, width), low),
            jax.ShapeDtypeStruct((rows, width), full),
            jax.ShapeDtypeStruct((rows, width), low),
            jax.ShapeDtypeStruct((8, rows), full),
            jax.ShapeDtypeStruct((heads, size, rows), low),
            jax.ShapeDtypeStruct((n_ctx, 3 * size, rows), low),
            jax.ShapeDtypeStruct((seq // BLOCK, BLOCK), full),
            jax.ShapeDtypeStruct((own_buckets * n_exp, 128), full),
            jax.ShapeDtypeStruct((experts, cap, width), low),
            jax.ShapeDtypeStruct((experts, cap, width), low),
            jax.ShapeDtypeStruct((experts, 8, 128), full),
        ],
        in_specs=in_vmem(6) + in_smem(1),
        out_specs=in_vmem(14),
        scratch_shapes=[
            pltpu.VMEM((heads, 3 * size, rows), low),
            pltpu.VMEM((n_ctx, size, rows), low),
            pltpu.VMEM((seq, size), low),
            pltpu.VMEM((size, seq), low),
            pltpu.VMEM((BLOCK, BLOCK), full),
            pltpu.VMEM((BLOCK // 2, BLOCK // 2), full),
            pltpu.VMEM((experts, cap, width), low),
            pltpu.VMEM((experts, cap, width), low),
            pltpu.VMEM((experts, 8, 128), full),
        ]
        + move_sems(n_exp) * 4
        + move_sems(n_ctx) * 2
        + move_sems(n_exp) * 2,
        compiler_params=remote_params(1),
        cost_estimate=cost(60_000_000_000, 100_000_000, 2_400_000),
        name="run_front",
    )(weight, small, proj, x, g, route_t, bounds)


def backward_kernel(
    sizes,
    heads,
    buckets,
    do_in,
    out_in,
    terms_in,
    qkv_ref,
    stat_ref,
    table_ref,
    bounds_ref,
    grad_out,
    out_out,
    terms_out,
    grad_ref,
    bias_ref,
    do_ref,
    sent_ref,
    k_ref,
    v_ref,
    kt_ref,
    dq_ref,
    dk_ref,
    dv_ref,
    diag_ref,
    side_ref,
    diag_sum,
    side_sum,
    *sems,
):
    parts, three, rows = qkv_ref.shape
    size = three // 3
    blocks = parts * rows // BLOCK
    half = BLOCK // 2
    scale = 1.0 / math.sqrt(size)
    greet(sizes, ["ctx", "exp"])
    arrive = Move(sizes, "ctx", do_in, do_ref, sems[0:3], split=True, takers=heads)
    back = Move(sizes, "ctx", sent_ref, grad_out, sems[3:6], split=True, senders=heads)
    experts = Move(sizes, "exp", out_in, out_out, sems[6:9], split=True)
    terms = Move(sizes, "exp", terms_in, terms_out, sems[9:12], split=True)
    start_all([arrive])
    start_all([experts, terms])
    is_head = lax.axis_index("ctx") < heads

    @pl.when(is_head)
    def _():
        diag_ref[...] = near_bias(table_ref, buckets, 0, BLOCK, BLOCK)
        side_ref[...] = near_bias(table_ref, buckets, half, half, half)
        diag_sum[...] = jnp.zeros_like(diag_sum)
        side_sum[...] = jnp.zeros_like(side_sum)
        dk_ref[...] = jnp.zeros_like(dk_ref)
        dv_ref[...] = jnp.zeros_like(dv_ref)
        for c in range(parts):
            at = slice(c * rows, (c + 1) * rows)
            kt_ref[:, at] = qkv_ref[c, size : 2 * size, :]
            k_ref[at, :] = transposed(qkv_ref[c, size : 2 * size, :])
            v_ref[at, :] = transposed(qkv_ref[c, 2 * size :, :])

    arrive.wait()

    @pl.when(is_head)
    def _():
        far = jnp.zeros((1, BLOCK), jnp.float32)
        for i in range(blocks):
            qt = scaled_queries(qkv_ref, i, size)
            dot_ = jnp.concatenate([do_ref[2 * i], do_ref[2 * i + 1]], axis=1)
            first = first_keys(bounds_ref, i * BLOCK)
            stat = stat_ref[i : i + 1, :]
            probs, grads = [], []
            delta = jnp.zeros((1, BLOCK), jnp.float32)
            for j in range(i + 1):
                s = block_scores(
                    i, j, blocks, qt, k_ref[block_of(j), :], diag_ref[...], side_ref[...], first
                )
                p = jnp.exp(s - stat)
                dp = dot_nn(v_ref[block_of(j), :], dot_)
                delta = delta + jnp.sum(p * dp, axis=0, keepdims=True)
                probs.append(p)
                grads.append(dp)
            dqt = jnp.zeros((size, BLOCK), jnp.float32)
            for j in range(i + 1):
                ds = probs[j] * (grads[j] - delta)
                if j == i:
                    diag_sum[...] += ds
                elif j == i - 1:
                    side_sum[...] += ds
                else:
                    far = far + jnp.sum(ds, axis=0, keepdims=True)
                low = ds.astype(jnp.bfloat16)
                dk_ref[:, block_of(j)] += dot_nt(qt, low)
                dv_ref[:, block_of(j)] += dot_nt(dot_, probs[j].astype(jnp.bfloat16))
                dqt = dqt + dot_nn(kt_ref[:, block_of(j)], low)
            dq_ref[:, block_of(i)] = (dqt * scale).astype(jnp.bfloat16)
        for c in range(parts):
            at = slice(c * rows, (c + 1) * rows)
            sent_ref[c, :size, :] = dq_ref[:, at]
            sent_ref[c, size : 2 * size, :] = dk_ref[:, at].astype(jnp.bfloat16)
            sent_ref[c, 2 * size :, :] = dv_ref[:, at].astype(jnp.bfloat16)
        bias_ref[0:1, :] = far

    start_all([back])

    @pl.when(is_head)
    def _():
        grad_ref[:size, :] = dq_ref[...]
        grad_ref[size : 2 * size, :] = dk_ref[...].astype(jnp.bfloat16)
        grad_ref[2 * size :, :] = dv_ref[...].astype(jnp.bfloat16)
        far = bias_ref[0:1, :] + jnp.sum(side_sum[:half, :], axis=0, keepdims=True)
        far_half = jnp.sum(side_sum[half:, half:], axis=0, keepdims=True)
        far = far + jnp.concatenate([jnp.zeros_like(far_half), far_half], axis=1)
        diag_bucket = near_buckets(buckets, 0, BLOCK, BLOCK)
        side_bucket = near_buckets(buckets, half, half, half)
        for b in range(buckets):
            one = jnp.sum(jnp.where(diag_bucket == b, diag_sum[...], 0.0), axis=0, keepdims=True)
            two = jnp.sum(
                jnp.where(side_bucket == b, side_sum[half:, :half], 0.0), axis=0, keepdims=True
            )
            row = one + jnp.concatenate([two, jnp.zeros_like(two)], axis=1)
            if b == buckets - 1:
                row = row + far
            bias_ref[b : b + 1, :] = row

    experts.wait()
    terms.wait()
    back.wait()
    for m in (arrive, back, experts, terms):
        m.wait_sent()


def attention_backward(sizes, do, expert_out, terms, qkv, stat, table, bounds):
    n_ctx, n_exp = sizes["ctx"], sizes["exp"]
    heads, size, rows = do.shape
    buckets = table.shape[0]
    seq = n_ctx * rows
    low, full = jnp.bfloat16, jnp.float32
    return pl.pallas_call(
        functools.partial(backward_kernel, sizes, heads, buckets),
        out_shape=[
            jax.ShapeDtypeStruct((heads, 3 * size, rows), low),
            jax.ShapeDtypeStruct(expert_out.shape, low),
            jax.ShapeDtypeStruct(terms.shape, low),
            jax.ShapeDtypeStruct((3 * size, seq), low),
            jax.ShapeDtypeStruct((buckets, BLOCK), full),
        ],
        in_specs=any_space(3) + in_vmem(3) + in_smem(1),
        out_specs=any_space(3) + in_vmem(2),
        scratch_shapes=[
            pltpu.VMEM((n_ctx, size, rows), low),
            pltpu.VMEM((n_ctx, 3 * size, rows), low),
            pltpu.VMEM((seq, size), low),
            pltpu.VMEM((seq, size), low),
            pltpu.VMEM((size, seq), low),
            pltpu.VMEM((size, seq), low),
            pltpu.VMEM((size, seq), full),
            pltpu.VMEM((size, seq), full),
            pltpu.VMEM((BLOCK, BLOCK), full),
            pltpu.VMEM((BLOCK // 2, BLOCK // 2), full),
            pltpu.VMEM((BLOCK, BLOCK), full),
            pltpu.VMEM((BLOCK, BLOCK), full),
        ]
        + move_sems(n_ctx)
        + move_sems(n_ctx)
        + move_sems(n_exp)
        + move_sems(n_exp),
        compiler_params=remote_params(3),
        cost_estimate=cost(20_000_000_000, 60_000_000, 2_400_000),
        name="attention_backward",
    )(do, expert_out, terms, qkv, stat, table, bounds)


def expert_kernel(
    rows_ref, g_ref, gate_ref, up_ref, down_ref, out_ref, back_ref, dgate_ref, wg_ref,
    dy_ref, sum_out, sum_back,
):
    step = pl.program_id(0)
    count, width = rows_ref.shape
    sources = gate_ref.shape[0]
    cap = count // sources

    @pl.when(step == 0)
    def _():
        lanes = jnp.concatenate([gate_ref[s, 0:1, :] for s in range(sources)], axis=0)
        columns = lanes.T
        for s in range(sources):
            at = slice(s * cap, (s + 1) * cap)
            gate = columns[:cap, s : s + 1]
            dy_ref[at, :] = (gate * g_ref[at, :].astype(jnp.float32)).astype(jnp.bfloat16)
        sum_out[...] = jnp.zeros_like(sum_out)
        sum_back[...] = jnp.zeros_like(sum_back)

    rows, dy = rows_ref[...], dy_ref[...]
    up, down = up_ref[0], down_ref[0]
    x = dot_nt(rows, up)
    c, a = math.sqrt(2.0 / math.pi), 0.044715
    square = x * x
    t = jnp.tanh(c * x * (1.0 + a * square))
    half = 0.5 * (1.0 + t)
    hidden = (x * half).astype(jnp.bfloat16)
    slope = half + 0.5 * x * (1.0 - t * t) * (c * (1.0 + 3.0 * a * square))
    dpre = (dot_nt(dy, down) * slope).astype(jnp.bfloat16)
    wg_ref[:, :width] = dot_tn(dpre, rows).astype(jnp.bfloat16)
    wg_ref[:, width:] = dot_tn(hidden, dy).astype(jnp.bfloat16)
    sum_out[...] += dot_nn(hidden, down)
    sum_back[...] += dot_nn(dpre, up)

    @pl.when(step == pl.num_programs(0) - 1)
    def _():
        back_ref[...] = sum_back[...].astype(jnp.bfloat16)
        out = sum_out[...].astype(jnp.bfloat16)
        out_ref[...] = out
        dgate = jnp.sum(out.astype(jnp.float32) * g_ref[...].astype(jnp.float32), axis=1, keepdims=True)
        lane = lax.broadcasted_iota(jnp.int32, (cap, 128), 1)
        columns = jnp.zeros((cap, 128), jnp.float32)
        for s in range(sources):
            columns = jnp.where(lane == s, dgate[s * cap : (s + 1) * cap, :], columns)
        turned = jnp.concatenate([columns] * (128 // cap), axis=0).T
        for s in range(sources):
            dgate_ref[s] = jnp.broadcast_to(turned[s : s + 1, :], (8, 128))


def run_expert(rows, g, gates, weights):
    count, width = rows.shape
    hidden = weights.shape[1]
    tile = 256
    low, full = jnp.bfloat16, jnp.float32
    whole = lambda shape: pl.BlockSpec(shape, lambda f: (0,) * len(shape))
    return pl.pallas_call(
        expert_kernel,
        grid=(hidden // tile,),
        out_shape=[
            jax.ShapeDtypeStruct((count, width), low),
            jax.ShapeDtypeStruct((count, width), low),
            jax.ShapeDtypeStruct(gates.shape, full),
            jax.ShapeDtypeStruct((hidden, 2 * width), low),
        ],
        in_specs=[
            whole((count, width)),
            whole((count, width)),
            whole(gates.shape),
            pl.BlockSpec((1, tile, width), lambda f: (0, f, 0)),
            pl.BlockSpec((1, tile, width), lambda f: (1, f, 0)),
        ],
        out_specs=[
            whole((count, width)),
            whole((count, width)),
            whole(gates.shape),
            pl.BlockSpec((tile, 2 * width), lambda f: (f, 0)),
        ],
        scratch_shapes=[
            pltpu.VMEM((count, width), low),
            pltpu.VMEM((count, width), full),
            pltpu.VMEM((count, width), full),
        ],
        compiler_params=pltpu.CompilerParams(vmem_limit_bytes=VMEM_BYTES),
        cost_estimate=cost(14_500_000_000, 24_000_000, 1_600_000),
        name="run_expert",
    )(rows, g, gates, weights, weights)


def total_kernel(
    sizes, heads, takers, head_in, small_in, out_in, qkv_out, weight_out, small_out, table_out,
    head_parts, small_parts, out_parts, head_sent, small_sent, out_sent,
    head_all, small_all, out_all, *sems,
):
    share, three = head_in.shape[1:]
    size = three // 3
    half = share // 2
    width = heads * size
    sixteen = out_sent.shape[0]
    me = lax.axis_index("ctx")
    greet(sizes, ["ctx", "exp"])
    first = [
        Move(sizes, "exp", head_in, head_parts, sems[0:3], split=True),
        Move(sizes, "exp", small_in, small_parts, sems[3:6], split=True),
        Move(sizes, "ctx", out_in, out_parts, sems[6:9], split=True, takers=takers),
    ]
    second = [
        Move(sizes, "ctx", head_sent, head_all, sems[9:12], senders=heads),
        Move(sizes, "ctx", small_sent, small_all, sems[12:15]),
        Move(sizes, "ctx", out_sent, out_all, sems[15:18], senders=takers),
    ]
    start_all(first)
    first[0].wait()
    total = head_parts[0].astype(jnp.float32)
    for s in range(1, sizes["exp"]):
        total = total + head_parts[s].astype(jnp.float32)
    total = total.astype(jnp.bfloat16)
    head_sent[:share, :] = total[:, : 2 * size]
    head_sent[share:, :] = jnp.concatenate(
        [total[:half, 2 * size :], total[half:, 2 * size :]], axis=1
    )
    start_all(second[:1])
    first[1].wait()
    little = small_parts[0]
    for s in range(1, sizes["exp"]):
        little = little + small_parts[s]
    small_sent[...] = little
    start_all(second[1:2])
    first[2].wait()

    @pl.when(me < takers)
    def _():
        weight = out_parts[0].astype(jnp.float32)
        for s in range(1, sizes["ctx"]):
            weight = weight + out_parts[s].astype(jnp.float32)
        out_sent[...] = weight.astype(jnp.bfloat16)

    start_all(second[2:])
    second[0].wait()
    for h in range(heads):
        got = head_all[h].astype(jnp.float32)
        at = h * size
        qkv_out[:, at : at + size] = got[:share, :size]
        qkv_out[:, width + at : width + at + size] = got[:share, size:]
        qkv_out[:half, 2 * width + at : 2 * width + at + size] = got[share:, :size]
        qkv_out[half:, 2 * width + at : 2 * width + at + size] = got[share:, size:]
    second[1].wait()
    sums = small_all[0]
    for s in range(1, sizes["ctx"]):
        sums = sums + small_all[s]
    small_out[...] = sums
    for h in range(heads):
        table_out[h : h + 1, :] = small_all[h, 0:1, :]
    second[2].wait()
    for s in range(takers):
        weight_out[s * sixteen : (s + 1) * sixteen, :] = out_all[s].astype(jnp.float32)
    for m in first + second:
        m.wait_sent()


def total_dense(sizes, heads, head_terms, small, out_terms):
    n_ctx, n_exp = sizes["ctx"], sizes["exp"]
    _, share, three = head_terms.shape
    takers, sixteen, width = out_terms.shape
    low, full = jnp.bfloat16, jnp.float32
    return pl.pallas_call(
        functools.partial(total_kernel, sizes, heads, takers),
        out_shape=[
            jax.ShapeDtypeStruct((share, 3 * width), full),
            jax.ShapeDtypeStruct((share, width), full),
            jax.ShapeDtypeStruct(small.shape[1:], full),
            jax.ShapeDtypeStruct((heads, 128), full),
        ],
        in_specs=in_vmem(3),
        out_specs=in_vmem(4),
        scratch_shapes=[
            pltpu.VMEM(head_terms.shape, low),
            pltpu.VMEM(small.shape, full),
            pltpu.VMEM((n_ctx, sixteen, width), low),
            pltpu.VMEM((share * 3 // 2, 128), low),
            pltpu.VMEM(small.shape[1:], full),
            pltpu.VMEM((sixteen, width), low),
            pltpu.VMEM((heads, share * 3 // 2, 128), low),
            pltpu.VMEM((n_ctx,) + small.shape[1:], full),
            pltpu.VMEM((takers, sixteen, width), low),
        ]
        + move_sems(n_exp)
        + move_sems(n_exp)
        + move_sems(n_ctx)
        + move_sems(n_ctx)
        + move_sems(n_ctx)
        + move_sems(n_ctx),
        compiler_params=remote_params(4),
        cost_estimate=cost(0, 60_000_000),
        name="total_dense",
    )(head_terms, small, out_terms)


def split_kernel(both_ref, up_ref, down_ref):
    width = up_ref.shape[1]
    up_ref[...] = both_ref[:, :width].astype(jnp.float32)
    down_ref[...] = both_ref[:, width:].astype(jnp.float32)


def split_weights(both):
    rows, width = both.shape[0], both.shape[1] // 2
    return pl.pallas_call(
        split_kernel,
        out_shape=[jax.ShapeDtypeStruct((rows, width), jnp.float32)] * 2,
        in_specs=in_vmem(1),
        out_specs=in_vmem(2),
        compiler_params=pltpu.CompilerParams(vmem_limit_bytes=8 * 1024 * 1024),
        cost_estimate=cost(0, 2_000_000),
        name="split_weights",
    )(both)


def rms_scale(values, gain_row):
    return (
        values * lax.rsqrt(jnp.mean(values * values, axis=-1, keepdims=True) + epsilon) * gain_row
    )


def local(
    sizes,
    block_in,
    attn_gain,
    moe_gain,
    query_key_value_weight,
    output_matrix,
    routing_weight,
    bias_table,
    up_weight,
    down_weight,
    routes,
    doc_lengths,
    cotangent,
):
    low, full = jnp.bfloat16, jnp.float32
    n_ctx, n_exp = sizes["ctx"], sizes["exp"]
    rows, width = block_in.shape[1:]
    seq_len = rows * n_ctx
    share = width // n_exp
    own_buckets, heads = bias_table.shape
    buckets = own_buckets * n_exp
    size = width // heads
    experts = routing_weight.shape[1]
    x_in = block_in[0].astype(full)
    g_low = cotangent[0]
    grad_out = g_low.astype(full)

    expert_weights = lax.all_gather(
        jnp.concatenate([up_weight, down_weight], axis=0), "ctx", axis=1, tiled=True
    )

    lanes = lambda a: jnp.pad(a, ((0, 0), (0, 128 - a.shape[1])))
    small = jnp.concatenate(
        [lanes(attn_gain[None]), lanes(moe_gain[None]), lanes(bias_table), lanes(routing_weight.T)],
        axis=0,
    )
    small = jnp.pad(small, ((0, -small.shape[0] % 16), (0, 0)))
    capacity = min(rows, 4 * rows // experts)
    piece = (experts, capacity, width)
    bounds = jnp.cumsum(doc_lengths[0]).astype(jnp.int32)
    (
        qkv_full,
        dense,
        proj_full,
        h_first,
        x_mid,
        h_second,
        info,
        mixed,
        qkv_head,
        stat,
        table_head,
        expert_rows,
        g_rows,
        gate_rows,
    ) = run_front(
        sizes,
        heads,
        experts,
        own_buckets,
        query_key_value_weight,
        small,
        output_matrix,
        block_in[0],
        g_low,
        routes[0].T,
        bounds,
    )
    h_all = lax.all_gather(h_first, "ctx", axis=0, tiled=True)
    qkv_full = qkv_full.reshape(width, 3 * width)
    proj_full = proj_full.reshape(width, width)
    attended_t = mixed.reshape(width, rows)
    gain_one = dense[:, 0, :share].reshape(width).astype(full)
    gain_two = dense[:, 1, :share].reshape(width).astype(full)
    router_t = dense[:, 2 + own_buckets : 2 + own_buckets + experts, :share]
    router_t = jnp.transpose(router_t, (1, 0, 2)).reshape(experts, width)
    gates = info[:2].T
    slots = jnp.arange(experts * capacity, dtype=jnp.int32).astype(full)
    found = [info[2 + c][:, None] == slots[None, :] for c in range(2)]
    choose = (routes[0][:, :, None] == jnp.arange(experts, dtype=jnp.int32)).astype(full)
    expert_out, expert_back, dgate, weight_terms = run_expert(
        expert_rows.reshape(experts * capacity, width),
        g_rows.reshape(experts * capacity, width),
        gate_rows,
        expert_weights,
    )
    h_all, weight_terms = lax.optimization_barrier((h_all, weight_terms))
    weight_grads = lax.psum_scatter(weight_terms, "ctx", scatter_dimension=0, tiled=True)
    grad_back, dgate = swap_experts(sizes, 6, expert_back.reshape(piece), dgate)

    grad_back = grad_back.reshape(experts * capacity, width)
    dgate = dgate[:, 0, :capacity].reshape(1, experts * capacity)
    grad_gates = jnp.stack(
        [jnp.sum(jnp.where(found[c], dgate, 0.0), axis=1) for c in range(2)], axis=-1
    )
    grad_chosen = gates * (grad_gates - jnp.sum(gates * grad_gates, axis=-1, keepdims=True))
    grad_logits = jnp.sum(choose * grad_chosen[:, :, None], axis=1).astype(low)
    grad_h_second = jnp.dot(
        (found[0] | found[1]).astype(low), grad_back, preferred_element_type=full
    ) + jnp.dot(grad_logits, router_t, preferred_element_type=full)
    grad_x_norm, grad_gain_two = jax.vjp(rms_scale, x_mid, gain_two)[1](grad_h_second)
    grad_x_mid = grad_out + grad_x_norm
    grad_proj = grad_x_mid.astype(low)
    grad_attended = dot_nt(proj_full, grad_proj).astype(low).reshape(heads, size, rows)
    out_terms = jnp.dot(attended_t, grad_proj, preferred_element_type=full).astype(low)

    grad_qkv_t, returned, out_parts, grad_head, bias_rows = attention_backward(
        sizes,
        grad_attended,
        expert_out.reshape(piece),
        out_terms.reshape(n_exp, share, width),
        qkv_head,
        stat,
        table_head,
        bounds,
    )
    grad_qkv_t = jnp.transpose(
        grad_qkv_t.reshape(heads, 3, size, rows), (1, 0, 2, 3)
    ).reshape(3 * width, rows)
    grad_h_first = lax.dot_general(
        grad_qkv_t, qkv_full, (((0,), (1,)), ((), ())), preferred_element_type=full
    )
    grad_x_first, grad_gain_one = jax.vjp(rms_scale, x_in, gain_one)[1](grad_h_first)
    grad_in = (grad_x_mid + grad_x_first)[None]
    grad_router = dot_tn(grad_logits, h_second).reshape(experts, n_exp, share)
    head_terms = (
        lax.dot_general(h_all, grad_head, (((0,), (1,)), ((), ())), preferred_element_type=full)
        .astype(low)
        .reshape(n_exp, share, 3 * size)
    )
    bias_part = jnp.sum(bias_rows, axis=1).reshape(n_exp, own_buckets)
    first_row = jnp.concatenate([grad_gain_one.reshape(n_exp, share), bias_part], axis=1)
    totals = jnp.concatenate(
        [
            lanes(first_row)[:, None, :],
            lanes(grad_gain_two.reshape(n_exp, share))[:, None, :],
            jnp.pad(jnp.transpose(grad_router, (1, 0, 2)), ((0, 0), (0, 0), (0, 128 - share))),
        ],
        axis=1,
    )
    totals = jnp.pad(totals, ((0, 0), (0, -totals.shape[1] % 8), (0, 0)))
    out_sum = jnp.sum(out_parts.astype(full), axis=0).astype(low).reshape(share // 16, 16, width)
    grad_qkv, grad_out_weight, sums, table_rows = total_dense(
        sizes, heads, head_terms, totals, out_sum
    )
    returned = returned.reshape(experts * capacity, width)
    picked = jnp.dot(
        jnp.concatenate(found, axis=0).astype(low), returned, preferred_element_type=full
    )
    block_out = x_mid + (gates[:, :1] * picked[:rows] + gates[:, 1:] * picked[rows:])
    grad_up, grad_down = split_weights(weight_grads)
    return (
        block_out.astype(low)[None],
        grad_in,
        sums[0, :share],
        sums[1, :share],
        grad_qkv,
        grad_out_weight,
        sums[2 : 2 + experts, :share].T,
        table_rows[:, share : share + own_buckets].T,
        grad_up[None],
        grad_down[None],
    )


def solution(mesh):
    sizes = {name: mesh.shape[name] for name in ("ctx", "exp")}
    tokens = P("exp", "ctx", None)
    row_split = P("exp", None)
    return jax.shard_map(
        functools.partial(local, sizes),
        mesh=mesh,
        in_specs=(
            tokens,
            P("exp"),
            P("exp"),
            row_split,
            row_split,
            row_split,
            row_split,
            tokens,
            tokens,
            tokens,
            row_split,
            tokens,
        ),
        out_specs=(
            tokens,
            tokens,
            P("exp"),
            P("exp"),
            row_split,
            row_split,
            row_split,
            row_split,
            tokens,
            tokens,
        ),
        check_vma=False,
    )
```

```python
import functools
import math

import jax
import jax.numpy as jnp
import numpy as np
from jax import lax
from jax.experimental import pallas as pl
from jax.experimental.pallas import tpu as pltpu
from jax.sharding import PartitionSpec as P

MAXD = 128
BLOCK = 256
MESH = pl.DeviceIdType.MESH
VMEM_BYTES = 60 * 1024 * 1024

epsilon = 1e-06
masked_score = -1e30


def bucket_thresholds(buckets, reach_len):
    exact_part = buckets // 2
    spread_part = buckets - exact_part
    return [
        int(math.ceil(exact_part * (reach_len / exact_part) ** (level / spread_part)))
        for level in range(1, spread_part)
    ]


def guarded(tests, action):
    tests = [t for t in tests if t is not None]
    if not tests:
        action()
    else:
        pl.when(functools.reduce(jnp.logical_and, tests))(action)


def greet(sizes, axes):
    barrier = pltpu.get_barrier_semaphore()
    total = 0
    for a in axes:
        me = lax.axis_index(a)
        for r in range(1, sizes[a]):
            peer = lax.rem(me + r, sizes[a])
            pl.semaphore_signal(barrier, inc=1, device_id={a: peer}, device_id_type=MESH)
            total += 1
    pl.semaphore_wait(barrier, total)


class Move:
    def __init__(self, sizes, axis, src, out, sems, split=False, senders=None, takers=None):
        self.n = sizes[axis]
        self.axis, self.src, self.out, self.split = axis, src, out, split
        self.send_sem, self.recv_sem, self.own_sem = sems
        self.senders, self.takers = senders or self.n, takers or self.n
        self.me = lax.axis_index(axis)

    def sends(self, device):
        return device < self.senders if self.senders < self.n else None

    def takes(self, device):
        return device < self.takers if self.takers < self.n else None

    def copy(self, r, peer, slot, piece):
        return pltpu.make_async_remote_copy(
            src_ref=self.src.at[piece] if self.split else self.src,
            dst_ref=self.out.at[slot],
            send_sem=self.send_sem.at[r],
            recv_sem=self.recv_sem.at[r],
            device_id={self.axis: peer},
            device_id_type=MESH,
        )

    def to(self, r):
        return lax.rem(self.me + r, self.n)

    def start(self, r):
        dst = self.to(r)
        guarded(
            [self.sends(self.me), self.takes(dst)],
            lambda: self.copy(r, dst, self.me, dst).start(),
        )

    def own(self):
        src = self.src.at[self.me] if self.split else self.src
        return pltpu.make_async_copy(src, self.out.at[self.me], self.own_sem)

    def start_own(self):
        guarded([self.sends(self.me), self.takes(self.me)], lambda: self.own().start())

    def wait(self):
        guarded([self.sends(self.me), self.takes(self.me)], lambda: self.own().wait())
        for r in range(1, self.n):
            src = lax.rem(self.me + self.n - r, self.n)
            guarded(
                [self.sends(src), self.takes(self.me)],
                lambda: self.copy(r, src, src, 0).wait_recv(),
            )

    def wait_sent(self):
        for r in range(1, self.n):
            dst = self.to(r)
            guarded(
                [self.sends(self.me), self.takes(dst)],
                lambda: self.copy(r, dst, self.me, dst).wait_send(),
            )


def start_all(moves):
    for r in range(1, max(m.n for m in moves)):
        for m in moves:
            if r < m.n:
                m.start(r)
    for m in moves:
        m.start_own()


class PairGather:
    def __init__(self, sizes, src, out, sems):
        self.n = sizes["exp"]
        self.src, self.out = src, out
        self.send_sem, self.recv_sem, self.own_sem = sems
        self.me = lax.axis_index("exp")
        core = lax.rem(self.me, 2)
        self.mate = self.me + 1 - 2 * core

    def copy(self, src, slot, k, peer):
        return pltpu.make_async_remote_copy(
            src_ref=src,
            dst_ref=self.out.at[slot],
            send_sem=self.send_sem.at[k],
            recv_sem=self.recv_sem.at[k],
            device_id={"exp": peer},
            device_id_type=MESH,
        )

    def own(self):
        return pltpu.make_async_copy(self.src, self.out.at[self.me], self.own_sem)

    def chips(self):
        return range(1, self.n // 2)

    def start(self):
        for r in self.chips():
            self.copy(self.src, self.me, r, lax.rem(self.me + 2 * r, self.n)).start()
        self.copy(self.src, self.me, 0, self.mate).start()
        self.own().start()

    def forward(self, r):
        slot = lax.rem(self.me + self.n - 2 * r, self.n)
        return self.copy(self.out.at[slot], slot, self.n // 2 + r, self.mate)

    def pass_on(self):
        for r in self.chips():
            slot = lax.rem(self.me + self.n - 2 * r, self.n)
            self.copy(self.src, slot, r, slot).wait_recv()
            self.forward(r).start()

    def finish(self):
        for r in self.chips():
            slot = lax.rem(self.mate + self.n - 2 * r, self.n)
            self.copy(self.src, slot, self.n // 2 + r, self.mate).wait_recv()
            self.forward(r).wait_send()
            self.copy(self.src, self.me, r, lax.rem(self.me + 2 * r, self.n)).wait_send()
        self.copy(self.src, self.mate, 0, self.mate).wait_recv()
        self.copy(self.src, self.me, 0, self.mate).wait_send()
        self.own().wait()


def move_sems(count):
    return [
        pltpu.SemaphoreType.DMA((count,)),
        pltpu.SemaphoreType.DMA((count,)),
        pltpu.SemaphoreType.DMA,
    ]


def any_space(count):
    return [pl.BlockSpec(memory_space=pl.ANY)] * count


def in_vmem(count):
    return [pl.BlockSpec(memory_space=pltpu.VMEM)] * count


def in_smem(count):
    return [pl.BlockSpec(memory_space=pltpu.SMEM)] * count


def remote_params(number, limit=VMEM_BYTES):
    return pltpu.CompilerParams(
        collective_id=number, has_side_effects=True, vmem_limit_bytes=limit
    )


def cost(flops, moved, special=0):
    return pl.CostEstimate(flops=flops, bytes_accessed=moved, transcendentals=special)


def dot_nt(left, right):
    return lax.dot_general(
        left, right, (((1,), (1,)), ((), ())), preferred_element_type=jnp.float32
    )


def dot_tn(left, right):
    return lax.dot_general(
        left, right, (((0,), (0,)), ((), ())), preferred_element_type=jnp.float32
    )


def dot_nn(left, right):
    return jnp.dot(left, right, preferred_element_type=jnp.float32)


def near_buckets(buckets, offset, rows, cols):
    key = lax.broadcasted_iota(jnp.int32, (rows, cols), 0)
    query = lax.broadcasted_iota(jnp.int32, (rows, cols), 1)
    distance = jnp.clip(query - key + offset, 0, MAXD)
    bucket = jnp.minimum(distance, buckets // 2)
    for level in bucket_thresholds(buckets, MAXD):
        bucket = bucket + (distance >= level).astype(jnp.int32)
    return bucket


def near_bias(table_ref, buckets, offset, rows, cols):
    bucket = near_buckets(buckets, offset, rows, cols)
    last = table_ref[buckets - 1 : buckets, 0:1]
    bias = jnp.zeros((rows, cols), jnp.float32)
    for b in range(buckets - 1):
        bias = jnp.where(bucket == b, table_ref[b : b + 1, 0:1] - last, bias)
    return bias


def first_keys(lengths_ref, start):
    query = start + lax.broadcasted_iota(jnp.int32, (1, BLOCK), 1)
    first = jnp.zeros((1, BLOCK), jnp.int32)
    bound = jnp.int32(0)
    for d in range(3):
        bound = bound + lengths_ref[d]
        first = jnp.where(query >= bound, bound, first)
    return first


def block_scores(i, j, blocks, qt, k, diag_bias, side_bias, first):
    s = dot_nn(k, qt)
    half = BLOCK // 2
    if j == i:
        s = s + diag_bias
    elif j == i - 1:
        lower = jnp.concatenate([s[half:, :half] + side_bias, s[half:, half:]], axis=1)
        s = jnp.concatenate([s[:half], lower], axis=0)
    if j == i or j == 0 or i == blocks - 1:
        key = lax.broadcasted_iota(jnp.int32, (BLOCK, BLOCK), 0)
        keep = key + j * BLOCK >= first
        if j == i:
            keep = keep & (key <= lax.broadcasted_iota(jnp.int32, (BLOCK, BLOCK), 1))
        s = jnp.where(keep, s, masked_score)
    return s


def transposed(piece):
    return piece.astype(jnp.float32).T.astype(jnp.bfloat16)


def scaled_queries(qkv_ref, i, size):
    scale = 1.0 / math.sqrt(size)
    both = jnp.concatenate([qkv_ref[2 * i, :size, :], qkv_ref[2 * i + 1, :size, :]], axis=1)
    return (both * scale).astype(jnp.bfloat16)


def block_of(j):
    return slice(j * BLOCK, (j + 1) * BLOCK)


def bucket_values(small_ref, own_buckets, heads):
    head = jnp.minimum(lax.axis_index("ctx"), heads - 1)
    rows = jnp.concatenate(
        [small_ref[e, 2 : 2 + own_buckets, :] for e in range(small_ref.shape[0])], axis=0
    ).astype(jnp.float32)
    lane = lax.broadcasted_iota(jnp.int32, rows.shape, 1)
    value = jnp.sum(jnp.where(lane == head, rows, 0.0), axis=1, keepdims=True)
    return jnp.broadcast_to(value, rows.shape)


def full_row(small_ref, row, share):
    pieces = [small_ref[e, row : row + 1, :share] for e in range(small_ref.shape[0])]
    return jnp.concatenate(pieces, axis=1).astype(jnp.float32)


def norm_rows(x, gain):
    scale = lax.rsqrt(jnp.mean(x * x, axis=-1, keepdims=True) + epsilon)
    return (x * scale * gain).astype(jnp.bfloat16)


def columns_to_rows(column, groups):
    cap = column.shape[0] // groups
    lane = lax.broadcasted_iota(jnp.int32, (cap, 128), 1)
    spread = jnp.zeros((cap, 128), jnp.float32)
    for s in range(groups):
        spread = jnp.where(lane == s, column[s * cap : (s + 1) * cap, :], spread)
    return jnp.concatenate([spread] * (128 // cap), axis=0).T


def front_kernel(
    sizes,
    heads,
    experts,
    own_buckets,
    w_in,
    small_in,
    proj_in,
    x_ref,
    g_ref,
    route_ref,
    lengths_ref,
    w_ref,
    small_ref,
    proj_ref,
    h_ref,
    mid_ref,
    second_ref,
    info_ref,
    mixed_ref,
    qkv_ref,
    stat_ref,
    table_ref,
    rows_out,
    g_out,
    gate_out,
    qkv_sent,
    sent_ref,
    k_ref,
    vt_ref,
    diag_ref,
    side_ref,
    rows_sent,
    g_sent,
    gate_sent,
    *sems,
):
    n_exp = sizes["exp"]
    parts, three, rows = qkv_ref.shape
    size = three // 3
    width = heads * size
    share = width // n_exp
    blocks = parts * rows // BLOCK
    half = BLOCK // 2
    buckets = own_buckets * n_exp
    cap = rows_sent.shape[1]
    greet(sizes, ["exp", "ctx"])
    weight = PairGather(sizes, w_in, w_ref, sems[0:3])
    little = Move(sizes, "exp", small_in, small_ref, sems[3:6])
    proj = PairGather(sizes, proj_in, proj_ref, sems[6:9])
    grads = Move(sizes, "exp", g_sent, g_out, sems[9:12], split=True)
    arrive = Move(sizes, "ctx", qkv_sent, qkv_ref, sems[12:15], split=True, takers=heads)
    back = Move(sizes, "ctx", sent_ref, mixed_ref, sems[15:18], split=True, senders=heads)
    hidden = Move(sizes, "exp", rows_sent, rows_out, sems[18:21], split=True)
    gating = Move(sizes, "exp", gate_sent, gate_out, sems[21:24], split=True)
    start_all([little])
    weight.start()

    expert = lax.broadcasted_iota(jnp.int32, (experts, rows), 0)
    chosen = [(expert == route_ref[c : c + 1, :]).astype(jnp.float32) for c in range(2)]
    earlier = lax.broadcasted_iota(jnp.int32, (rows, rows), 0) < lax.broadcasted_iota(
        jnp.int32, (rows, rows), 1
    )
    count = dot_nn((chosen[0] + chosen[1]).astype(jnp.bfloat16), earlier.astype(jnp.bfloat16))
    place = count + (expert * cap).astype(jnp.float32)
    slot = [jnp.sum(chosen[c] * place, axis=0, keepdims=True) for c in range(2)]
    slots = lax.broadcasted_iota(jnp.int32, (experts * cap, rows), 0).astype(jnp.float32)
    hit = [slots == slot[c] for c in range(2)]
    either = (hit[0] | hit[1]).astype(jnp.bfloat16)
    send_g = dot_nn(either, g_ref[...]).astype(jnp.bfloat16)
    for e in range(experts):
        g_sent[e] = send_g[e * cap : (e + 1) * cap, :]

    little.wait()
    table_ref[...] = bucket_values(small_ref, own_buckets, heads)
    x = x_ref[...].astype(jnp.float32)
    h = norm_rows(x, full_row(small_ref, 0, share))
    h_ref[...] = h
    diag_ref[...] = near_bias(table_ref, buckets, 0, BLOCK, BLOCK)
    side_ref[...] = near_bias(table_ref, buckets, half, half, half)
    weight.pass_on()
    proj.start()
    weight.finish()
    for at in range(0, 3 * width, 2 * rows):
        piece = w_ref[:, :, at : at + 2 * rows].reshape(width, 2 * rows)
        turned = dot_nn(h, piece).T.astype(jnp.bfloat16)
        for begin in range(0, 2 * rows, size):
            part, head = divmod((at + begin) // size, heads)
            qkv_sent[head, part * size : (part + 1) * size, :] = turned[begin : begin + size, :]
    start_all([arrive])
    proj.pass_on()
    start_all([grads])
    arrive.wait()

    @pl.when(lax.axis_index("ctx") < heads)
    def _():
        for c in range(parts):
            at = slice(c * rows, (c + 1) * rows)
            k_ref[at, :] = transposed(qkv_ref[c, size : 2 * size, :])
            vt_ref[:, at] = qkv_ref[c, 2 * size :, :]
        for i in range(blocks):
            qt = scaled_queries(qkv_ref, i, size)
            first = first_keys(lengths_ref, i * BLOCK)
            scores = []
            top = None
            for j in range(i + 1):
                s = block_scores(
                    i, j, blocks, qt, k_ref[block_of(j), :], diag_ref[...], side_ref[...], first
                )
                scores.append(s)
                here = jnp.max(s, axis=0, keepdims=True)
                top = here if top is None else jnp.maximum(top, here)
            total = jnp.zeros((1, BLOCK), jnp.float32)
            for j in range(i + 1):
                scores[j] = jnp.exp(scores[j] - top)
                total = total + jnp.sum(scores[j], axis=0, keepdims=True)
            inverse = 1.0 / total
            mixed = jnp.zeros((size, BLOCK), jnp.float32)
            for j in range(i + 1):
                probs = (scores[j] * inverse).astype(jnp.bfloat16)
                mixed = mixed + dot_nn(vt_ref[:, block_of(j)], probs)
            mixed = mixed.astype(jnp.bfloat16)
            sent_ref[2 * i] = mixed[:, :half]
            sent_ref[2 * i + 1] = mixed[:, half:]
            stat_ref[i : i + 1, :] = top + jnp.log(total)

    start_all([back])
    proj.finish()
    back.wait()

    attended = transposed(mixed_ref[...].reshape(width, rows))
    mid = x + dot_nn(attended, proj_ref[...].reshape(width, width))
    mid_ref[...] = mid
    second = norm_rows(mid, full_row(small_ref, 1, share))
    second_ref[...] = second
    send = dot_nn(either, second).astype(jnp.bfloat16)
    for e in range(experts):
        rows_sent[e] = send[e * cap : (e + 1) * cap, :]
    start_all([hidden])
    begin = 2 + own_buckets
    router = jnp.concatenate(
        [small_ref[e, begin : begin + experts, :share] for e in range(n_exp)], axis=1
    )
    z = dot_nt(router, second)
    picked = [jnp.sum(chosen[c] * z, axis=0, keepdims=True) for c in range(2)]
    top = jnp.maximum(picked[0], picked[1])
    raised = [jnp.exp(p - top) for p in picked]
    gates = [r / (raised[0] + raised[1]) for r in raised]
    column = sum(
        jnp.sum(jnp.where(hit[c], gates[c], 0.0), axis=1, keepdims=True) for c in range(2)
    )
    turned = columns_to_rows(column, experts)
    for e in range(experts):
        gate_sent[e] = jnp.broadcast_to(turned[e : e + 1, :], (8, 128))
    start_all([gating])
    info_ref[...] = jnp.concatenate(
        gates + slot + [route_ref[c : c + 1, :].astype(jnp.float32) for c in range(2)] + slot,
        axis=0,
    )
    grads.wait()
    gating.wait()
    hidden.wait()
    for m in (little, grads, arrive, back, hidden, gating):
        m.wait_sent()


def run_front(sizes, heads, experts, own_buckets, weight, small, proj, x, g, route_t, lengths):
    n_ctx, n_exp = sizes["ctx"], sizes["exp"]
    rows, width = x.shape
    size = width // heads
    seq = n_ctx * rows
    cap = min(rows, 4 * rows // experts)
    low, full = jnp.bfloat16, jnp.float32
    assert 2 * rows == BLOCK and rows == 128 and 3 * width % (2 * rows) == 0
    return pl.pallas_call(
        functools.partial(front_kernel, sizes, heads, experts, own_buckets),
        out_shape=[
            jax.ShapeDtypeStruct((n_exp,) + weight.shape, low),
            jax.ShapeDtypeStruct((n_exp,) + small.shape, low),
            jax.ShapeDtypeStruct((n_exp,) + proj.shape, low),
            jax.ShapeDtypeStruct((rows, width), low),
            jax.ShapeDtypeStruct((rows, width), full),
            jax.ShapeDtypeStruct((rows, width), low),
            jax.ShapeDtypeStruct((8, rows), full),
            jax.ShapeDtypeStruct((heads, size, rows), low),
            jax.ShapeDtypeStruct((n_ctx, 3 * size, rows), low),
            jax.ShapeDtypeStruct((seq // BLOCK, BLOCK), full),
            jax.ShapeDtypeStruct((own_buckets * n_exp, 128), full),
            jax.ShapeDtypeStruct((experts, cap, width), low),
            jax.ShapeDtypeStruct((experts, cap, width), low),
            jax.ShapeDtypeStruct((experts, 8, 128), full),
        ],
        in_specs=in_vmem(6) + in_smem(1),
        out_specs=in_vmem(14),
        scratch_shapes=[
            pltpu.VMEM((heads, 3 * size, rows), low),
            pltpu.VMEM((n_ctx, size, rows), low),
            pltpu.VMEM((seq, size), low),
            pltpu.VMEM((size, seq), low),
            pltpu.VMEM((BLOCK, BLOCK), full),
            pltpu.VMEM((BLOCK // 2, BLOCK // 2), full),
            pltpu.VMEM((experts, cap, width), low),
            pltpu.VMEM((experts, cap, width), low),
            pltpu.VMEM((experts, 8, 128), full),
        ]
        + move_sems(n_exp) * 4
        + move_sems(n_ctx) * 2
        + move_sems(n_exp) * 2,
        compiler_params=remote_params(1),
        cost_estimate=cost(60_000_000_000, 100_000_000, 2_400_000),
        name="run_front",
    )(weight, small, proj, x, g, route_t, lengths)


def expert_kernel(
    rows_ref, g_ref, gate_ref, up_ref, down_ref, out_ref, back_ref, dgate_ref, gup_ref, gdown_ref,
    dy_ref, sum_out, sum_back,
):
    step = pl.program_id(0)
    count, width = rows_ref.shape
    sources = gate_ref.shape[0]
    cap = count // sources

    @pl.when(step == 0)
    def _():
        lanes = jnp.concatenate([gate_ref[s, 0:1, :] for s in range(sources)], axis=0)
        columns = lanes.T
        for s in range(sources):
            at = slice(s * cap, (s + 1) * cap)
            gate = columns[:cap, s : s + 1]
            dy_ref[at, :] = (gate * g_ref[at, :].astype(jnp.float32)).astype(jnp.bfloat16)
        sum_out[...] = jnp.zeros_like(sum_out)
        sum_back[...] = jnp.zeros_like(sum_back)

    rows, dy = rows_ref[...], dy_ref[...]
    up, down = up_ref[0], down_ref[0]
    x = dot_nt(rows, up)
    c, a = math.sqrt(2.0 / math.pi), 0.044715
    square = x * x
    t = jnp.tanh(c * x * (1.0 + a * square))
    half = 0.5 * (1.0 + t)
    hidden = (x * half).astype(jnp.bfloat16)
    slope = half + 0.5 * x * (1.0 - t * t) * (c * (1.0 + 3.0 * a * square))
    dpre = (dot_nt(dy, down) * slope).astype(jnp.bfloat16)
    gup_ref[...] = dot_tn(dpre, rows).astype(jnp.bfloat16)
    gdown_ref[...] = dot_tn(hidden, dy).astype(jnp.bfloat16)
    sum_out[...] += dot_nn(hidden, down)
    sum_back[...] += dot_nn(dpre, up)

    @pl.when(step == pl.num_programs(0) - 1)
    def _():
        back_ref[...] = sum_back[...].astype(jnp.bfloat16)
        out = sum_out[...].astype(jnp.bfloat16)
        out_ref[...] = out
        dgate = jnp.sum(out.astype(jnp.float32) * g_ref[...].astype(jnp.float32), axis=1, keepdims=True)
        lane = lax.broadcasted_iota(jnp.int32, (cap, 128), 1)
        columns = jnp.zeros((cap, 128), jnp.float32)
        for s in range(sources):
            columns = jnp.where(lane == s, dgate[s * cap : (s + 1) * cap, :], columns)
        turned = jnp.concatenate([columns] * (128 // cap), axis=0).T
        for s in range(sources):
            dgate_ref[s] = jnp.broadcast_to(turned[s : s + 1, :], (8, 128))


def run_expert(rows, g, gates, weights):
    count, width = rows.shape
    hidden = weights.shape[1]
    tile = 768
    low, full = jnp.bfloat16, jnp.float32
    whole = lambda shape: pl.BlockSpec(shape, lambda f: (0,) * len(shape))
    return pl.pallas_call(
        expert_kernel,
        grid=(hidden // tile,),
        out_shape=[
            jax.ShapeDtypeStruct((count, width), low),
            jax.ShapeDtypeStruct((count, width), low),
            jax.ShapeDtypeStruct(gates.shape, full),
            jax.ShapeDtypeStruct((hidden, width), low),
            jax.ShapeDtypeStruct((hidden, width), low),
        ],
        in_specs=[
            whole((count, width)),
            whole((count, width)),
            whole(gates.shape),
            pl.BlockSpec((1, tile, width), lambda f: (0, f, 0)),
            pl.BlockSpec((1, tile, width), lambda f: (1, f, 0)),
        ],
        out_specs=[
            whole((count, width)),
            whole((count, width)),
            whole(gates.shape),
            pl.BlockSpec((tile, width), lambda f: (f, 0)),
            pl.BlockSpec((tile, width), lambda f: (f, 0)),
        ],
        scratch_shapes=[
            pltpu.VMEM((count, width), low),
            pltpu.VMEM((count, width), full),
            pltpu.VMEM((count, width), full),
        ],
        compiler_params=pltpu.CompilerParams(vmem_limit_bytes=VMEM_BYTES),
        cost_estimate=cost(14_500_000_000, 24_000_000, 1_600_000),
        name="run_expert",
    )(rows, g, gates, weights, weights)


class RingSum:
    def __init__(self, along_major, view, bufs, sems):
        place = lax.axis_index("ctx")
        major, minor = lax.div(place, 4), lax.rem(place, 4)
        self.me = major if along_major else minor
        self.device = (lambda k: k * 4 + minor) if along_major else (lambda k: major * 4 + k)
        self.plus, self.minus = lax.rem(self.me + 1, 4), lax.rem(self.me + 3, 4)
        self.far = lax.rem(self.me + 2, 4)
        self.view = view
        self.step, self.added, self.got, self.own = bufs
        self.send_sem, self.recv_sem, self.own_sem = sems

    def copy(self, k):
        src, dst, peer = (
            (lambda: self.view(self.far, 0), self.step.at[0], self.plus),
            (lambda: self.view(self.far, 1), self.step.at[1], self.minus),
            (lambda: self.view(self.plus, 1), self.got.at[0, 1], self.plus),
            (lambda: self.view(self.minus, 0), self.got.at[1, 0], self.minus),
            (lambda: self.added.at[0], self.got.at[0, 0], self.plus),
            (lambda: self.added.at[1], self.got.at[1, 1], self.minus),
        )[k]
        return pltpu.make_async_remote_copy(
            src_ref=src(),
            dst_ref=dst,
            send_sem=self.send_sem.at[k],
            recv_sem=self.recv_sem.at[k],
            device_id={"ctx": self.device(peer)},
            device_id_type=MESH,
        )

    def local(self, k):
        src, dst = (
            (self.view(self.plus, 0), self.added.at[0]),
            (self.view(self.minus, 1), self.added.at[1]),
            (self.view(self.me, 0), self.own.at[0]),
            (self.view(self.me, 1), self.own.at[1]),
        )[k]
        return pltpu.make_async_copy(src, dst, self.own_sem.at[k])

    def start(self):
        for k in range(4):
            self.copy(k).start()
        for k in range(4):
            self.local(k).start()

    def turn(self):
        for k in range(2):
            self.copy(k).wait_recv()
            self.local(k).wait()
            total = self.added[k].astype(jnp.float32) + self.step[k].astype(jnp.float32)
            self.added[k] = total.astype(jnp.bfloat16)
            self.copy(4 + k).start()

    def wait(self):
        for k in range(2, 4):
            self.local(k).wait()
        for k in range(2, 6):
            self.copy(k).wait_recv()

    def half(self, h, *at):
        parts = (self.own[(h,) + at], self.got[(0, h) + at], self.got[(1, h) + at])
        return sum(p.astype(jnp.float32) for p in parts)

    def wait_sent(self):
        for k in range(6):
            self.copy(k).wait_send()


def ring_space(shape):
    low = jnp.bfloat16
    return [
        pltpu.VMEM((2,) + shape, low),
        pltpu.VMEM((2,) + shape, low),
        pltpu.VMEM((2, 2) + shape, low),
        pltpu.VMEM((2,) + shape, low),
    ]


def ring_sems():
    return [pltpu.SemaphoreType.DMA((6,)), pltpu.SemaphoreType.DMA((6,)), pltpu.SemaphoreType.DMA((4,))]


def norm_back(x, gain, grad):
    scale = lax.rsqrt(jnp.mean(x * x, axis=-1, keepdims=True) + epsilon)
    scaled = grad * gain
    inner = jnp.mean(scaled * x, axis=-1, keepdims=True)
    grad_x = scale * scaled - x * (scale * scale * scale) * inner
    return grad_x, jnp.sum(grad * x * scale, axis=0, keepdims=True)


def summed(ref, count):
    total = ref[0].astype(jnp.float32)
    for s in range(1, count):
        total = total + ref[s].astype(jnp.float32)
    return total


def middle_kernel(
    sizes,
    heads,
    experts,
    own_buckets,
    back_in,
    dgate_in,
    out_in,
    up_in,
    down_in,
    info_ref,
    g_ref,
    mid_ref,
    second_ref,
    small_ref,
    proj_ref,
    mixed_ref,
    qkv_ref,
    stat_ref,
    table_ref,
    lengths_ref,
    grad_out,
    out_out,
    piece_ref,
    grad_ref,
    bias_ref,
    dmid_ref,
    part_ref,
    up_sum,
    down_sum,
    back_got,
    dgate_got,
    do_sent,
    do_ref,
    sent_ref,
    terms_sent,
    terms_got,
    up_a,
    up_b,
    up_c,
    up_d,
    down_a,
    down_b,
    down_c,
    down_d,
    k_ref,
    v_ref,
    kt_ref,
    dq_ref,
    dk_ref,
    dv_ref,
    diag_ref,
    side_ref,
    diag_sum,
    side_sum,
    *sems,
):
    n_exp = sizes["exp"]
    parts, three, rows = qkv_ref.shape
    size = three // 3
    width = heads * size
    share = width // n_exp
    blocks = parts * rows // BLOCK
    half = BLOCK // 2
    buckets = own_buckets * n_exp
    cap = back_got.shape[1]
    side = math.isqrt(parts)
    scale = 1.0 / math.sqrt(size)
    greet(sizes, ["exp", "ctx"])
    returned = Move(sizes, "exp", back_in, back_got, sems[0:3], split=True)
    gating = Move(sizes, "exp", dgate_in, dgate_got, sems[3:6], split=True)
    outs = Move(sizes, "exp", out_in, out_out, sems[6:9], split=True)
    terms = Move(sizes, "exp", terms_sent, terms_got, sems[9:12], split=True)
    arrive = Move(sizes, "ctx", do_sent, do_ref, sems[12:15], split=True, takers=heads)
    back = Move(sizes, "ctx", sent_ref, grad_out, sems[15:18], split=True, senders=heads)
    ups = RingSum(
        True, lambda k, h: up_in.at[k, pl.ds(2 * h, 2)], (up_a, up_b, up_c, up_d), sems[18:21]
    )
    downs = RingSum(
        False,
        lambda k, h: down_in.at[pl.ds(2 * h, 2), k],
        (down_a, down_b, down_c, down_d),
        sems[21:24],
    )
    start_all([gating, returned])
    ups.start()
    downs.start()
    is_head = lax.axis_index("ctx") < heads

    @pl.when(is_head)
    def _():
        diag_ref[...] = near_bias(table_ref, buckets, 0, BLOCK, BLOCK)
        side_ref[...] = near_bias(table_ref, buckets, half, half, half)
        diag_sum[...] = jnp.zeros_like(diag_sum)
        side_sum[...] = jnp.zeros_like(side_sum)
        dk_ref[...] = jnp.zeros_like(dk_ref)
        dv_ref[...] = jnp.zeros_like(dv_ref)
        for c in range(parts):
            at = slice(c * rows, (c + 1) * rows)
            kt_ref[:, at] = qkv_ref[c, size : 2 * size, :]
            k_ref[at, :] = transposed(qkv_ref[c, size : 2 * size, :])
            v_ref[at, :] = transposed(qkv_ref[c, 2 * size :, :])

    gates = [info_ref[c : c + 1, :] for c in range(2)]
    slots = lax.broadcasted_iota(jnp.int32, (experts * cap, rows), 0).astype(jnp.float32)
    hit = [slots == info_ref[2 + c : 3 + c, :] for c in range(2)]
    expert = lax.broadcasted_iota(jnp.int32, (experts, rows), 0).astype(jnp.float32)
    chosen = [(expert == info_ref[4 + c : 5 + c, :]).astype(jnp.float32) for c in range(2)]
    begin = 2 + own_buckets
    router = jnp.concatenate(
        [small_ref[e, begin : begin + experts, :share] for e in range(n_exp)], axis=1
    )
    either = (hit[0] | hit[1]).astype(jnp.bfloat16)

    gating.wait()
    turned = jnp.concatenate([dgate_got[e, 0:1, :] for e in range(experts)], axis=0).T
    column = jnp.concatenate([turned[:cap, e : e + 1] for e in range(experts)], axis=0)
    dgate = [jnp.sum(jnp.where(hit[c], column, 0.0), axis=0, keepdims=True) for c in range(2)]
    inner = gates[0] * dgate[0] + gates[1] * dgate[1]
    dz = sum(chosen[c] * (gates[c] * (dgate[c] - inner)) for c in range(2))
    dz_low = dz.astype(jnp.bfloat16)
    dz_tall = jnp.concatenate([dz, jnp.zeros((rows - experts, rows), jnp.float32)], axis=0)
    router_tall = jnp.concatenate(
        [router, jnp.zeros((rows - experts, width), jnp.bfloat16)], axis=0
    )
    from_router = dot_nn(dz_tall.T.astype(jnp.bfloat16), router_tall)
    part_ref[...] = jnp.zeros_like(part_ref)
    part_ref[8 : 8 + experts, :] = dot_nn(dz_low, second_ref[...])

    returned.wait()
    start_all([outs])
    dh = dot_tn(either, back_got[...].reshape(experts * cap, width)) + from_router
    grad_mid, grad_gain = norm_back(mid_ref[...], full_row(small_ref, 1, share), dh)
    grad_mid = g_ref[...].astype(jnp.float32) + grad_mid
    dmid_ref[...] = grad_mid
    part_ref[0:1, :] = grad_gain
    low_mid = grad_mid.astype(jnp.bfloat16)
    do_all = dot_nt(proj_ref[...].reshape(width, width), low_mid).astype(jnp.bfloat16)
    for h in range(heads):
        do_sent[h] = do_all[h * size : (h + 1) * size, :]
    start_all([arrive])
    terms_sent[...] = (
        dot_nn(mixed_ref[...].reshape(width, rows), low_mid)
        .astype(jnp.bfloat16)
        .reshape(n_exp, share, width)
    )
    start_all([terms])
    ups.turn()
    downs.turn()
    arrive.wait()

    @pl.when(is_head)
    def _():
        far = jnp.zeros((1, BLOCK), jnp.float32)
        for i in range(blocks):
            qt = scaled_queries(qkv_ref, i, size)
            dot_ = jnp.concatenate([do_ref[2 * i], do_ref[2 * i + 1]], axis=1)
            first = first_keys(lengths_ref, i * BLOCK)
            stat = stat_ref[i : i + 1, :]
            probs, grads = [], []
            delta = jnp.zeros((1, BLOCK), jnp.float32)
            for j in range(i + 1):
                s = block_scores(
                    i, j, blocks, qt, k_ref[block_of(j), :], diag_ref[...], side_ref[...], first
                )
                p = jnp.exp(s - stat)
                dp = dot_nn(v_ref[block_of(j), :], dot_)
                delta = delta + jnp.sum(p * dp, axis=0, keepdims=True)
                probs.append(p)
                grads.append(dp)
            dqt = jnp.zeros((size, BLOCK), jnp.float32)
            for j in range(i + 1):
                ds = probs[j] * (grads[j] - delta)
                if j == i:
                    diag_sum[...] += ds
                elif j == i - 1:
                    side_sum[...] += ds
                else:
                    far = far + jnp.sum(ds, axis=0, keepdims=True)
                low = ds.astype(jnp.bfloat16)
                dk_ref[:, block_of(j)] += dot_nt(qt, low)
                dv_ref[:, block_of(j)] += dot_nt(dot_, probs[j].astype(jnp.bfloat16))
                dqt = dqt + dot_nn(kt_ref[:, block_of(j)], low)
            dq_ref[:, block_of(i)] = (dqt * scale).astype(jnp.bfloat16)
        for c in range(parts):
            at = slice(c * rows, (c + 1) * rows)
            sent_ref[c, :size, :] = dq_ref[:, at]
            sent_ref[c, size : 2 * size, :] = dk_ref[:, at].astype(jnp.bfloat16)
            sent_ref[c, 2 * size :, :] = dv_ref[:, at].astype(jnp.bfloat16)
        bias_ref[0:1, :] = far[:, :half] + far[:, half:]

    start_all([back])

    @pl.when(is_head)
    def _():
        grad_ref[:size, :] = dq_ref[...]
        grad_ref[size : 2 * size, :] = dk_ref[...].astype(jnp.bfloat16)
        grad_ref[2 * size :, :] = dv_ref[...].astype(jnp.bfloat16)
        far = bias_ref[0:1, :] + jnp.sum(side_sum[:half, :half], axis=0, keepdims=True)
        far = far + jnp.sum(side_sum[:, half:], axis=0, keepdims=True)
        diag_bucket = near_buckets(buckets, 0, BLOCK, BLOCK)
        side_bucket = near_buckets(buckets, half, half, half)
        for b in range(buckets):
            one = jnp.sum(jnp.where(diag_bucket == b, diag_sum[...], 0.0), axis=0, keepdims=True)
            two = jnp.sum(
                jnp.where(side_bucket == b, side_sum[half:, :half], 0.0), axis=0, keepdims=True
            )
            row = one[:, :half] + one[:, half:] + two
            if b == buckets - 1:
                row = row + far
            bias_ref[b : b + 1, :] = row

    terms.wait()
    total = summed(terms_got, n_exp).astype(jnp.bfloat16)
    for t in range(piece_ref.shape[0]):
        piece_ref[t] = total[t * 16 : (t + 1) * 16, :]
    ups.wait()
    downs.wait()
    for k in range(side):
        up_sum[k] = ups.half(k // 2, k % 2).astype(jnp.bfloat16)
        down_sum[k] = downs.half(k // 2, k % 2).astype(jnp.bfloat16)
    outs.wait()
    back.wait()
    for m in (returned, gating, outs, terms, arrive, back, ups, downs):
        m.wait_sent()


def run_middle(
    sizes, heads, experts, own_buckets, expert_back, dgate, expert_out, up_terms, down_terms, info,
    g, mid, second, dense, proj, mixed, qkv, stat, table, lengths,
):
    n_ctx, n_exp = sizes["ctx"], sizes["exp"]
    rows, width = mid.shape
    size = width // heads
    seq = n_ctx * rows
    share = width // n_exp
    side = math.isqrt(n_ctx)
    low, full = jnp.bfloat16, jnp.float32
    chunk = up_terms.shape[0] // n_ctx
    square = (side, side, chunk, width)
    assert n_ctx == 16 and experts == 8 and rows == 128
    return pl.pallas_call(
        functools.partial(middle_kernel, sizes, heads, experts, own_buckets),
        out_shape=[
            jax.ShapeDtypeStruct((heads, 3 * size, rows), low),
            jax.ShapeDtypeStruct(expert_out.shape, low),
            jax.ShapeDtypeStruct((share // 16, 16, width), low),
            jax.ShapeDtypeStruct((3 * size, seq), low),
            jax.ShapeDtypeStruct(table.shape, full),
            jax.ShapeDtypeStruct((rows, width), full),
            jax.ShapeDtypeStruct((16, width), full),
            jax.ShapeDtypeStruct((side, chunk, width), low),
            jax.ShapeDtypeStruct((side, chunk, width), low),
        ],
        in_specs=in_vmem(2) + any_space(3) + in_vmem(10) + in_smem(1),
        out_specs=in_vmem(1) + any_space(1) + in_vmem(7),
        scratch_shapes=[
            pltpu.VMEM(expert_back.shape, low),
            pltpu.VMEM(dgate.shape, full),
            pltpu.VMEM((heads, size, rows), low),
            pltpu.VMEM((n_ctx, size, rows), low),
            pltpu.VMEM((n_ctx, 3 * size, rows), low),
            pltpu.VMEM((n_exp, share, width), low),
            pltpu.VMEM((n_exp, share, width), low),
        ]
        + ring_space((2, chunk, width)) * 2
        + [
            pltpu.VMEM((seq, size), low),
            pltpu.VMEM((seq, size), low),
            pltpu.VMEM((size, seq), low),
            pltpu.VMEM((size, seq), low),
            pltpu.VMEM((size, seq), full),
            pltpu.VMEM((size, seq), full),
            pltpu.VMEM((BLOCK, BLOCK), full),
            pltpu.VMEM((BLOCK // 2, BLOCK // 2), full),
            pltpu.VMEM((BLOCK, BLOCK), full),
            pltpu.VMEM((BLOCK, BLOCK), full),
        ]
        + move_sems(n_exp) * 4
        + move_sems(n_ctx) * 2
        + ring_sems() * 2,
        compiler_params=remote_params(2),
        cost_estimate=cost(60_000_000_000, 100_000_000, 2_400_000),
        name="run_middle",
    )(
        expert_back, dgate, expert_out, up_terms.reshape(square), down_terms.reshape(square), info,
        g, mid, second, dense, proj, mixed, qkv, stat, table, lengths,
    )


def last_kernel(
    sizes, heads, experts, own_buckets,
    grad_ref, w_ref, x_ref, small_ref, dmid_ref, turned_ref, h_ref, bias_ref, part_ref, piece_in,
    out_ref, mid_ref, info_ref, up_in, down_in,
    in_out, block_out, head_all, small_all, piece_all, up_c, up_d, down_c, down_d,
    head_in, small_in, dqkv_ref, head_parts, small_parts, piece_parts, head_sent, small_sent,
    piece_sent, up_a, up_b, down_a, down_b, *sems,
):
    n_ctx, n_exp = sizes["ctx"], sizes["exp"]
    takers, sixteen, width = piece_in.shape
    rows = x_ref.shape[0]
    size = width // heads
    share = width // n_exp
    half = share // 2
    me = lax.axis_index("ctx")
    greet(sizes, ["exp", "ctx"])
    first = [
        Move(sizes, "exp", head_in, head_parts, sems[0:3], split=True),
        Move(sizes, "exp", small_in, small_parts, sems[3:6], split=True),
        Move(sizes, "ctx", piece_in, piece_parts, sems[6:9], split=True, takers=takers),
    ]
    second = [
        Move(sizes, "ctx", head_sent, head_all, sems[9:12], senders=heads),
        Move(sizes, "ctx", small_sent, small_all, sems[12:15]),
        Move(sizes, "ctx", piece_sent, piece_all, sems[15:18], senders=takers),
    ]
    part_rows = up_d.shape[1]
    ups = RingSum(
        False,
        lambda k, h: up_in.at[k, pl.ds(h * part_rows, part_rows)],
        (up_a, up_b, up_c, up_d),
        sems[18:21],
    )
    downs = RingSum(
        True,
        lambda k, h: down_in.at[k, pl.ds(h * part_rows, part_rows)],
        (down_a, down_b, down_c, down_d),
        sems[21:24],
    )
    start_all(first[2:])

    @pl.when(me < heads)
    def _():
        terms = dot_nn(turned_ref[...], h_ref[...]).T.astype(jnp.bfloat16)
        for e in range(n_exp):
            head_in[e] = terms[e * share : (e + 1) * share, :]

    start_all(first[:1])
    ups.start()
    downs.start()

    for part in range(3):
        for pair in range(heads // 2):
            both = jnp.concatenate(
                [
                    grad_ref[2 * pair + k, part * size : (part + 1) * size, :]
                    for k in range(2)
                ],
                axis=0,
            )
            at = part * width + 2 * size * pair
            dqkv_ref[:, at : at + 2 * size] = transposed(both)
    dh = jnp.zeros((rows, width), jnp.float32)
    for at in range(0, 3 * width, 256):
        piece = w_ref[:, :, at : at + 256].reshape(width, 256)
        dh = dh + dot_nt(dqkv_ref[:, at : at + 256], piece)
    x = x_ref[...].astype(jnp.float32)
    grad_x, grad_gain = norm_back(x, full_row(small_ref, 0, share), dh)
    in_out[...] = dmid_ref[...] + grad_x

    bias = jnp.sum(bias_ref[...], axis=1, keepdims=True)
    small_in[...] = jnp.zeros_like(small_in)
    for e in range(n_exp):
        at = slice(e * share, (e + 1) * share)
        small_in[e, 0:1, :share] = grad_gain[:, at]
        small_in[e, 1:2, :share] = part_ref[0:1, at]
        small_in[e, 2 : 2 + experts, :share] = part_ref[8 : 8 + experts, at]
        small_in[e, 2 + experts : 2 + experts + own_buckets, :] = jnp.broadcast_to(
            bias[e * own_buckets : (e + 1) * own_buckets, :], (own_buckets, 128)
        )
    start_all(first[1:2])
    ups.turn()
    downs.turn()

    first[0].wait()
    total = summed(head_parts, n_exp).astype(jnp.bfloat16)
    head_sent[:share, :] = total[:, : 2 * size]
    head_sent[share:, :] = jnp.concatenate(
        [total[:half, 2 * size :], total[half:, 2 * size :]], axis=1
    )
    start_all(second[:1])
    first[2].wait()

    @pl.when(me < takers)
    def _():
        piece_sent[...] = summed(piece_parts, n_ctx).astype(jnp.bfloat16)

    start_all(second[2:])
    first[1].wait()
    small_sent[...] = summed(small_parts, n_exp)
    start_all(second[1:2])

    slots = lax.broadcasted_iota(jnp.int32, (experts * rows // 2, rows), 0).astype(jnp.float32)
    hit = [(slots == info_ref[2 + c : 3 + c, :]).astype(jnp.bfloat16) for c in range(2)]
    both = jnp.concatenate(hit, axis=1)
    picked = dot_tn(both, out_ref[...].reshape(experts * rows // 2, width))
    tall = jnp.concatenate([info_ref[...], jnp.zeros((rows - 8, rows), jnp.float32)], axis=0).T
    mixed = mid_ref[...] + (tall[:, 0:1] * picked[:rows] + tall[:, 1:2] * picked[rows:])
    block_out[...] = mixed.astype(jnp.bfloat16)

    ups.wait()
    downs.wait()
    for m in second:
        m.wait()
    for m in first + second + [ups, downs]:
        m.wait_sent()


def run_last(
    sizes, heads, experts, own_buckets, grad_qkv, weight, x, dense, dmid, turned, h_all, bias,
    parts, pieces, returned, mid, info, up_sum, down_sum,
):
    n_ctx, n_exp = sizes["ctx"], sizes["exp"]
    rows, width = x.shape
    size = width // heads
    share = width // n_exp
    takers, sixteen, _ = pieces.shape
    side, chunk, _ = up_sum.shape
    low, full = jnp.bfloat16, jnp.float32
    assert 2 + experts + own_buckets <= 16
    return pl.pallas_call(
        functools.partial(last_kernel, sizes, heads, experts, own_buckets),
        out_shape=[
            jax.ShapeDtypeStruct((rows, width), full),
            jax.ShapeDtypeStruct((rows, width), low),
            jax.ShapeDtypeStruct((heads, share * 3 // 2, 128), low),
            jax.ShapeDtypeStruct((n_ctx, 16, 128), full),
            jax.ShapeDtypeStruct((takers, sixteen, width), low),
        ]
        + [
            jax.ShapeDtypeStruct((2, 2, chunk // 2, width), low),
            jax.ShapeDtypeStruct((2, chunk // 2, width), low),
        ]
        * 2,
        in_specs=in_vmem(15),
        out_specs=in_vmem(9),
        scratch_shapes=[
            pltpu.VMEM((n_exp, share, 3 * size), low),
            pltpu.VMEM((n_exp, 16, 128), full),
            pltpu.VMEM((rows, 3 * width), low),
            pltpu.VMEM((n_exp, share, 3 * size), low),
            pltpu.VMEM((n_exp, 16, 128), full),
            pltpu.VMEM((n_ctx, sixteen, width), low),
            pltpu.VMEM((share * 3 // 2, 128), low),
            pltpu.VMEM((16, 128), full),
            pltpu.VMEM((sixteen, width), low),
        ]
        + ring_space((chunk // 2, width))[:2] * 2
        + move_sems(n_exp) * 2
        + move_sems(n_ctx) * 4
        + ring_sems() * 2,
        compiler_params=remote_params(3),
        cost_estimate=cost(4_000_000_000, 60_000_000),
        name="run_last",
    )(
        grad_qkv, weight, x, dense, dmid, turned, h_all, bias, parts, pieces, returned, mid, info,
        up_sum, down_sum,
    )


def finish_kernel(
    sizes, experts, in_ref, block_ref, head_ref, small_ref, piece_ref, up_got, up_own, down_got,
    down_own, block_out, in_out, one_out, two_out, qkv_out, weight_out, router_out, table_out,
    up_out, down_out,
):
    heads = head_ref.shape[0]
    share, width = weight_out.shape
    size = width // heads
    half = share // 2
    own_buckets = table_out.shape[0]
    block_out[0] = block_ref[...]
    in_out[0] = in_ref[...]
    for h in range(heads):
        got = head_ref[h].astype(jnp.float32)
        at = h * size
        qkv_out[:, at : at + size] = got[:share, :size]
        qkv_out[:, width + at : width + at + size] = got[:share, size:]
        qkv_out[:half, 2 * width + at : 2 * width + at + size] = got[share:, :size]
        qkv_out[half:, 2 * width + at : 2 * width + at + size] = got[share:, size:]
    takers, sixteen, _ = piece_ref.shape
    for t in range(takers):
        weight_out[t * sixteen : (t + 1) * sixteen, :] = piece_ref[t].astype(jnp.float32)
    sums = summed(small_ref, sizes["ctx"])
    one_out[...] = sums[0:1, :share]
    two_out[...] = sums[1:2, :share]
    router_out[...] = sums[2 : 2 + experts, :share]
    begin = 2 + experts
    table_out[...] = jnp.concatenate(
        [small_ref[h, begin : begin + own_buckets, 0:1] for h in range(heads)], axis=1
    )
    for got, own, out in ((up_got, up_own, up_out), (down_got, down_own, down_out)):
        rows = own.shape[1]
        for h in range(2):
            out[0, h * rows : (h + 1) * rows, :] = sum(
                p.astype(jnp.float32) for p in (own[h], got[0, h], got[1, h])
            )


def finish(sizes, heads, experts, own_buckets, parts):
    rows, width = parts[0].shape
    share = width // sizes["exp"]
    chunk = 2 * parts[-1].shape[1]
    low, full = jnp.bfloat16, jnp.float32
    return pl.pallas_call(
        functools.partial(finish_kernel, sizes, experts),
        out_shape=[
            jax.ShapeDtypeStruct((1, rows, width), low),
            jax.ShapeDtypeStruct((1, rows, width), full),
            jax.ShapeDtypeStruct((1, share), full),
            jax.ShapeDtypeStruct((1, share), full),
            jax.ShapeDtypeStruct((share, 3 * width), full),
            jax.ShapeDtypeStruct((share, width), full),
            jax.ShapeDtypeStruct((experts, share), full),
            jax.ShapeDtypeStruct((own_buckets, heads), full),
            jax.ShapeDtypeStruct((1, chunk, width), full),
            jax.ShapeDtypeStruct((1, chunk, width), full),
        ],
        in_specs=in_vmem(len(parts)),
        out_specs=in_vmem(10),
        compiler_params=pltpu.CompilerParams(vmem_limit_bytes=VMEM_BYTES),
        cost_estimate=cost(0, 8_000_000),
        name="finish",
    )(*parts)


def local(
    sizes,
    block_in,
    attn_gain,
    moe_gain,
    query_key_value_weight,
    output_matrix,
    routing_weight,
    bias_table,
    up_weight,
    down_weight,
    routes,
    doc_lengths,
    cotangent,
):
    low, full = jnp.bfloat16, jnp.float32
    n_ctx, n_exp = sizes["ctx"], sizes["exp"]
    rows, width = block_in.shape[1:]
    share = width // n_exp
    own_buckets, heads = bias_table.shape
    experts = routing_weight.shape[1]
    g_low = cotangent[0]

    expert_weights = lax.all_gather(
        jnp.concatenate([up_weight, down_weight], axis=0), "ctx", axis=1, tiled=True
    )

    lanes = lambda a: jnp.pad(a, ((0, 0), (0, 128 - a.shape[1])))
    small = jnp.concatenate(
        [lanes(attn_gain[None]), lanes(moe_gain[None]), lanes(bias_table), lanes(routing_weight.T)],
        axis=0,
    )
    small = jnp.pad(small, ((0, -small.shape[0] % 16), (0, 0)))
    capacity = min(rows, 4 * rows // experts)
    piece = (experts, capacity, width)
    lengths = doc_lengths[0]
    (
        qkv_full,
        dense,
        proj_full,
        h_first,
        x_mid,
        h_second,
        info,
        mixed,
        qkv_head,
        stat,
        table_head,
        expert_rows,
        g_rows,
        gate_rows,
    ) = run_front(
        sizes,
        heads,
        experts,
        own_buckets,
        query_key_value_weight,
        small,
        output_matrix,
        block_in[0],
        g_low,
        routes[0].T,
        lengths,
    )
    h_all = lax.all_gather(h_first, "ctx", axis=0, tiled=True)
    expert_out, expert_back, dgate, up_terms, down_terms = run_expert(
        expert_rows.reshape(experts * capacity, width),
        g_rows.reshape(experts * capacity, width),
        gate_rows,
        expert_weights,
    )
    grad_qkv_t, returned, pieces, grad_head, bias_rows, grad_mid, parts, up_sum, down_sum = (
        run_middle(
            sizes,
            heads,
            experts,
            own_buckets,
            expert_back.reshape(piece),
            dgate,
            expert_out.reshape(piece),
            up_terms,
            down_terms,
            info,
            g_low,
            x_mid,
            h_second,
            dense,
            proj_full,
            mixed,
            qkv_head,
            stat,
            table_head,
            lengths,
        )
    )
    last = run_last(
        sizes,
        heads,
        experts,
        own_buckets,
        grad_qkv_t,
        qkv_full,
        block_in[0],
        dense,
        grad_mid,
        grad_head,
        h_all,
        bias_rows,
        parts,
        pieces,
        returned,
        x_mid,
        info,
        up_sum,
        down_sum,
    )
    out = finish(sizes, heads, experts, own_buckets, last)
    block_out, grad_in, one, two, qkv, proj, router, *rest = out
    return (block_out, grad_in, one[0], two[0], qkv, proj, router.T, *rest)


def solution(mesh):
    sizes = {name: mesh.shape[name] for name in ("ctx", "exp")}
    tokens = P("exp", "ctx", None)
    row_split = P("exp", None)
    return jax.shard_map(
        functools.partial(local, sizes),
        mesh=mesh,
        in_specs=(
            tokens,
            P("exp"),
            P("exp"),
            row_split,
            row_split,
            row_split,
            row_split,
            tokens,
            tokens,
            tokens,
            row_split,
            tokens,
        ),
        out_specs=(
            tokens,
            tokens,
            P("exp"),
            P("exp"),
            row_split,
            row_split,
            row_split,
            row_split,
            tokens,
            tokens,
        ),
        check_vma=False,
    )
```

```python
import functools
import math

import jax
import jax.numpy as jnp
import numpy as np
from jax import lax
from jax.experimental import pallas as pl
from jax.experimental.pallas import tpu as pltpu
from jax.sharding import PartitionSpec as P

MAXD = 128
BLOCK = 256
MESH = pl.DeviceIdType.MESH
VMEM_BYTES = 60 * 1024 * 1024

epsilon = 1e-06
masked_score = -1e30


def bucket_thresholds(buckets, reach_len):
    exact_part = buckets // 2
    spread_part = buckets - exact_part
    return [
        int(math.ceil(exact_part * (reach_len / exact_part) ** (level / spread_part)))
        for level in range(1, spread_part)
    ]


def guarded(tests, action):
    tests = [t for t in tests if t is not None]
    if not tests:
        action()
    else:
        pl.when(functools.reduce(jnp.logical_and, tests))(action)


def greet(sizes, axes):
    barrier = pltpu.get_barrier_semaphore()
    total = 0
    for a in axes:
        me = lax.axis_index(a)
        for r in range(1, sizes[a]):
            peer = lax.rem(me + r, sizes[a])
            pl.semaphore_signal(barrier, inc=1, device_id={a: peer}, device_id_type=MESH)
            total += 1
    pl.semaphore_wait(barrier, total)


class Move:
    def __init__(self, sizes, axis, src, out, sems, split=False, senders=None, takers=None):
        self.n = sizes[axis]
        self.axis, self.src, self.out, self.split = axis, src, out, split
        self.send_sem, self.recv_sem, self.own_sem = sems
        self.senders, self.takers = senders or self.n, takers or self.n
        self.me = lax.axis_index(axis)

    def sends(self, device):
        return device < self.senders if self.senders < self.n else None

    def takes(self, device):
        return device < self.takers if self.takers < self.n else None

    def copy(self, r, peer, slot, piece):
        return pltpu.make_async_remote_copy(
            src_ref=self.src.at[piece] if self.split else self.src,
            dst_ref=self.out.at[slot],
            send_sem=self.send_sem.at[r],
            recv_sem=self.recv_sem.at[r],
            device_id={self.axis: peer},
            device_id_type=MESH,
        )

    def to(self, r):
        return lax.rem(self.me + r, self.n)

    def start(self, r):
        dst = self.to(r)
        guarded(
            [self.sends(self.me), self.takes(dst)],
            lambda: self.copy(r, dst, self.me, dst).start(),
        )

    def own(self):
        src = self.src.at[self.me] if self.split else self.src
        return pltpu.make_async_copy(src, self.out.at[self.me], self.own_sem)

    def start_own(self):
        guarded([self.sends(self.me), self.takes(self.me)], lambda: self.own().start())

    def wait(self):
        guarded([self.sends(self.me), self.takes(self.me)], lambda: self.own().wait())
        for r in range(1, self.n):
            src = lax.rem(self.me + self.n - r, self.n)
            guarded(
                [self.sends(src), self.takes(self.me)],
                lambda: self.copy(r, src, src, 0).wait_recv(),
            )

    def wait_sent(self):
        for r in range(1, self.n):
            dst = self.to(r)
            guarded(
                [self.sends(self.me), self.takes(dst)],
                lambda: self.copy(r, dst, self.me, dst).wait_send(),
            )


def start_all(moves):
    for r in range(1, max(m.n for m in moves)):
        for m in moves:
            if r < m.n:
                m.start(r)
    for m in moves:
        m.start_own()


class PairGather:
    def __init__(self, sizes, src, out, sems):
        self.n = sizes["exp"]
        self.src, self.out = src, out
        self.send_sem, self.recv_sem, self.own_sem = sems
        self.me = lax.axis_index("exp")
        core = lax.rem(self.me, 2)
        self.mate = self.me + 1 - 2 * core

    def copy(self, src, slot, k, peer):
        return pltpu.make_async_remote_copy(
            src_ref=src,
            dst_ref=self.out.at[slot],
            send_sem=self.send_sem.at[k],
            recv_sem=self.recv_sem.at[k],
            device_id={"exp": peer},
            device_id_type=MESH,
        )

    def own(self):
        return pltpu.make_async_copy(self.src, self.out.at[self.me], self.own_sem)

    def chips(self):
        return range(1, self.n // 2)

    def start(self):
        for r in self.chips():
            self.copy(self.src, self.me, r, lax.rem(self.me + 2 * r, self.n)).start()
        self.copy(self.src, self.me, 0, self.mate).start()
        self.own().start()

    def forward(self, r):
        slot = lax.rem(self.me + self.n - 2 * r, self.n)
        return self.copy(self.out.at[slot], slot, self.n // 2 + r, self.mate)

    def pass_on(self):
        for r in self.chips():
            slot = lax.rem(self.me + self.n - 2 * r, self.n)
            self.copy(self.src, slot, r, slot).wait_recv()
            self.forward(r).start()

    def finish(self):
        for r in self.chips():
            slot = lax.rem(self.mate + self.n - 2 * r, self.n)
            self.copy(self.src, slot, self.n // 2 + r, self.mate).wait_recv()
            self.forward(r).wait_send()
            self.copy(self.src, self.me, r, lax.rem(self.me + 2 * r, self.n)).wait_send()
        self.copy(self.src, self.mate, 0, self.mate).wait_recv()
        self.copy(self.src, self.me, 0, self.mate).wait_send()
        self.own().wait()


def move_sems(count):
    return [
        pltpu.SemaphoreType.DMA((count,)),
        pltpu.SemaphoreType.DMA((count,)),
        pltpu.SemaphoreType.DMA,
    ]


def any_space(count):
    return [pl.BlockSpec(memory_space=pl.ANY)] * count


def in_vmem(count):
    return [pl.BlockSpec(memory_space=pltpu.VMEM)] * count


def in_smem(count):
    return [pl.BlockSpec(memory_space=pltpu.SMEM)] * count


def remote_params(number, limit=VMEM_BYTES):
    return pltpu.CompilerParams(
        collective_id=number, has_side_effects=True, vmem_limit_bytes=limit
    )


def cost(flops, moved, special=0):
    return pl.CostEstimate(flops=flops, bytes_accessed=moved, transcendentals=special)


def dot_nt(left, right):
    return lax.dot_general(
        left, right, (((1,), (1,)), ((), ())), preferred_element_type=jnp.float32
    )


def dot_tn(left, right):
    return lax.dot_general(
        left, right, (((0,), (0,)), ((), ())), preferred_element_type=jnp.float32
    )


def dot_nn(left, right):
    return jnp.dot(left, right, preferred_element_type=jnp.float32)


def near_buckets(buckets, offset, rows, cols):
    key = lax.broadcasted_iota(jnp.int32, (rows, cols), 0)
    query = lax.broadcasted_iota(jnp.int32, (rows, cols), 1)
    distance = jnp.clip(query - key + offset, 0, MAXD)
    bucket = jnp.minimum(distance, buckets // 2)
    for level in bucket_thresholds(buckets, MAXD):
        bucket = bucket + (distance >= level).astype(jnp.int32)
    return bucket


def near_bias(table_ref, buckets, offset, rows, cols):
    bucket = near_buckets(buckets, offset, rows, cols)
    last = table_ref[buckets - 1 : buckets, 0:1]
    bias = jnp.zeros((rows, cols), jnp.float32)
    for b in range(buckets - 1):
        bias = jnp.where(bucket == b, table_ref[b : b + 1, 0:1] - last, bias)
    return bias


def first_keys(lengths_ref, start):
    query = start + lax.broadcasted_iota(jnp.int32, (1, BLOCK), 1)
    first = jnp.zeros((1, BLOCK), jnp.int32)
    bound = jnp.int32(0)
    for d in range(3):
        bound = bound + lengths_ref[d]
        first = jnp.where(query >= bound, bound, first)
    return first


def block_scores(i, j, blocks, qt, k, diag_bias, side_bias, first):
    s = dot_nn(k, qt)
    half = BLOCK // 2
    if j == i:
        s = s + diag_bias
    elif j == i - 1:
        lower = jnp.concatenate([s[half:, :half] + side_bias, s[half:, half:]], axis=1)
        s = jnp.concatenate([s[:half], lower], axis=0)
    if j == i or j == 0 or i == blocks - 1:
        key = lax.broadcasted_iota(jnp.int32, (BLOCK, BLOCK), 0)
        keep = key + j * BLOCK >= first
        if j == i:
            keep = keep & (key <= lax.broadcasted_iota(jnp.int32, (BLOCK, BLOCK), 1))
        s = jnp.where(keep, s, masked_score)
    return s


def transposed(piece):
    return piece.astype(jnp.float32).T.astype(jnp.bfloat16)


def scaled_queries(qkv_ref, i, size):
    scale = 1.0 / math.sqrt(size)
    both = jnp.concatenate([qkv_ref[2 * i, :size, :], qkv_ref[2 * i + 1, :size, :]], axis=1)
    return (both * scale).astype(jnp.bfloat16)


def block_of(j):
    return slice(j * BLOCK, (j + 1) * BLOCK)


def bucket_values(small_ref, own_buckets, heads):
    head = jnp.minimum(lax.axis_index("ctx"), heads - 1)
    rows = jnp.concatenate(
        [small_ref[e, 2 : 2 + own_buckets, :] for e in range(small_ref.shape[0])], axis=0
    ).astype(jnp.float32)
    lane = lax.broadcasted_iota(jnp.int32, rows.shape, 1)
    value = jnp.sum(jnp.where(lane == head, rows, 0.0), axis=1, keepdims=True)
    return jnp.broadcast_to(value, rows.shape)


def full_row(small_ref, row, share):
    pieces = [small_ref[e, row : row + 1, :share] for e in range(small_ref.shape[0])]
    return jnp.concatenate(pieces, axis=1).astype(jnp.float32)


def norm_rows(x, gain):
    scale = lax.rsqrt(jnp.mean(x * x, axis=-1, keepdims=True) + epsilon)
    return (x * scale * gain).astype(jnp.bfloat16)


def columns_to_rows(column, groups):
    cap = column.shape[0] // groups
    lane = lax.broadcasted_iota(jnp.int32, (cap, 128), 1)
    spread = jnp.zeros((cap, 128), jnp.float32)
    for s in range(groups):
        spread = jnp.where(lane == s, column[s * cap : (s + 1) * cap, :], spread)
    return jnp.concatenate([spread] * (128 // cap), axis=0).T


def front_kernel(
    sizes,
    heads,
    experts,
    own_buckets,
    w_in,
    small_in,
    proj_in,
    x_ref,
    g_ref,
    route_ref,
    lengths_ref,
    w_ref,
    small_ref,
    proj_ref,
    h_ref,
    mid_ref,
    second_ref,
    info_ref,
    mixed_ref,
    qkv_ref,
    stat_ref,
    table_ref,
    rows_out,
    g_out,
    gate_out,
    qkv_sent,
    sent_ref,
    k_ref,
    vt_ref,
    diag_ref,
    side_ref,
    rows_sent,
    g_sent,
    gate_sent,
    *sems,
):
    n_exp = sizes["exp"]
    parts, three, rows = qkv_ref.shape
    size = three // 3
    width = heads * size
    share = width // n_exp
    blocks = parts * rows // BLOCK
    half = BLOCK // 2
    buckets = own_buckets * n_exp
    cap = rows_sent.shape[1]
    greet(sizes, ["exp", "ctx"])
    weight = PairGather(sizes, w_in, w_ref, sems[0:3])
    little = Move(sizes, "exp", small_in, small_ref, sems[3:6])
    proj = PairGather(sizes, proj_in, proj_ref, sems[6:9])
    grads = Move(sizes, "exp", g_sent, g_out, sems[9:12], split=True)
    arrive = Move(sizes, "ctx", qkv_sent, qkv_ref, sems[12:15], split=True, takers=heads)
    back = Move(sizes, "ctx", sent_ref, mixed_ref, sems[15:18], split=True, senders=heads)
    hidden = Move(sizes, "exp", rows_sent, rows_out, sems[18:21], split=True)
    gating = Move(sizes, "exp", gate_sent, gate_out, sems[21:24], split=True)
    start_all([little])
    weight.start()

    expert = lax.broadcasted_iota(jnp.int32, (experts, rows), 0)
    chosen = [(expert == route_ref[c : c + 1, :]).astype(jnp.float32) for c in range(2)]
    earlier = lax.broadcasted_iota(jnp.int32, (rows, rows), 0) < lax.broadcasted_iota(
        jnp.int32, (rows, rows), 1
    )
    count = dot_nn((chosen[0] + chosen[1]).astype(jnp.bfloat16), earlier.astype(jnp.bfloat16))
    place = count + (expert * cap).astype(jnp.float32)
    slot = [jnp.sum(chosen[c] * place, axis=0, keepdims=True) for c in range(2)]
    slots = lax.broadcasted_iota(jnp.int32, (experts * cap, rows), 0).astype(jnp.float32)
    hit = [slots == slot[c] for c in range(2)]
    either = (hit[0] | hit[1]).astype(jnp.bfloat16)
    send_g = dot_nn(either, g_ref[...]).astype(jnp.bfloat16)
    for e in range(experts):
        g_sent[e] = send_g[e * cap : (e + 1) * cap, :]

    little.wait()
    table_ref[...] = bucket_values(small_ref, own_buckets, heads)
    x = x_ref[...].astype(jnp.float32)
    h = norm_rows(x, full_row(small_ref, 0, share))
    h_ref[...] = h
    diag_ref[...] = near_bias(table_ref, buckets, 0, BLOCK, BLOCK)
    side_ref[...] = near_bias(table_ref, buckets, half, half, half)
    weight.pass_on()
    proj.start()
    weight.finish()
    for at in range(0, 3 * width, 2 * rows):
        piece = w_ref[:, :, at : at + 2 * rows].reshape(width, 2 * rows)
        turned = dot_nn(h, piece).T.astype(jnp.bfloat16)
        for begin in range(0, 2 * rows, size):
            part, head = divmod((at + begin) // size, heads)
            qkv_sent[head, part * size : (part + 1) * size, :] = turned[begin : begin + size, :]
    start_all([arrive])
    proj.pass_on()
    start_all([grads])
    arrive.wait()

    @pl.when(lax.axis_index("ctx") < heads)
    def _():
        for c in range(parts):
            at = slice(c * rows, (c + 1) * rows)
            k_ref[at, :] = transposed(qkv_ref[c, size : 2 * size, :])
            vt_ref[:, at] = qkv_ref[c, 2 * size :, :]
        for i in range(blocks):
            qt = scaled_queries(qkv_ref, i, size)
            first = first_keys(lengths_ref, i * BLOCK)
            scores = []
            top = None
            for j in range(i + 1):
                s = block_scores(
                    i, j, blocks, qt, k_ref[block_of(j), :], diag_ref[...], side_ref[...], first
                )
                scores.append(s)
                here = jnp.max(s, axis=0, keepdims=True)
                top = here if top is None else jnp.maximum(top, here)
            total = jnp.zeros((1, BLOCK), jnp.float32)
            for j in range(i + 1):
                scores[j] = jnp.exp(scores[j] - top)
                total = total + jnp.sum(scores[j], axis=0, keepdims=True)
            inverse = 1.0 / total
            mixed = jnp.zeros((size, BLOCK), jnp.float32)
            for j in range(i + 1):
                probs = (scores[j] * inverse).astype(jnp.bfloat16)
                mixed = mixed + dot_nn(vt_ref[:, block_of(j)], probs)
            mixed = mixed.astype(jnp.bfloat16)
            sent_ref[2 * i] = mixed[:, :half]
            sent_ref[2 * i + 1] = mixed[:, half:]
            stat_ref[i : i + 1, :] = top + jnp.log(total)

    start_all([back])
    proj.finish()
    back.wait()

    attended = transposed(mixed_ref[...].reshape(width, rows))
    mid = x + dot_nn(attended, proj_ref[...].reshape(width, width))
    mid_ref[...] = mid
    second = norm_rows(mid, full_row(small_ref, 1, share))
    second_ref[...] = second
    send = dot_nn(either, second).astype(jnp.bfloat16)
    for e in range(experts):
        rows_sent[e] = send[e * cap : (e + 1) * cap, :]
    start_all([hidden])
    begin = 2 + own_buckets
    router = jnp.concatenate(
        [small_ref[e, begin : begin + experts, :share] for e in range(n_exp)], axis=1
    )
    z = dot_nt(router, second)
    picked = [jnp.sum(chosen[c] * z, axis=0, keepdims=True) for c in range(2)]
    top = jnp.maximum(picked[0], picked[1])
    raised = [jnp.exp(p - top) for p in picked]
    gates = [r / (raised[0] + raised[1]) for r in raised]
    column = sum(
        jnp.sum(jnp.where(hit[c], gates[c], 0.0), axis=1, keepdims=True) for c in range(2)
    )
    turned = columns_to_rows(column, experts)
    for e in range(experts):
        gate_sent[e] = jnp.broadcast_to(turned[e : e + 1, :], (8, 128))
    start_all([gating])
    info_ref[...] = jnp.concatenate(
        gates + slot + [route_ref[c : c + 1, :].astype(jnp.float32) for c in range(2)] + slot,
        axis=0,
    )
    grads.wait()
    gating.wait()
    hidden.wait()
    for m in (little, grads, arrive, back, hidden, gating):
        m.wait_sent()


def run_front(sizes, heads, experts, own_buckets, weight, small, proj, x, g, route_t, lengths):
    n_ctx, n_exp = sizes["ctx"], sizes["exp"]
    rows, width = x.shape
    size = width // heads
    seq = n_ctx * rows
    cap = min(rows, 4 * rows // experts)
    low, full = jnp.bfloat16, jnp.float32
    assert 2 * rows == BLOCK and rows == 128 and 3 * width % (2 * rows) == 0
    return pl.pallas_call(
        functools.partial(front_kernel, sizes, heads, experts, own_buckets),
        out_shape=[
            jax.ShapeDtypeStruct((n_exp,) + weight.shape, low),
            jax.ShapeDtypeStruct((n_exp,) + small.shape, low),
            jax.ShapeDtypeStruct((n_exp,) + proj.shape, low),
            jax.ShapeDtypeStruct((rows, width), low),
            jax.ShapeDtypeStruct((rows, width), full),
            jax.ShapeDtypeStruct((rows, width), low),
            jax.ShapeDtypeStruct((8, rows), full),
            jax.ShapeDtypeStruct((heads, size, rows), low),
            jax.ShapeDtypeStruct((n_ctx, 3 * size, rows), low),
            jax.ShapeDtypeStruct((seq // BLOCK, BLOCK), full),
            jax.ShapeDtypeStruct((own_buckets * n_exp, 128), full),
            jax.ShapeDtypeStruct((experts, cap, width), low),
            jax.ShapeDtypeStruct((experts, cap, width), low),
            jax.ShapeDtypeStruct((experts, 8, 128), full),
        ],
        in_specs=in_vmem(6) + in_smem(1),
        out_specs=in_vmem(14),
        scratch_shapes=[
            pltpu.VMEM((heads, 3 * size, rows), low),
            pltpu.VMEM((n_ctx, size, rows), low),
            pltpu.VMEM((seq, size), low),
            pltpu.VMEM((size, seq), low),
            pltpu.VMEM((BLOCK, BLOCK), full),
            pltpu.VMEM((BLOCK // 2, BLOCK // 2), full),
            pltpu.VMEM((experts, cap, width), low),
            pltpu.VMEM((experts, cap, width), low),
            pltpu.VMEM((experts, 8, 128), full),
        ]
        + move_sems(n_exp) * 4
        + move_sems(n_ctx) * 2
        + move_sems(n_exp) * 2,
        compiler_params=remote_params(1),
        cost_estimate=cost(60_000_000_000, 100_000_000, 2_400_000),
        name="run_front",
    )(weight, small, proj, x, g, route_t, lengths)


def expert_kernel(
    rows_ref, g_ref, gate_ref, up_ref, down_ref, out_ref, back_ref, dgate_ref, gup_ref, gdown_ref,
    dy_ref, sum_out, sum_back,
):
    step = pl.program_id(0)
    count, width = rows_ref.shape
    sources = gate_ref.shape[0]
    cap = count // sources

    @pl.when(step == 0)
    def _():
        lanes = jnp.concatenate([gate_ref[s, 0:1, :] for s in range(sources)], axis=0)
        columns = lanes.T
        for s in range(sources):
            at = slice(s * cap, (s + 1) * cap)
            gate = columns[:cap, s : s + 1]
            dy_ref[at, :] = (gate * g_ref[at, :].astype(jnp.float32)).astype(jnp.bfloat16)
        sum_out[...] = jnp.zeros_like(sum_out)
        sum_back[...] = jnp.zeros_like(sum_back)

    rows, dy = rows_ref[...], dy_ref[...]
    up, down = up_ref[0], down_ref[0]
    x = dot_nt(rows, up)
    c, a = math.sqrt(2.0 / math.pi), 0.044715
    square = x * x
    t = jnp.tanh(c * x * (1.0 + a * square))
    half = 0.5 * (1.0 + t)
    hidden = (x * half).astype(jnp.bfloat16)
    slope = half + 0.5 * x * (1.0 - t * t) * (c * (1.0 + 3.0 * a * square))
    dpre = (dot_nt(dy, down) * slope).astype(jnp.bfloat16)
    gup_ref[...] = dot_tn(dpre, rows).astype(jnp.bfloat16)
    gdown_ref[...] = dot_tn(hidden, dy).astype(jnp.bfloat16)
    sum_out[...] += dot_nn(hidden, down)
    sum_back[...] += dot_nn(dpre, up)

    @pl.when(step == pl.num_programs(0) - 1)
    def _():
        back_ref[...] = sum_back[...].astype(jnp.bfloat16)
        out = sum_out[...].astype(jnp.bfloat16)
        out_ref[...] = out
        dgate = jnp.sum(out.astype(jnp.float32) * g_ref[...].astype(jnp.float32), axis=1, keepdims=True)
        lane = lax.broadcasted_iota(jnp.int32, (cap, 128), 1)
        columns = jnp.zeros((cap, 128), jnp.float32)
        for s in range(sources):
            columns = jnp.where(lane == s, dgate[s * cap : (s + 1) * cap, :], columns)
        turned = jnp.concatenate([columns] * (128 // cap), axis=0).T
        for s in range(sources):
            dgate_ref[s] = jnp.broadcast_to(turned[s : s + 1, :], (8, 128))


def run_expert(rows, g, gates, weights):
    count, width = rows.shape
    hidden = weights.shape[1]
    tile = 768
    low, full = jnp.bfloat16, jnp.float32
    whole = lambda shape: pl.BlockSpec(shape, lambda f: (0,) * len(shape))
    return pl.pallas_call(
        expert_kernel,
        grid=(hidden // tile,),
        out_shape=[
            jax.ShapeDtypeStruct((count, width), low),
            jax.ShapeDtypeStruct((count, width), low),
            jax.ShapeDtypeStruct(gates.shape, full),
            jax.ShapeDtypeStruct((hidden, width), low),
            jax.ShapeDtypeStruct((hidden, width), low),
        ],
        in_specs=[
            whole((count, width)),
            whole((count, width)),
            whole(gates.shape),
            pl.BlockSpec((1, tile, width), lambda f: (0, f, 0)),
            pl.BlockSpec((1, tile, width), lambda f: (1, f, 0)),
        ],
        out_specs=[
            whole((count, width)),
            whole((count, width)),
            whole(gates.shape),
            pl.BlockSpec((tile, width), lambda f: (f, 0)),
            pl.BlockSpec((tile, width), lambda f: (f, 0)),
        ],
        scratch_shapes=[
            pltpu.VMEM((count, width), low),
            pltpu.VMEM((count, width), full),
            pltpu.VMEM((count, width), full),
        ],
        compiler_params=pltpu.CompilerParams(vmem_limit_bytes=VMEM_BYTES),
        cost_estimate=cost(14_500_000_000, 24_000_000, 1_600_000),
        name="run_expert",
    )(rows, g, gates, weights, weights)


class RingSum:
    def __init__(self, along_major, view, bufs, sems):
        place = lax.axis_index("ctx")
        major, minor = lax.div(place, 4), lax.rem(place, 4)
        self.me = major if along_major else minor
        self.device = (lambda k: k * 4 + minor) if along_major else (lambda k: major * 4 + k)
        self.plus, self.minus = lax.rem(self.me + 1, 4), lax.rem(self.me + 3, 4)
        self.far = lax.rem(self.me + 2, 4)
        self.view = view
        self.step, self.added, self.got, self.own = bufs
        self.send_sem, self.recv_sem, self.own_sem = sems

    def copy(self, k):
        src, dst, peer = (
            (lambda: self.view(self.far, 0), self.step.at[0], self.plus),
            (lambda: self.view(self.far, 1), self.step.at[1], self.minus),
            (lambda: self.view(self.plus, 1), self.got.at[0, 1], self.plus),
            (lambda: self.view(self.minus, 0), self.got.at[1, 0], self.minus),
            (lambda: self.added.at[0], self.got.at[0, 0], self.plus),
            (lambda: self.added.at[1], self.got.at[1, 1], self.minus),
        )[k]
        return pltpu.make_async_remote_copy(
            src_ref=src(),
            dst_ref=dst,
            send_sem=self.send_sem.at[k],
            recv_sem=self.recv_sem.at[k],
            device_id={"ctx": self.device(peer)},
            device_id_type=MESH,
        )

    def local(self, k):
        src, dst = (
            (self.view(self.plus, 0), self.added.at[0]),
            (self.view(self.minus, 1), self.added.at[1]),
            (self.view(self.me, 0), self.own.at[0]),
            (self.view(self.me, 1), self.own.at[1]),
        )[k]
        return pltpu.make_async_copy(src, dst, self.own_sem.at[k])

    def start(self):
        for k in range(4):
            self.copy(k).start()
        for k in range(4):
            self.local(k).start()

    def turn(self):
        for k in range(2):
            self.copy(k).wait_recv()
            self.local(k).wait()
            total = self.added[k].astype(jnp.float32) + self.step[k].astype(jnp.float32)
            self.added[k] = total.astype(jnp.bfloat16)
            self.copy(4 + k).start()

    def wait(self):
        for k in range(2, 4):
            self.local(k).wait()
        for k in range(2, 6):
            self.copy(k).wait_recv()

    def half(self, h, *at):
        parts = (self.own[(h,) + at], self.got[(0, h) + at], self.got[(1, h) + at])
        return sum(p.astype(jnp.float32) for p in parts)

    def wait_sent(self):
        for k in range(6):
            self.copy(k).wait_send()


def ring_space(shape):
    low = jnp.bfloat16
    return [
        pltpu.VMEM((2,) + shape, low),
        pltpu.VMEM((2,) + shape, low),
        pltpu.VMEM((2, 2) + shape, low),
        pltpu.VMEM((2,) + shape, low),
    ]


def ring_sems():
    return [pltpu.SemaphoreType.DMA((6,)), pltpu.SemaphoreType.DMA((6,)), pltpu.SemaphoreType.DMA((4,))]


def norm_back(x, gain, grad):
    scale = lax.rsqrt(jnp.mean(x * x, axis=-1, keepdims=True) + epsilon)
    scaled = grad * gain
    inner = jnp.mean(scaled * x, axis=-1, keepdims=True)
    grad_x = scale * scaled - x * (scale * scale * scale) * inner
    return grad_x, jnp.sum(grad * x * scale, axis=0, keepdims=True)


def summed(ref, count):
    total = ref[0].astype(jnp.float32)
    for s in range(1, count):
        total = total + ref[s].astype(jnp.float32)
    return total


def middle_kernel(
    sizes,
    heads,
    experts,
    own_buckets,
    back_in,
    dgate_in,
    out_in,
    up_in,
    down_in,
    info_ref,
    g_ref,
    mid_ref,
    second_ref,
    small_ref,
    proj_ref,
    mixed_ref,
    qkv_ref,
    stat_ref,
    table_ref,
    lengths_ref,
    grad_out,
    out_out,
    piece_ref,
    grad_ref,
    bias_ref,
    dmid_ref,
    part_ref,
    up_sum,
    down_sum,
    back_got,
    dgate_got,
    do_sent,
    do_ref,
    sent_ref,
    terms_sent,
    terms_got,
    up_a,
    up_b,
    up_c,
    up_d,
    down_a,
    down_b,
    down_c,
    down_d,
    k_ref,
    v_ref,
    kt_ref,
    dq_ref,
    dk_ref,
    dv_ref,
    diag_ref,
    side_ref,
    diag_sum,
    side_sum,
    *sems,
):
    n_exp = sizes["exp"]
    parts, three, rows = qkv_ref.shape
    size = three // 3
    width = heads * size
    share = width // n_exp
    blocks = parts * rows // BLOCK
    half = BLOCK // 2
    buckets = own_buckets * n_exp
    cap = back_got.shape[1]
    side = math.isqrt(parts)
    scale = 1.0 / math.sqrt(size)
    greet(sizes, ["exp", "ctx"])
    returned = Move(sizes, "exp", back_in, back_got, sems[0:3], split=True)
    gating = Move(sizes, "exp", dgate_in, dgate_got, sems[3:6], split=True)
    outs = Move(sizes, "exp", out_in, out_out, sems[6:9], split=True)
    terms = Move(sizes, "exp", terms_sent, terms_got, sems[9:12], split=True)
    arrive = Move(sizes, "ctx", do_sent, do_ref, sems[12:15], split=True, takers=heads)
    back = Move(sizes, "ctx", sent_ref, grad_out, sems[15:18], split=True, senders=heads)
    ups = RingSum(
        True, lambda k, h: up_in.at[k, pl.ds(2 * h, 2)], (up_a, up_b, up_c, up_d), sems[18:21]
    )
    downs = RingSum(
        True,
        lambda k, h: down_in.at[k, pl.ds(2 * h, 2)],
        (down_a, down_b, down_c, down_d),
        sems[21:24],
    )
    start_all([gating, returned])
    ups.start()
    downs.start()
    is_head = lax.axis_index("ctx") < heads

    @pl.when(is_head)
    def _():
        diag_ref[...] = near_bias(table_ref, buckets, 0, BLOCK, BLOCK)
        side_ref[...] = near_bias(table_ref, buckets, half, half, half)
        diag_sum[...] = jnp.zeros_like(diag_sum)
        side_sum[...] = jnp.zeros_like(side_sum)
        dk_ref[...] = jnp.zeros_like(dk_ref)
        dv_ref[...] = jnp.zeros_like(dv_ref)
        for c in range(parts):
            at = slice(c * rows, (c + 1) * rows)
            kt_ref[:, at] = qkv_ref[c, size : 2 * size, :]
            k_ref[at, :] = transposed(qkv_ref[c, size : 2 * size, :])
            v_ref[at, :] = transposed(qkv_ref[c, 2 * size :, :])

    gates = [info_ref[c : c + 1, :] for c in range(2)]
    slots = lax.broadcasted_iota(jnp.int32, (experts * cap, rows), 0).astype(jnp.float32)
    hit = [slots == info_ref[2 + c : 3 + c, :] for c in range(2)]
    expert = lax.broadcasted_iota(jnp.int32, (experts, rows), 0).astype(jnp.float32)
    chosen = [(expert == info_ref[4 + c : 5 + c, :]).astype(jnp.float32) for c in range(2)]
    begin = 2 + own_buckets
    router = jnp.concatenate(
        [small_ref[e, begin : begin + experts, :share] for e in range(n_exp)], axis=1
    )
    either = (hit[0] | hit[1]).astype(jnp.bfloat16)

    gating.wait()
    turned = jnp.concatenate([dgate_got[e, 0:1, :] for e in range(experts)], axis=0).T
    column = jnp.concatenate([turned[:cap, e : e + 1] for e in range(experts)], axis=0)
    dgate = [jnp.sum(jnp.where(hit[c], column, 0.0), axis=0, keepdims=True) for c in range(2)]
    inner = gates[0] * dgate[0] + gates[1] * dgate[1]
    dz = sum(chosen[c] * (gates[c] * (dgate[c] - inner)) for c in range(2))
    dz_low = dz.astype(jnp.bfloat16)
    dz_tall = jnp.concatenate([dz, jnp.zeros((rows - experts, rows), jnp.float32)], axis=0)
    router_tall = jnp.concatenate(
        [router, jnp.zeros((rows - experts, width), jnp.bfloat16)], axis=0
    )
    from_router = dot_nn(dz_tall.T.astype(jnp.bfloat16), router_tall)
    part_ref[...] = jnp.zeros_like(part_ref)
    part_ref[8 : 8 + experts, :] = dot_nn(dz_low, second_ref[...])

    returned.wait()
    start_all([outs])
    dh = dot_tn(either, back_got[...].reshape(experts * cap, width)) + from_router
    grad_mid, grad_gain = norm_back(mid_ref[...], full_row(small_ref, 1, share), dh)
    grad_mid = g_ref[...].astype(jnp.float32) + grad_mid
    dmid_ref[...] = grad_mid
    part_ref[0:1, :] = grad_gain
    low_mid = grad_mid.astype(jnp.bfloat16)
    do_all = dot_nt(proj_ref[...].reshape(width, width), low_mid).astype(jnp.bfloat16)
    for h in range(heads):
        do_sent[h] = do_all[h * size : (h + 1) * size, :]
    start_all([arrive])
    terms_sent[...] = (
        dot_nn(mixed_ref[...].reshape(width, rows), low_mid)
        .astype(jnp.bfloat16)
        .reshape(n_exp, share, width)
    )
    start_all([terms])
    ups.turn()
    downs.turn()
    arrive.wait()

    @pl.when(is_head)
    def _():
        far = jnp.zeros((1, BLOCK), jnp.float32)
        for i in range(blocks):
            qt = scaled_queries(qkv_ref, i, size)
            dot_ = jnp.concatenate([do_ref[2 * i], do_ref[2 * i + 1]], axis=1)
            first = first_keys(lengths_ref, i * BLOCK)
            stat = stat_ref[i : i + 1, :]
            probs, grads = [], []
            delta = jnp.zeros((1, BLOCK), jnp.float32)
            for j in range(i + 1):
                s = block_scores(
                    i, j, blocks, qt, k_ref[block_of(j), :], diag_ref[...], side_ref[...], first
                )
                p = jnp.exp(s - stat)
                dp = dot_nn(v_ref[block_of(j), :], dot_)
                delta = delta + jnp.sum(p * dp, axis=0, keepdims=True)
                probs.append(p)
                grads.append(dp)
            dqt = jnp.zeros((size, BLOCK), jnp.float32)
            for j in range(i + 1):
                ds = probs[j] * (grads[j] - delta)
                if j == i:
                    diag_sum[...] += ds
                elif j == i - 1:
                    side_sum[...] += ds
                else:
                    far = far + jnp.sum(ds, axis=0, keepdims=True)
                low = ds.astype(jnp.bfloat16)
                dk_ref[:, block_of(j)] += dot_nt(qt, low)
                dv_ref[:, block_of(j)] += dot_nt(dot_, probs[j].astype(jnp.bfloat16))
                dqt = dqt + dot_nn(kt_ref[:, block_of(j)], low)
            dq_ref[:, block_of(i)] = (dqt * scale).astype(jnp.bfloat16)
        for c in range(parts):
            at = slice(c * rows, (c + 1) * rows)
            sent_ref[c, :size, :] = dq_ref[:, at]
            sent_ref[c, size : 2 * size, :] = dk_ref[:, at].astype(jnp.bfloat16)
            sent_ref[c, 2 * size :, :] = dv_ref[:, at].astype(jnp.bfloat16)
        bias_ref[0:1, :] = far[:, :half] + far[:, half:]

    start_all([back])

    @pl.when(is_head)
    def _():
        grad_ref[:size, :] = dq_ref[...]
        grad_ref[size : 2 * size, :] = dk_ref[...].astype(jnp.bfloat16)
        grad_ref[2 * size :, :] = dv_ref[...].astype(jnp.bfloat16)
        far = bias_ref[0:1, :] + jnp.sum(side_sum[:half, :half], axis=0, keepdims=True)
        far = far + jnp.sum(side_sum[:, half:], axis=0, keepdims=True)
        diag_bucket = near_buckets(buckets, 0, BLOCK, BLOCK)
        side_bucket = near_buckets(buckets, half, half, half)
        for b in range(buckets):
            one = jnp.sum(jnp.where(diag_bucket == b, diag_sum[...], 0.0), axis=0, keepdims=True)
            two = jnp.sum(
                jnp.where(side_bucket == b, side_sum[half:, :half], 0.0), axis=0, keepdims=True
            )
            row = one[:, :half] + one[:, half:] + two
            if b == buckets - 1:
                row = row + far
            bias_ref[b : b + 1, :] = row

    terms.wait()
    total = summed(terms_got, n_exp).astype(jnp.bfloat16)
    for t in range(piece_ref.shape[0]):
        piece_ref[t] = total[t * 16 : (t + 1) * 16, :]
    ups.wait()
    downs.wait()
    for k in range(side):
        up_sum[k] = ups.half(k // 2, k % 2).astype(jnp.bfloat16)
        down_sum[k] = downs.half(k // 2, k % 2).astype(jnp.bfloat16)
    outs.wait()
    back.wait()
    for m in (returned, gating, outs, terms, arrive, back, ups, downs):
        m.wait_sent()


def run_middle(
    sizes, heads, experts, own_buckets, expert_back, dgate, expert_out, up_terms, down_terms, info,
    g, mid, second, dense, proj, mixed, qkv, stat, table, lengths,
):
    n_ctx, n_exp = sizes["ctx"], sizes["exp"]
    rows, width = mid.shape
    size = width // heads
    seq = n_ctx * rows
    share = width // n_exp
    side = math.isqrt(n_ctx)
    low, full = jnp.bfloat16, jnp.float32
    chunk = up_terms.shape[0] // n_ctx
    square = (side, side, chunk, width)
    assert n_ctx == 16 and experts == 8 and rows == 128
    return pl.pallas_call(
        functools.partial(middle_kernel, sizes, heads, experts, own_buckets),
        out_shape=[
            jax.ShapeDtypeStruct((heads, 3 * size, rows), low),
            jax.ShapeDtypeStruct(expert_out.shape, low),
            jax.ShapeDtypeStruct((share // 16, 16, width), low),
            jax.ShapeDtypeStruct((3 * size, seq), low),
            jax.ShapeDtypeStruct(table.shape, full),
            jax.ShapeDtypeStruct((rows, width), full),
            jax.ShapeDtypeStruct((16, width), full),
            jax.ShapeDtypeStruct((side, chunk, width), low),
            jax.ShapeDtypeStruct((side, chunk, width), low),
        ],
        in_specs=in_vmem(2) + any_space(3) + in_vmem(10) + in_smem(1),
        out_specs=in_vmem(1) + any_space(1) + in_vmem(7),
        scratch_shapes=[
            pltpu.VMEM(expert_back.shape, low),
            pltpu.VMEM(dgate.shape, full),
            pltpu.VMEM((heads, size, rows), low),
            pltpu.VMEM((n_ctx, size, rows), low),
            pltpu.VMEM((n_ctx, 3 * size, rows), low),
            pltpu.VMEM((n_exp, share, width), low),
            pltpu.VMEM((n_exp, share, width), low),
        ]
        + ring_space((2, chunk, width)) * 2
        + [
            pltpu.VMEM((seq, size), low),
            pltpu.VMEM((seq, size), low),
            pltpu.VMEM((size, seq), low),
            pltpu.VMEM((size, seq), low),
            pltpu.VMEM((size, seq), full),
            pltpu.VMEM((size, seq), full),
            pltpu.VMEM((BLOCK, BLOCK), full),
            pltpu.VMEM((BLOCK // 2, BLOCK // 2), full),
            pltpu.VMEM((BLOCK, BLOCK), full),
            pltpu.VMEM((BLOCK, BLOCK), full),
        ]
        + move_sems(n_exp) * 4
        + move_sems(n_ctx) * 2
        + ring_sems() * 2,
        compiler_params=remote_params(2),
        cost_estimate=cost(60_000_000_000, 100_000_000, 2_400_000),
        name="run_middle",
    )(
        expert_back, dgate, expert_out, up_terms.reshape(square), down_terms.reshape(square), info,
        g, mid, second, dense, proj, mixed, qkv, stat, table, lengths,
    )


def last_kernel(
    sizes, heads, experts, own_buckets,
    grad_ref, w_ref, x_ref, small_ref, dmid_ref, turned_ref, h_ref, bias_ref, part_ref, piece_in,
    out_ref, mid_ref, info_ref, up_in, down_in,
    in_out, block_out, head_all, small_all, piece_all, up_c, up_d, down_c, down_d,
    head_in, small_in, dqkv_ref, head_parts, small_parts, piece_parts, head_sent, small_sent,
    piece_sent, up_a, up_b, down_a, down_b, *sems,
):
    n_ctx, n_exp = sizes["ctx"], sizes["exp"]
    takers, sixteen, width = piece_in.shape
    rows = x_ref.shape[0]
    size = width // heads
    share = width // n_exp
    half = share // 2
    me = lax.axis_index("ctx")
    greet(sizes, ["exp", "ctx"])
    first = [
        Move(sizes, "exp", head_in, head_parts, sems[0:3], split=True),
        Move(sizes, "exp", small_in, small_parts, sems[3:6], split=True),
        Move(sizes, "ctx", piece_in, piece_parts, sems[6:9], split=True, takers=takers),
    ]
    second = [
        Move(sizes, "ctx", head_sent, head_all, sems[9:12], senders=heads),
        Move(sizes, "ctx", small_sent, small_all, sems[12:15]),
        Move(sizes, "ctx", piece_sent, piece_all, sems[15:18], senders=takers),
    ]
    part_rows = up_d.shape[1]
    ups = RingSum(
        False,
        lambda k, h: up_in.at[k, pl.ds(h * part_rows, part_rows)],
        (up_a, up_b, up_c, up_d),
        sems[18:21],
    )
    downs = RingSum(
        False,
        lambda k, h: down_in.at[k, pl.ds(h * part_rows, part_rows)],
        (down_a, down_b, down_c, down_d),
        sems[21:24],
    )
    start_all(first[2:])

    @pl.when(me < heads)
    def _():
        terms = dot_nn(turned_ref[...], h_ref[...]).T.astype(jnp.bfloat16)
        for e in range(n_exp):
            head_in[e] = terms[e * share : (e + 1) * share, :]

    start_all(first[:1])
    ups.start()
    downs.start()

    for part in range(3):
        for pair in range(heads // 2):
            both = jnp.concatenate(
                [
                    grad_ref[2 * pair + k, part * size : (part + 1) * size, :]
                    for k in range(2)
                ],
                axis=0,
            )
            at = part * width + 2 * size * pair
            dqkv_ref[:, at : at + 2 * size] = transposed(both)
    dh = jnp.zeros((rows, width), jnp.float32)
    for at in range(0, 3 * width, 256):
        piece = w_ref[:, :, at : at + 256].reshape(width, 256)
        dh = dh + dot_nt(dqkv_ref[:, at : at + 256], piece)
    x = x_ref[...].astype(jnp.float32)
    grad_x, grad_gain = norm_back(x, full_row(small_ref, 0, share), dh)
    in_out[...] = dmid_ref[...] + grad_x

    bias = jnp.sum(bias_ref[...], axis=1, keepdims=True)
    small_in[...] = jnp.zeros_like(small_in)
    for e in range(n_exp):
        at = slice(e * share, (e + 1) * share)
        small_in[e, 0:1, :share] = grad_gain[:, at]
        small_in[e, 1:2, :share] = part_ref[0:1, at]
        small_in[e, 2 : 2 + experts, :share] = part_ref[8 : 8 + experts, at]
        small_in[e, 2 + experts : 2 + experts + own_buckets, :] = jnp.broadcast_to(
            bias[e * own_buckets : (e + 1) * own_buckets, :], (own_buckets, 128)
        )
    start_all(first[1:2])
    ups.turn()
    downs.turn()

    first[0].wait()
    total = summed(head_parts, n_exp).astype(jnp.bfloat16)
    head_sent[:share, :] = total[:, : 2 * size]
    head_sent[share:, :] = jnp.concatenate(
        [total[:half, 2 * size :], total[half:, 2 * size :]], axis=1
    )
    start_all(second[:1])
    first[2].wait()

    @pl.when(me < takers)
    def _():
        piece_sent[...] = summed(piece_parts, n_ctx).astype(jnp.bfloat16)

    start_all(second[2:])
    first[1].wait()
    small_sent[...] = summed(small_parts, n_exp)
    start_all(second[1:2])

    slots = lax.broadcasted_iota(jnp.int32, (experts * rows // 2, rows), 0).astype(jnp.float32)
    hit = [(slots == info_ref[2 + c : 3 + c, :]).astype(jnp.bfloat16) for c in range(2)]
    both = jnp.concatenate(hit, axis=1)
    picked = dot_tn(both, out_ref[...].reshape(experts * rows // 2, width))
    tall = jnp.concatenate([info_ref[...], jnp.zeros((rows - 8, rows), jnp.float32)], axis=0).T
    mixed = mid_ref[...] + (tall[:, 0:1] * picked[:rows] + tall[:, 1:2] * picked[rows:])
    block_out[...] = mixed.astype(jnp.bfloat16)

    ups.wait()
    downs.wait()
    for m in second:
        m.wait()
    for m in first + second + [ups, downs]:
        m.wait_sent()


def run_last(
    sizes, heads, experts, own_buckets, grad_qkv, weight, x, dense, dmid, turned, h_all, bias,
    parts, pieces, returned, mid, info, up_sum, down_sum,
):
    n_ctx, n_exp = sizes["ctx"], sizes["exp"]
    rows, width = x.shape
    size = width // heads
    share = width // n_exp
    takers, sixteen, _ = pieces.shape
    side, chunk, _ = up_sum.shape
    low, full = jnp.bfloat16, jnp.float32
    assert 2 + experts + own_buckets <= 16
    return pl.pallas_call(
        functools.partial(last_kernel, sizes, heads, experts, own_buckets),
        out_shape=[
            jax.ShapeDtypeStruct((rows, width), full),
            jax.ShapeDtypeStruct((rows, width), low),
            jax.ShapeDtypeStruct((heads, share * 3 // 2, 128), low),
            jax.ShapeDtypeStruct((n_ctx, 16, 128), full),
            jax.ShapeDtypeStruct((takers, sixteen, width), low),
        ]
        + [
            jax.ShapeDtypeStruct((2, 2, chunk // 2, width), low),
            jax.ShapeDtypeStruct((2, chunk // 2, width), low),
        ]
        * 2,
        in_specs=in_vmem(15),
        out_specs=in_vmem(9),
        scratch_shapes=[
            pltpu.VMEM((n_exp, share, 3 * size), low),
            pltpu.VMEM((n_exp, 16, 128), full),
            pltpu.VMEM((rows, 3 * width), low),
            pltpu.VMEM((n_exp, share, 3 * size), low),
            pltpu.VMEM((n_exp, 16, 128), full),
            pltpu.VMEM((n_ctx, sixteen, width), low),
            pltpu.VMEM((share * 3 // 2, 128), low),
            pltpu.VMEM((16, 128), full),
            pltpu.VMEM((sixteen, width), low),
        ]
        + ring_space((chunk // 2, width))[:2] * 2
        + move_sems(n_exp) * 2
        + move_sems(n_ctx) * 4
        + ring_sems() * 2,
        compiler_params=remote_params(3),
        cost_estimate=cost(4_000_000_000, 60_000_000),
        name="run_last",
    )(
        grad_qkv, weight, x, dense, dmid, turned, h_all, bias, parts, pieces, returned, mid, info,
        up_sum, down_sum,
    )


def finish_kernel(
    sizes, experts, in_ref, block_ref, head_ref, small_ref, piece_ref, up_got, up_own, down_got,
    down_own, block_out, in_out, one_out, two_out, qkv_out, weight_out, router_out, table_out,
    up_out, down_out,
):
    heads = head_ref.shape[0]
    share, width = weight_out.shape
    size = width // heads
    half = share // 2
    own_buckets = table_out.shape[0]
    block_out[0] = block_ref[...]
    in_out[0] = in_ref[...]
    for h in range(heads):
        got = head_ref[h].astype(jnp.float32)
        at = h * size
        qkv_out[:, at : at + size] = got[:share, :size]
        qkv_out[:, width + at : width + at + size] = got[:share, size:]
        qkv_out[:half, 2 * width + at : 2 * width + at + size] = got[share:, :size]
        qkv_out[half:, 2 * width + at : 2 * width + at + size] = got[share:, size:]
    takers, sixteen, _ = piece_ref.shape
    for t in range(takers):
        weight_out[t * sixteen : (t + 1) * sixteen, :] = piece_ref[t].astype(jnp.float32)
    sums = summed(small_ref, sizes["ctx"])
    one_out[...] = sums[0:1, :share]
    two_out[...] = sums[1:2, :share]
    router_out[...] = sums[2 : 2 + experts, :share]
    begin = 2 + experts
    table_out[...] = jnp.concatenate(
        [small_ref[h, begin : begin + own_buckets, 0:1] for h in range(heads)], axis=1
    )
    for got, own, out in ((up_got, up_own, up_out), (down_got, down_own, down_out)):
        rows = own.shape[1]
        for h in range(2):
            out[0, h * rows : (h + 1) * rows, :] = sum(
                p.astype(jnp.float32) for p in (own[h], got[0, h], got[1, h])
            )


def finish(sizes, heads, experts, own_buckets, parts):
    rows, width = parts[0].shape
    share = width // sizes["exp"]
    chunk = 2 * parts[-1].shape[1]
    low, full = jnp.bfloat16, jnp.float32
    return pl.pallas_call(
        functools.partial(finish_kernel, sizes, experts),
        out_shape=[
            jax.ShapeDtypeStruct((1, rows, width), low),
            jax.ShapeDtypeStruct((1, rows, width), full),
            jax.ShapeDtypeStruct((1, share), full),
            jax.ShapeDtypeStruct((1, share), full),
            jax.ShapeDtypeStruct((share, 3 * width), full),
            jax.ShapeDtypeStruct((share, width), full),
            jax.ShapeDtypeStruct((experts, share), full),
            jax.ShapeDtypeStruct((own_buckets, heads), full),
            jax.ShapeDtypeStruct((1, chunk, width), full),
            jax.ShapeDtypeStruct((1, chunk, width), full),
        ],
        in_specs=in_vmem(len(parts)),
        out_specs=in_vmem(10),
        compiler_params=pltpu.CompilerParams(vmem_limit_bytes=VMEM_BYTES),
        cost_estimate=cost(0, 8_000_000),
        name="finish",
    )(*parts)


def local(
    sizes,
    block_in,
    attn_gain,
    moe_gain,
    query_key_value_weight,
    output_matrix,
    routing_weight,
    bias_table,
    up_weight,
    down_weight,
    routes,
    doc_lengths,
    cotangent,
):
    low, full = jnp.bfloat16, jnp.float32
    n_ctx, n_exp = sizes["ctx"], sizes["exp"]
    rows, width = block_in.shape[1:]
    share = width // n_exp
    own_buckets, heads = bias_table.shape
    experts = routing_weight.shape[1]
    g_low = cotangent[0]

    expert_weights = lax.all_gather(
        jnp.concatenate([up_weight, down_weight], axis=0), "ctx", axis=1, tiled=True
    )

    lanes = lambda a: jnp.pad(a, ((0, 0), (0, 128 - a.shape[1])))
    small = jnp.concatenate(
        [lanes(attn_gain[None]), lanes(moe_gain[None]), lanes(bias_table), lanes(routing_weight.T)],
        axis=0,
    )
    small = jnp.pad(small, ((0, -small.shape[0] % 16), (0, 0)))
    capacity = min(rows, 4 * rows // experts)
    piece = (experts, capacity, width)
    lengths = doc_lengths[0]
    (
        qkv_full,
        dense,
        proj_full,
        h_first,
        x_mid,
        h_second,
        info,
        mixed,
        qkv_head,
        stat,
        table_head,
        expert_rows,
        g_rows,
        gate_rows,
    ) = run_front(
        sizes,
        heads,
        experts,
        own_buckets,
        query_key_value_weight,
        small,
        output_matrix,
        block_in[0],
        g_low,
        routes[0].T,
        lengths,
    )
    h_all = lax.all_gather(h_first, "ctx", axis=0, tiled=True)
    expert_out, expert_back, dgate, up_terms, down_terms = run_expert(
        expert_rows.reshape(experts * capacity, width),
        g_rows.reshape(experts * capacity, width),
        gate_rows,
        expert_weights,
    )
    grad_qkv_t, returned, pieces, grad_head, bias_rows, grad_mid, parts, up_sum, down_sum = (
        run_middle(
            sizes,
            heads,
            experts,
            own_buckets,
            expert_back.reshape(piece),
            dgate,
            expert_out.reshape(piece),
            up_terms,
            down_terms,
            info,
            g_low,
            x_mid,
            h_second,
            dense,
            proj_full,
            mixed,
            qkv_head,
            stat,
            table_head,
            lengths,
        )
    )
    last = run_last(
        sizes,
        heads,
        experts,
        own_buckets,
        grad_qkv_t,
        qkv_full,
        block_in[0],
        dense,
        grad_mid,
        grad_head,
        h_all,
        bias_rows,
        parts,
        pieces,
        returned,
        x_mid,
        info,
        up_sum,
        down_sum,
    )
    out = finish(sizes, heads, experts, own_buckets, last)
    block_out, grad_in, one, two, qkv, proj, router, *rest = out
    return (block_out, grad_in, one[0], two[0], qkv, proj, router.T, *rest)


def solution(mesh):
    sizes = {name: mesh.shape[name] for name in ("ctx", "exp")}
    tokens = P("exp", "ctx", None)
    row_split = P("exp", None)
    return jax.shard_map(
        functools.partial(local, sizes),
        mesh=mesh,
        in_specs=(
            tokens,
            P("exp"),
            P("exp"),
            row_split,
            row_split,
            row_split,
            row_split,
            tokens,
            tokens,
            tokens,
            row_split,
            tokens,
        ),
        out_specs=(
            tokens,
            tokens,
            P("exp"),
            P("exp"),
            row_split,
            row_split,
            row_split,
            row_split,
            tokens,
            tokens,
        ),
        check_vma=False,
    )
```
